32 devices in a mesh: dp: 8 (over y, x, core), tensor: 4 (over z).
Axes of the slice: x: 2, y: 2, z: 4, core: 2. Of those that a mesh axis runs over, the one named last changes fastest.
Arguments:
- tokens: bfloat16 [8192, 2048], P(('dp', 'tensor')), may hold values from -6 to 6
- segments: int32 [8192], P('dp'), may hold values from 0 to 2, as said below
- attn_gain: bfloat16 [2048], P('dp'), may hold values from 0.5 to 1.5
- w_query: bfloat16 [2048, 2048], P('dp', 'tensor'), may hold values from -0.125 to 0.125
- w_key: bfloat16 [2048, 256], P('dp', 'tensor'), may hold values from -0.125 to 0.125
- w_value: bfloat16 [2048, 256], P('dp', 'tensor'), may hold values from -0.125 to 0.125
- w_out: bfloat16 [2048, 2048], P('tensor', 'dp'), may hold values from -1 to 1
- mlp_gain: bfloat16 [2048], P('dp'), may hold values from 0.5 to 1.5
- w_gate: bfloat16 [2048, 5632], P('dp', 'tensor'), may hold values from -0.125 to 0.125
- w_up: bfloat16 [2048, 5632], P('dp', 'tensor'), may hold values from -0.125 to 0.125
- w_down: bfloat16 [5632, 2048], P('tensor', 'dp'), may hold values from -0.078125 to 0.078125
- cotangent: bfloat16 [8192, 2048], P(('dp', 'tensor')), may hold values from -6 to 6
Outputs:
- output: bfloat16 [8192, 2048], P(('dp', 'tensor'))
- grad_tokens: float32 [8192, 2048], P(('dp', 'tensor'))
- grad_attn_gain: float32 [2048], P('dp')
- grad_query: float32 [2048, 2048], P('dp', 'tensor')
- grad_key: float32 [2048, 256], P('dp', 'tensor')
- grad_value: float32 [2048, 256], P('dp', 'tensor')
- grad_out: float32 [2048, 2048], P('tensor', 'dp')
- grad_mlp_gain: float32 [2048], P('dp')
- grad_gate: float32 [2048, 5632], P('dp', 'tensor')
- grad_up: float32 [2048, 5632], P('dp', 'tensor')
- grad_down: float32 [5632, 2048], P('tensor', 'dp')
The draws below stay inside these ranges and needn't reach their ends.
Inputs may be any that keep to these rules, and one draw needn't show every extreme that they name: `segments`: within each group of 1024 tokens (one index of dp) segment numbers never fall and name three sequences: the first starts at token 0 and is shorter than 256, the last has at most 64 tokens, the middle one holds the rest.
All inputs are finite; a program needn't handle non-finite values.
Results may differ from the reference program's by a relative error of at most 0.02.
Values may be sent and summed in bfloat16 or wider, within the bound.
A program may use at most 192 MiB of HBM per device.

```python
import math
import jax
import jax.numpy as jnp
from jax import lax

D = 2048
HEADS = 32
KV = 4
HD = 64
FF = 5632
TOK_DEV = 256
GROUP = 1024
TOKENS = 8192


def draw_segments(key, part):
    key = jax.random.fold_in(key, 7)
    group_count = TOKENS // GROUP
    key_head, key_tail = jax.random.split(key)
    head_len = jax.random.randint(key_head, (group_count, 1), 1, TOK_DEV)
    tail_len = jax.random.randint(key_tail, (group_count, 1), 1, TOK_DEV // 4 + 1)
    indices = jnp.arange(GROUP, dtype=jnp.int32)[None, :]
    numbers = (indices >= head_len).astype(jnp.int32) + (indices >= GROUP - tail_len).astype(jnp.int32)
    return numbers.reshape(TOKENS)


def shard_levels(own_key, shape, cuts, low, top_value):
    def one(axis_at, shards_of):
        draws = jax.random.uniform(jax.random.fold_in(jax.random.fold_in(own_key, 6), axis_at), (shards_of,), jnp.float32, low / len(cuts), top_value / len(cuts))
        return jnp.repeat(jnp.exp(draws), shape[axis_at] // shards_of).reshape((-1,) + (1,) * (len(shape) - axis_at - 1))

    level = one(*cuts[0])
    for cut in cuts[1:]:
        level = level * one(*cut)
    return level


def gaussian(stream_key, extent, width, limit, shards=(), kind=jnp.bfloat16):
    values = width * jax.random.normal(stream_key, extent, jnp.float32)
    if shards:
        values = values * shard_levels(stream_key, extent, shards, -0.22, 0.18)
    return jnp.clip(values, -limit, limit).astype(kind)


def setup_inputs(seed: int = 0) -> dict:
    streams_of = jax.random.split(jax.random.key(seed), 13)
    return {
        "tokens": gaussian(streams_of[0], (TOKENS, D), 1.0, 6.0, ((0, 32),)),
        "segments": draw_segments(jax.random.fold_in(streams_of[12], 71), 0),
        "attn_gain": jnp.clip(1.0 + 0.1 * jax.random.normal(streams_of[2], (D,), jnp.float32), 0.5, 1.5).astype(jnp.bfloat16),
        "w_query": gaussian(streams_of[3], (D, HEADS * HD), D ** -0.5, 0.125, ((0, 8), (1, 4))),
        "w_key": gaussian(streams_of[4], (D, KV * HD), D ** -0.5, 0.125, ((0, 8), (1, 4))),
        "w_value": gaussian(streams_of[5], (D, KV * HD), D ** -0.5, 0.125, ((0, 8), (1, 4))),
        "w_out": gaussian(streams_of[6], (HEADS * HD, D), (HEADS * HD // 64) ** -0.5, 1.0, ((0, 4), (1, 8))),
        "mlp_gain": jnp.clip(1.0 + 0.1 * jax.random.normal(streams_of[7], (D,), jnp.float32), 0.5, 1.5).astype(jnp.bfloat16),
        "w_gate": gaussian(streams_of[8], (D, FF), D ** -0.5, 0.125, ((0, 8), (1, 4))),
        "w_up": gaussian(streams_of[9], (D, FF), D ** -0.5, 0.125, ((0, 8), (1, 4))),
        "w_down": gaussian(streams_of[10], (FF, D), FF ** -0.5, 0.078125, ((0, 4), (1, 8))),
        "cotangent": gaussian(streams_of[11], (TOKENS, D), 1.0, 6.0, ((0, 32),)),
    }


@jax.custom_vjp
def low(v):
    return lax.optimization_barrier(v.astype(jnp.bfloat16)).astype(jnp.float32)

@jax.custom_vjp
def low_back(v):
    return v

def low_keep(v):
    return (low(v), None)

def low_pass(kept, grad):
    return (grad,)

def back_keep(v):
    return (v, None)

def back_low(kept, grad):
    return (low(grad),)
low.defvjp(low_keep, low_pass)
low_back.defvjp(back_keep, back_low)
EPSILON = 1e-05
MASKED = -1e+30
HIGHEST = lax.Precision.HIGHEST

def matmul(left, right):
    return jnp.dot(left, right, precision=HIGHEST, preferred_element_type=jnp.float32)

def rms_scale(values_in, gain_row):
    factor = lax.rsqrt(lax.optimization_barrier(jnp.mean(values_in * values_in, axis=-1, keepdims=True)) + EPSILON)
    return values_in * factor * gain_row

def positions_of(segment_row):
    indices = jnp.arange(segment_row.shape[0], dtype=jnp.int32)
    starts = jnp.concatenate([jnp.ones((1,), jnp.bool_), segment_row[1:] != segment_row[:-1]])
    first_index = lax.cummax(jnp.where(starts, indices, jnp.zeros_like(indices)), axis=0)
    return indices - first_index

def rope_tables(positions, head_width):
    half_width = head_width // 2
    frequency = jnp.exp(jnp.arange(half_width, dtype=jnp.float32) * (-2.0 * math.log(10000.0) / head_width))
    angles = positions.astype(jnp.float32)[:, None] * frequency[None, :]
    cosine = jnp.cos(angles)
    sine_rows = jnp.sin(angles)
    return (jnp.concatenate([cosine, cosine], 1), jnp.concatenate([sine_rows, sine_rows], 1))

def rotate(arrays, cosine, sine_rows):
    half_width = arrays.shape[-1] // 2
    turned = jnp.concatenate([-arrays[..., half_width:], arrays[..., :half_width]], -1)
    return arrays * cosine + turned * sine_rows

def block_forward(token_float, attn_gain, w_query, w_key, w_value, w_out, mlp_gain, w_gate, w_up, w_down, segment_row):
    group_len = token_float.shape[0]
    positions = positions_of(segment_row)
    cosine, sine_rows = rope_tables(positions, HD)
    indices = jnp.arange(group_len)
    attn_mask = (indices[None, :] <= indices[:, None]) & (segment_row[None, :] == segment_row[:, None])
    normed = low(rms_scale(token_float, attn_gain))
    queries = low_back(matmul(normed, w_query)).reshape(group_len, HEADS, HD).transpose(1, 0, 2)
    keys_raw = low_back(matmul(normed, w_key)).reshape(group_len, KV, HD).transpose(1, 0, 2)
    values_raw = low_back(matmul(normed, w_value)).reshape(group_len, KV, HD).transpose(1, 0, 2)
    query_rot = low(rotate(queries, cosine, sine_rows) * HD ** (-0.5))
    key_rot = low(rotate(keys_raw, cosine, sine_rows))
    value_low = low(values_raw)
    query_groups = query_rot.reshape(KV, HEADS // KV, group_len, HD)

    def attend(bundle):
        query_group, key_group, value_group = bundle
        scores = jnp.einsum('rqd,kd->rqk', query_group, key_group, precision=HIGHEST)
        scores = low_back(jnp.where(attn_mask, scores, MASKED))
        row_peak = lax.optimization_barrier(jnp.max(scores, axis=-1, keepdims=True))
        exponent = jnp.exp(scores - row_peak)
        prob_rows = exponent / lax.optimization_barrier(jnp.sum(exponent, axis=-1, keepdims=True))
        return jnp.einsum('rqk,kd->rqd', low(prob_rows), value_group, precision=HIGHEST)
    attended = lax.map(jax.checkpoint(attend), (query_groups, key_rot, value_low))
    mixed = attended.reshape(HEADS, group_len, HD).transpose(1, 0, 2).reshape(group_len, HEADS * HD)
    mixed = low_back(low(mixed))
    residual = token_float + low_back(matmul(mixed, w_out))
    normed_mlp = low(rms_scale(residual, mlp_gain))
    gate_value = low_back(matmul(normed_mlp, w_gate))
    up_value = low_back(matmul(normed_mlp, w_up))
    hidden = low(jax.nn.silu(gate_value) * up_value)
    return residual + matmul(hidden, w_down)

def reference(tokens, segments, attn_gain, w_query, w_key, w_value, w_out, mlp_gain, w_gate, w_up, w_down, cotangent):
    weights = tuple((array.astype(jnp.float32) for array in (attn_gain, w_query, w_key, w_value, w_out, mlp_gain, w_gate, w_up, w_down)))
    group_count = TOKENS // GROUP
    token_groups = tokens.astype(jnp.float32).reshape(group_count, GROUP, D)
    cot_groups = cotangent.astype(jnp.float32).reshape(group_count, GROUP, D)
    segment_groups = segments.reshape(group_count, GROUP)

    def group_step(totals, bundle):
        token_float, cot_float, segment_row = bundle

        def forward(inputs_now, *weight_list):
            return block_forward(inputs_now, *weight_list, segment_row)
        out_value, pullback = jax.vjp(forward, token_float, *weights)
        gradient = pullback(cot_float)
        summed = tuple((left + right for left, right in zip(totals, gradient[1:])))
        return (summed, (out_value, gradient[0]))
    zero_grads = tuple((jnp.zeros_like(array) for array in weights))
    totals, results = lax.scan(group_step, zero_grads, (token_groups, cot_groups, segment_groups))
    out_groups, grad_groups = results
    return (out_groups.reshape(TOKENS, D).astype(jnp.bfloat16), grad_groups.reshape(TOKENS, D), totals[0], totals[1], totals[2], totals[3], totals[4], totals[5], totals[6], totals[7], totals[8])
```

```python
import functools
import math

import jax
import jax.numpy as jnp
from jax import lax
from jax.experimental import pallas as pl
from jax.experimental.pallas import tpu as pltpu
from jax.sharding import PartitionSpec as P

HD = 64
RATIO = 8
EPSILON = 1e-05
MASKED = -1e30
BF = jnp.bfloat16
F32 = jnp.float32


def dot_nn(left, right):
    return lax.dot_general(left, right, (((1,), (0,)), ((), ())), preferred_element_type=F32)


def dot_nt(left, right):
    return lax.dot_general(left, right, (((1,), (1,)), ((), ())), preferred_element_type=F32)


def dot_tn(left, right):
    return lax.dot_general(left, right, (((0,), (0,)), ((), ())), preferred_element_type=F32)


def rms_forward(values_in, gain_row):
    factor = lax.rsqrt(jnp.mean(values_in * values_in, axis=-1, keepdims=True) + EPSILON)
    return (values_in * factor * gain_row, factor)


def rms_backward(values_in, factor, gain_row, gradient):
    scaled = gain_row * gradient
    grad_gain = jnp.sum(gradient * values_in * factor, axis=0)
    grad_input = factor * scaled - values_in * (factor * factor * factor) * jnp.mean(
        scaled * values_in, axis=-1, keepdims=True
    )
    return (grad_input, grad_gain)


def rope_t(u, cos, sin):
    half = HD // 2
    return u * cos + jnp.concatenate([-u[half:], u[:half]], 0) * sin


def rope_back_t(w, cos, sin):
    half = HD // 2
    ws = w * sin
    return w * cos + jnp.concatenate([ws[half:], -ws[:half]], 0)


def bias_of(first, row0, keys, rows):
    key = lax.broadcasted_iota(jnp.int32, (keys, rows), 0)
    row = lax.broadcasted_iota(jnp.int32, (keys, rows), 1) + row0
    return jnp.where((key <= row) & (key >= first), 0.0, MASKED).astype(F32)


def attn_forward_kernel(row0_ref, a1_ref, wq_ref, kv_ref, cos_ref, sin_ref, first_ref, o_ref, q_ref, lse_ref, bias_ref, s_ref, vt_ref):
    keys, rows = bias_ref.shape

    @pl.when(pl.program_id(0) == 0)
    def _():
        bias_ref[...] = bias_of(first_ref[...], row0_ref[0], keys, rows)

    kv = kv_ref[0]
    kvt = kv.T
    vt_ref[...] = jnp.concatenate([kvt[HD:], jnp.ones((16, keys), BF)], 0)
    qt = dot_nn(a1_ref[...], wq_ref[0]).T
    cos, sin = cos_ref[...], sin_ref[...]
    for h in range(RATIO):
        q = (rope_t(qt[h * HD : (h + 1) * HD], cos, sin) * HD ** (-0.5)).astype(BF)
        q_ref[0, h * HD : (h + 1) * HD] = q
        s_ref[...] = dot_nn(kv, jnp.concatenate([q, jnp.zeros_like(q)], 0)) + bias_ref[...]
        peak = jnp.max(s_ref[...], axis=0, keepdims=True)
        e = jnp.exp(s_ref[...] - peak).astype(BF)
        ot = dot_nn(vt_ref[...], e)
        total = ot[HD : HD + 1]
        o_ref[0, h * HD : (h + 1) * HD] = (ot[:HD] / total).astype(BF)
        lse_ref[0, h : h + 1] = peak + jnp.log(total)


def attn_backward_kernel(row0_ref, q_ref, kv_ref, do_ref, o_ref, lse_ref, cos_ref, sin_ref, first_ref, dq_ref, dkv_ref, bias_ref, acc_ref):
    keys, rows = bias_ref.shape

    @pl.when(pl.program_id(0) == 0)
    def _():
        bias_ref[...] = bias_of(first_ref[...], row0_ref[0], keys, rows)

    kv = kv_ref[0]
    kt = kv.T[:HD]
    cos, sin = cos_ref[...], sin_ref[...]
    for h in range(RATIO):
        part = slice(h * HD, (h + 1) * HD)
        q, do, o = q_ref[0, part], do_ref[0, part], o_ref[0, part]
        qz = jnp.concatenate([q, jnp.zeros_like(q)], 0)
        doz = jnp.concatenate([jnp.zeros_like(do), do], 0)
        delta = jnp.sum(do.astype(F32) * o.astype(F32), axis=0, keepdims=True)
        p = jnp.exp(dot_nn(kv, qz) + bias_ref[...] - lse_ref[0, h : h + 1])
        ds = (p * (dot_nn(kv, doz) - delta)).astype(BF)
        grad = dot_nt(ds, qz) + dot_nt(p.astype(BF), doz)
        if h == 0:
            acc_ref[...] = grad
        else:
            acc_ref[...] += grad
        dq = dot_nn(kt, ds) * HD ** (-0.5)
        dq_ref[0, part] = rope_back_t(dq, cos, sin).astype(BF)
    dkv_ref[0] = acc_ref[...]


def params():
    return pltpu.CompilerParams(vmem_limit_bytes=56 * 2**20)


def attn_forward(row0, a1, wq, kv, cos, sin, first):
    groups, width, cols = wq.shape
    rows, keys = a1.shape[0], kv.shape[1]
    whole = lambda *shape: pl.BlockSpec(shape, lambda i: (0,) * len(shape))
    part = lambda *shape: pl.BlockSpec((1,) + shape, lambda i: (i,) + (0,) * len(shape))
    return pl.pallas_call(
        attn_forward_kernel,
        grid=(groups,),
        in_specs=[pl.BlockSpec(memory_space=pltpu.SMEM), whole(rows, width), part(width, cols), part(keys, 2 * HD), whole(HD, rows), whole(HD, rows), whole(1, rows)],
        out_specs=[part(cols, rows), part(cols, rows), part(RATIO, rows)],
        out_shape=[jax.ShapeDtypeStruct((groups, cols, rows), BF), jax.ShapeDtypeStruct((groups, cols, rows), BF), jax.ShapeDtypeStruct((groups, RATIO, rows), F32)],
        scratch_shapes=[pltpu.VMEM((keys, rows), F32), pltpu.VMEM((keys, rows), F32), pltpu.VMEM((HD + 16, keys), BF)],
        compiler_params=params(),
        name="attn_forward",
    )(row0, a1, wq, kv, cos, sin, first)


def attn_backward(row0, q, kv, do, o, lse, cos, sin, first):
    groups, cols, rows = q.shape
    keys = kv.shape[1]
    whole = lambda *shape: pl.BlockSpec(shape, lambda i: (0,) * len(shape))
    part = lambda *shape: pl.BlockSpec((1,) + shape, lambda i: (i,) + (0,) * len(shape))
    return pl.pallas_call(
        attn_backward_kernel,
        grid=(groups,),
        in_specs=[pl.BlockSpec(memory_space=pltpu.SMEM), part(cols, rows), part(keys, 2 * HD), part(cols, rows), part(cols, rows), part(RATIO, rows), whole(HD, rows), whole(HD, rows), whole(1, rows)],
        out_specs=[part(cols, rows), part(keys, 2 * HD)],
        out_shape=[jax.ShapeDtypeStruct((groups, cols, rows), BF), jax.ShapeDtypeStruct((groups, keys, 2 * HD), F32)],
        scratch_shapes=[pltpu.VMEM((keys, rows), F32), pltpu.VMEM((keys, 2 * HD), F32)],
        compiler_params=params(),
        name="attn_backward",
    )(row0, q, kv, do, o, lse, cos, sin, first)


MESH = pl.DeviceIdType.MESH
ANY = pl.BlockSpec(memory_space=pl.ANY)


class Place:
    def __init__(self):
        d, self.t = lax.axis_index("dp"), lax.axis_index("tensor")
        self.c, self.p = d % 2, d // 2
        x, y = self.p % 2, self.p // 2
        self.px, self.py, self.pd = self.p + 1 - 2 * x, self.p + 2 - 4 * y, 3 - self.p
        self.across = [self.t + 1 - 2 * (self.t % 2), (self.t + 2) % 4, 3 - self.t]
        self.order = [self.t] + self.across

    def at(self, p, c, t):
        return {"dp": p * 2 + c, "tensor": t}

    def x_side(self):
        return self.at(self.px, self.c, self.t)

    def y_side(self):
        return self.at(self.py, self.c, self.t)

    def twin(self):
        return self.at(self.p, 1 - self.c, self.t)

    def line(self, t):
        return self.at(self.p, self.c, t)

    def greet(self):
        barrier = pltpu.get_barrier_semaphore()
        others = [self.x_side(), self.y_side(), self.twin()] + [self.line(t) for t in self.across]
        for other in others:
            pl.semaphore_signal(barrier, inc=1, device_id=other, device_id_type=MESH)
        pl.semaphore_wait(barrier, len(others))


def half_of(ref, part):
    rows = ref.shape[0] // 2
    return ref.at[pl.ds(part * rows, rows)]


def gather_kernel(kv, wq, wo, wg, wu, wd, kv_out, q_out, o_out, g_out, u_out, d_out, z_send, z_recv, send, recv, local):
    me = Place()
    me.greet()
    sources = [kv, wq, wo, wg, wu, wd]
    outs = [kv_out, q_out, o_out, g_out, u_out, d_out]

    def piece(k, s, p, c):
        if k == 2:
            return o_out.at[p, c, s]
        return outs[k].at[s, p, c] if k < 2 else outs[k].at[p, c]

    def pair(k, s, c):
        if k == 2:
            return o_out.at[:, c, s]
        return outs[k].at[s, :, c] if k < 2 else outs[k].at[:, c]

    def remote(src, dst, send_sem, recv_sem, to):
        copy = pltpu.make_async_remote_copy(src, dst, send_sem, recv_sem, device_id=to, device_id_type=MESH)
        copy.start()
        return copy

    lines = {}
    for k in range(3):
        for j, z in enumerate(me.across):
            lines[k, j + 1] = remote(sources[k], piece(k, me.t, me.p, me.c), z_send.at[k, j], z_recv.at[k, j], me.line(z))
    items = [(k, j) for k in range(3) for j in range(4)] + [(k, 0) for k in range(3, 6)]
    going = {}

    def push(i, kind, src, dst, to):
        going[i, kind] = remote(src, dst, send.at[i, kind], recv.at[i, kind], to)

    def first(i):
        k, j = items[i]
        s = me.order[j]
        mine = piece(k, s, me.p, me.c)
        if j == 0:
            src = sources[k]
            going[i, "local"] = pltpu.make_async_copy(src, mine, local.at[i])
            going[i, "local"].start()
        else:
            lines[k, j].wait_recv()
            src = mine
        push(i, 0, src, mine, me.x_side())
        push(i, 1, src, mine, me.y_side())

    def second(i):
        k, j = items[i]
        s = me.order[j]
        going[i, 0].wait_recv()
        part = half_of(piece(k, s, me.px, me.c), 0)
        push(i, 2, part, part, me.y_side())
        going[i, 1].wait_recv()
        part = half_of(piece(k, s, me.py, me.c), 1)
        push(i, 3, part, part, me.x_side())

    def third(i):
        k, j = items[i]
        going[i, 2].wait_recv()
        going[i, 3].wait_recv()
        if (i, "local") in going:
            going[i, "local"].wait()
        part = pair(k, me.order[j], me.c)
        push(i, 4, part, part, me.twin())

    count = len(items)
    for tick in range(count + 4):
        if tick < count:
            first(tick)
        if 0 <= tick - 1 < count:
            second(tick - 1)
        if 0 <= tick - 2 < count:
            third(tick - 2)
        if 0 <= tick - 4 < count:
            going[tick - 4, 4].wait_recv()
    for copy in lines.values():
        copy.wait_send()
    for i in range(count):
        for kind in range(5):
            going[i, kind].wait_send()


def gather_weights(kv, wq, wo, wg, wu, wd):
    dma = pltpu.SemaphoreType.DMA
    shape = lambda lead, w: jax.ShapeDtypeStruct(lead + w.shape, BF)
    return pl.pallas_call(
        gather_kernel,
        out_shape=[shape((4, 4, 2), kv), shape((4, 4, 2), wq), shape((4, 2, 4), wo), shape((4, 2), wg), shape((4, 2), wu), shape((4, 2), wd)],
        in_specs=[ANY] * 6,
        out_specs=[ANY] * 6,
        scratch_shapes=[dma((3, 3)), dma((3, 3)), dma((15, 5)), dma((15, 5)), dma((15,))],
        compiler_params=pltpu.CompilerParams(collective_id=1, has_side_effects=True, vmem_limit_bytes=48 * 2**20),
        name="gather_weights",
    )(kv, wq, wo, wg, wu, wd)


def body(tokens, segments, attn_gain, w_query, w_key, w_value, w_out, mlp_gain, w_gate, w_up, w_down, cotangent):
    rows, width = tokens.shape
    hidden = w_gate.shape[1]
    nt = lax.axis_size("tensor")
    row0 = lax.axis_index("tensor") * rows
    keys = segments.shape[0]

    own_seg = lax.dynamic_slice_in_dim(segments, row0, rows)
    first = jnp.sum((segments[:, None] < own_seg[None, :]).astype(jnp.int32), axis=0)
    index = jnp.arange(rows, dtype=jnp.int32) + row0
    freq = jnp.exp(jnp.arange(HD // 2, dtype=F32) * (-2.0 * math.log(10000.0) / HD))
    angle = freq[:, None] * (index - first).astype(F32)[None, :]
    cos, sin = jnp.cos(angle), jnp.sin(angle)
    cos, sin = jnp.concatenate([cos, cos], 0), jnp.concatenate([sin, sin], 0)
    first = first[None, :]
    row0_s = row0[None].astype(jnp.int32)

    gain1 = lax.all_gather(attn_gain, "dp", axis=0, tiled=True).astype(F32)
    gain2 = lax.all_gather(mlp_gain, "dp", axis=0, tiled=True).astype(F32)
    w_kv = jnp.concatenate([w_key, w_value], 1)
    if lax.axis_size("dp") == 8 and nt == 4:
        wkv, wq, wo, wg, wu, wd = gather_weights(w_kv, w_query, w_out, w_gate, w_up, w_down)
        wkv, wq = wkv.reshape(4, width, -1), wq.reshape(4, width, -1)
        wo = wo.reshape(8, width, -1).transpose(1, 0, 2).reshape(width, width)
        wg, wu = wg.reshape(width, -1), wu.reshape(width, -1)
        wd = wd.reshape(8, hidden, -1).transpose(1, 0, 2).reshape(hidden, width)
    else:
        full = lambda w, axis: lax.all_gather(lax.all_gather(w, "dp", axis=axis, tiled=True), "tensor", axis=0)
        wq = full(w_query, 0)
        wkv = full(w_kv, 0)
        wo = full(w_out, 1).reshape(width, width)
        wg = lax.all_gather(w_gate, "dp", axis=0, tiled=True)
        wu = lax.all_gather(w_up, "dp", axis=0, tiled=True)
        wd = lax.all_gather(w_down, "dp", axis=1, tiled=True)

    x = tokens.astype(F32)
    n1, r1 = rms_forward(x, gain1)
    a1 = n1.astype(BF)
    kv = jnp.einsum("rd,gdc->grc", a1, wkv, preferred_element_type=F32)
    cos_r, sin_r = cos.T, sin.T
    k = kv[..., :HD]
    k = k * cos_r + jnp.concatenate([-k[..., HD // 2 :], k[..., : HD // 2]], -1) * sin_r
    kv = jnp.concatenate([k, kv[..., HD:]], -1).astype(BF)
    kv = lax.all_gather(kv, "tensor", axis=1, tiled=True)
    o, q, lse = attn_forward(row0_s, a1, wq, kv, cos, sin, first)
    o2 = o.reshape(-1, rows)
    h = x + dot_tn(o2, wo)

    n2, r2 = rms_forward(h, gain2)
    a2 = lax.all_gather(n2.astype(BF), "tensor", axis=0, tiled=True)
    cot = lax.all_gather(cotangent, "tensor", axis=0, tiled=True)
    g, u = dot_nn(a2, wg), dot_nn(a2, wu)
    sig = jax.nn.sigmoid(g)
    act = g * sig
    z = (act * u).astype(BF)
    scatter = lambda v: lax.psum_scatter(v.astype(BF), "tensor", scatter_dimension=0, tiled=True).astype(F32)
    output = (h + scatter(dot_nn(z, wd))).astype(BF)
    dz = dot_nt(cot, wd)
    dg = (dz * u * (sig * (1.0 + g * (1.0 - sig)))).astype(BF)
    du = (dz * act).astype(BF)
    gd_part = dot_tn(z, cot)
    gg_part = dot_tn(a2, dg)
    gu_part = dot_tn(a2, du)
    da2 = scatter(dot_nt(dg, wg) + dot_nt(du, wu))
    dres, gain2_part = rms_backward(h, r2, gain2, da2)
    dh = cotangent.astype(F32) + dres
    dhb = dh.astype(BF)

    do = dot_nt(wo, dhb).astype(BF).reshape(o.shape)
    go_part = dot_nn(o2, dhb)
    dq, dkv = attn_backward(row0_s, q, kv, do, o, lse, cos, sin, first)
    groups = dkv.shape[0]
    dkv = lax.psum_scatter(dkv.astype(BF), "tensor", scatter_dimension=1, tiled=True).astype(F32)
    dk = dkv[..., :HD]
    ws = dk * sin_r
    dk = dk * cos_r + jnp.concatenate([ws[..., HD // 2 :], -ws[..., : HD // 2]], -1)
    dkv = jnp.concatenate([dk, dkv[..., HD:]], -1).astype(BF)
    gq_part = jnp.einsum("rd,gcr->gdc", a1, dq, preferred_element_type=F32)
    gkv_part = jnp.einsum("rd,grc->gdc", a1, dkv, preferred_element_type=F32)
    da1 = jnp.einsum("gcr,gdc->rd", dq, wq, preferred_element_type=F32) + jnp.einsum("grc,gdc->rd", dkv, wkv, preferred_element_type=F32)
    din, gain1_part = rms_backward(x, r1, gain1, da1)
    grad_tokens = dh + din

    def home(v, dim):
        v = lax.psum_scatter(v.astype(BF), "dp", scatter_dimension=dim, tiled=True)
        return v

    def home_all(v, dim):
        return lax.psum_scatter(home(v, dim + 1), "tensor", scatter_dimension=0, tiled=False).astype(F32)

    gq = home_all(gq_part, 0)
    gkv = home_all(gkv_part, 0)
    go = home_all(go_part.reshape(nt, -1, width), 1)
    gg, gu = home(gg_part, 0).astype(F32), home(gu_part, 0).astype(F32)
    gd = home(gd_part, 1).astype(F32)
    gains = lax.psum_scatter(jnp.stack([gain1_part, gain2_part]), "dp", scatter_dimension=1, tiled=True)
    gains = lax.psum(gains, "tensor")
    return (output, grad_tokens, gains[0], gq, gkv[:, :HD], gkv[:, HD:], go, gains[1], gg, gu, gd)


def solution(mesh):
    rows, block = P(("dp", "tensor"), None), P("dp", "tensor")
    turned, line = P("tensor", "dp"), P("dp")
    return jax.shard_map(
        body,
        mesh=mesh,
        in_specs=(rows, line, line, block, block, block, turned, line, block, block, turned, rows),
        out_specs=(rows, rows, line, block, block, block, turned, line, block, block, turned),
        check_vma=False,
    )
```

```python
import functools
import math

import jax
import jax.numpy as jnp
from jax import lax
from jax.experimental import pallas as pl
from jax.experimental.pallas import tpu as pltpu
from jax.sharding import PartitionSpec as P

HD = 64
RATIO = 8
EPSILON = 1e-05
MASKED = -1e30
BF = jnp.bfloat16
F32 = jnp.float32


def dot_nn(left, right):
    return lax.dot_general(left, right, (((1,), (0,)), ((), ())), preferred_element_type=F32)


def dot_nt(left, right):
    return lax.dot_general(left, right, (((1,), (1,)), ((), ())), preferred_element_type=F32)


def dot_tn(left, right):
    return lax.dot_general(left, right, (((0,), (0,)), ((), ())), preferred_element_type=F32)


def rms_forward(values_in, gain_row):
    factor = lax.rsqrt(jnp.mean(values_in * values_in, axis=-1, keepdims=True) + EPSILON)
    return (values_in * factor * gain_row, factor)


def rms_backward(values_in, factor, gain_row, gradient):
    scaled = gain_row * gradient
    grad_gain = jnp.sum(gradient * values_in * factor, axis=0)
    grad_input = factor * scaled - values_in * (factor * factor * factor) * jnp.mean(
        scaled * values_in, axis=-1, keepdims=True
    )
    return (grad_input, grad_gain)


def rope_t(u, cos, sin):
    half = HD // 2
    return u * cos + jnp.concatenate([-u[half:], u[:half]], 0) * sin


def rope_back_t(w, cos, sin):
    half = HD // 2
    ws = w * sin
    return w * cos + jnp.concatenate([ws[half:], -ws[:half]], 0)


def bias_of(first, row0, keys, rows):
    key = lax.broadcasted_iota(jnp.int32, (keys, rows), 0)
    row = lax.broadcasted_iota(jnp.int32, (keys, rows), 1) + row0
    return jnp.where((key <= row) & (key >= first), 0.0, MASKED).astype(F32)


def attn_forward_kernel(row0_ref, a1_ref, wq_ref, kv_ref, cos_ref, sin_ref, first_ref, o_ref, q_ref, lse_ref, bias_ref, s_ref, vt_ref):
    keys, rows = bias_ref.shape

    @pl.when(pl.program_id(0) == 0)
    def _():
        bias_ref[...] = bias_of(first_ref[...], row0_ref[0], keys, rows)

    kv = kv_ref[0]
    kvt = kv.T
    vt_ref[...] = jnp.concatenate([kvt[HD:], jnp.ones((16, keys), BF)], 0)
    qt = dot_nn(a1_ref[...], wq_ref[0]).T
    cos, sin = cos_ref[...], sin_ref[...]
    for h in range(RATIO):
        q = (rope_t(qt[h * HD : (h + 1) * HD], cos, sin) * HD ** (-0.5)).astype(BF)
        q_ref[0, h * HD : (h + 1) * HD] = q
        s_ref[...] = dot_nn(kv, jnp.concatenate([q, jnp.zeros_like(q)], 0)) + bias_ref[...]
        peak = jnp.max(s_ref[...], axis=0, keepdims=True)
        e = jnp.exp(s_ref[...] - peak).astype(BF)
        ot = dot_nn(vt_ref[...], e)
        total = ot[HD : HD + 1]
        o_ref[0, h * HD : (h + 1) * HD] = (ot[:HD] / total).astype(BF)
        lse_ref[0, h : h + 1] = peak + jnp.log(total)


def attn_backward_kernel(row0_ref, q_ref, kv_ref, do_ref, o_ref, lse_ref, cos_ref, sin_ref, first_ref, dq_ref, dkv_ref, bias_ref, acc_ref):
    keys, rows = bias_ref.shape

    @pl.when(pl.program_id(0) == 0)
    def _():
        bias_ref[...] = bias_of(first_ref[...], row0_ref[0], keys, rows)

    kv = kv_ref[0]
    kt = kv.T[:HD]
    cos, sin = cos_ref[...], sin_ref[...]
    for h in range(RATIO):
        part = slice(h * HD, (h + 1) * HD)
        q, do, o = q_ref[0, part], do_ref[0, part], o_ref[0, part]
        qz = jnp.concatenate([q, jnp.zeros_like(q)], 0)
        doz = jnp.concatenate([jnp.zeros_like(do), do], 0)
        delta = jnp.sum(do.astype(F32) * o.astype(F32), axis=0, keepdims=True)
        p = jnp.exp(dot_nn(kv, qz) + bias_ref[...] - lse_ref[0, h : h + 1])
        ds = (p * (dot_nn(kv, doz) - delta)).astype(BF)
        grad = dot_nt(ds, qz) + dot_nt(p.astype(BF), doz)
        if h == 0:
            acc_ref[...] = grad
        else:
            acc_ref[...] += grad
        dq = dot_nn(kt, ds) * HD ** (-0.5)
        dq_ref[0, part] = rope_back_t(dq, cos, sin).astype(BF)
    dkv_ref[0] = acc_ref[...]


def params():
    return pltpu.CompilerParams(vmem_limit_bytes=56 * 2**20)


def attn_forward(row0, a1, wq, kv, cos, sin, first):
    groups, width, cols = wq.shape
    rows, keys = a1.shape[0], kv.shape[1]
    whole = lambda *shape: pl.BlockSpec(shape, lambda i: (0,) * len(shape))
    part = lambda *shape: pl.BlockSpec((1,) + shape, lambda i: (i,) + (0,) * len(shape))
    return pl.pallas_call(
        attn_forward_kernel,
        grid=(groups,),
        in_specs=[pl.BlockSpec(memory_space=pltpu.SMEM), whole(rows, width), part(width, cols), part(keys, 2 * HD), whole(HD, rows), whole(HD, rows), whole(1, rows)],
        out_specs=[part(cols, rows), part(cols, rows), part(RATIO, rows)],
        out_shape=[jax.ShapeDtypeStruct((groups, cols, rows), BF), jax.ShapeDtypeStruct((groups, cols, rows), BF), jax.ShapeDtypeStruct((groups, RATIO, rows), F32)],
        scratch_shapes=[pltpu.VMEM((keys, rows), F32), pltpu.VMEM((keys, rows), F32), pltpu.VMEM((HD + 16, keys), BF)],
        compiler_params=params(),
        name="attn_forward",
    )(row0, a1, wq, kv, cos, sin, first)


def attn_backward(row0, q, kv, do, o, lse, cos, sin, first):
    groups, cols, rows = q.shape
    keys = kv.shape[1]
    whole = lambda *shape: pl.BlockSpec(shape, lambda i: (0,) * len(shape))
    part = lambda *shape: pl.BlockSpec((1,) + shape, lambda i: (i,) + (0,) * len(shape))
    return pl.pallas_call(
        attn_backward_kernel,
        grid=(groups,),
        in_specs=[pl.BlockSpec(memory_space=pltpu.SMEM), part(cols, rows), part(keys, 2 * HD), part(cols, rows), part(cols, rows), part(RATIO, rows), whole(HD, rows), whole(HD, rows), whole(1, rows)],
        out_specs=[part(cols, rows), part(keys, 2 * HD)],
        out_shape=[jax.ShapeDtypeStruct((groups, cols, rows), BF), jax.ShapeDtypeStruct((groups, keys, 2 * HD), F32)],
        scratch_shapes=[pltpu.VMEM((keys, rows), F32), pltpu.VMEM((keys, 2 * HD), F32)],
        compiler_params=params(),
        name="attn_backward",
    )(row0, q, kv, do, o, lse, cos, sin, first)


MESH = pl.DeviceIdType.MESH
ANY = pl.BlockSpec(memory_space=pl.ANY)


class Place:
    def __init__(self):
        d, self.t = lax.axis_index("dp"), lax.axis_index("tensor")
        self.c, self.p = d % 2, d // 2
        x, y = self.p % 2, self.p // 2
        self.px, self.py, self.pd = self.p + 1 - 2 * x, self.p + 2 - 4 * y, 3 - self.p
        self.across = [self.t + 1 - 2 * (self.t % 2), (self.t + 2) % 4, 3 - self.t]
        self.order = [self.t] + self.across

    def at(self, p, c, t):
        return {"dp": p * 2 + c, "tensor": t}

    def x_side(self):
        return self.at(self.px, self.c, self.t)

    def y_side(self):
        return self.at(self.py, self.c, self.t)

    def twin(self):
        return self.at(self.p, 1 - self.c, self.t)

    def line(self, t):
        return self.at(self.p, self.c, t)

    def greet(self):
        barrier = pltpu.get_barrier_semaphore()
        others = [self.x_side(), self.y_side(), self.twin()] + [self.line(t) for t in self.across]
        for other in others:
            pl.semaphore_signal(barrier, inc=1, device_id=other, device_id_type=MESH)
        pl.semaphore_wait(barrier, len(others))


def half_of(ref, part):
    rows = ref.shape[0] // 2
    return ref.at[pl.ds(part * rows, rows)]


def gather_kernel(kv, wq, wo, wg, wu, wd, kv_out, q_out, o_out, g_out, u_out, d_out, z_send, z_recv, send, recv, local):
    me = Place()
    me.greet()
    sources = [kv, wq, wo, wg, wu, wd]
    outs = [kv_out, q_out, o_out, g_out, u_out, d_out]

    def piece(k, s, p, c):
        if k == 2:
            return o_out.at[p, c, s]
        return outs[k].at[s, p, c] if k < 2 else outs[k].at[p, c]

    def pair(k, s, c):
        if k == 2:
            return o_out.at[:, c, s]
        return outs[k].at[s, :, c] if k < 2 else outs[k].at[:, c]

    def remote(src, dst, send_sem, recv_sem, to):
        copy = pltpu.make_async_remote_copy(src, dst, send_sem, recv_sem, device_id=to, device_id_type=MESH)
        copy.start()
        return copy

    lines = {}
    for k in range(3):
        for j, z in enumerate(me.across):
            lines[k, j + 1] = remote(sources[k], piece(k, me.t, me.p, me.c), z_send.at[k, j], z_recv.at[k, j], me.line(z))
    items = [(k, j) for k in range(3) for j in range(4)] + [(k, 0) for k in range(3, 6)]
    going = {}

    def push(i, kind, src, dst, to):
        going[i, kind] = remote(src, dst, send.at[i, kind], recv.at[i, kind], to)

    def first(i):
        k, j = items[i]
        s = me.order[j]
        mine = piece(k, s, me.p, me.c)
        if j == 0:
            src = sources[k]
            going[i, "local"] = pltpu.make_async_copy(src, mine, local.at[i])
            going[i, "local"].start()
        else:
            lines[k, j].wait_recv()
            src = mine
        push(i, 0, src, mine, me.x_side())
        push(i, 1, src, mine, me.y_side())

    def second(i):
        k, j = items[i]
        s = me.order[j]
        going[i, 0].wait_recv()
        part = half_of(piece(k, s, me.px, me.c), 0)
        push(i, 2, part, part, me.y_side())
        going[i, 1].wait_recv()
        part = half_of(piece(k, s, me.py, me.c), 1)
        push(i, 3, part, part, me.x_side())

    def third(i):
        k, j = items[i]
        going[i, 2].wait_recv()
        going[i, 3].wait_recv()
        if (i, "local") in going:
            going[i, "local"].wait()
        part = pair(k, me.order[j], me.c)
        push(i, 4, part, part, me.twin())

    count = len(items)
    for tick in range(count + 4):
        if tick < count:
            first(tick)
        if 0 <= tick - 1 < count:
            second(tick - 1)
        if 0 <= tick - 2 < count:
            third(tick - 2)
        if 0 <= tick - 4 < count:
            going[tick - 4, 4].wait_recv()
    for copy in lines.values():
        copy.wait_send()
    for i in range(count):
        for kind in range(5):
            going[i, kind].wait_send()


def gather_weights(kv, wq, wo, wg, wu, wd):
    dma = pltpu.SemaphoreType.DMA
    shape = lambda lead, w: jax.ShapeDtypeStruct(lead + w.shape, BF)
    return pl.pallas_call(
        gather_kernel,
        out_shape=[shape((4, 4, 2), kv), shape((4, 4, 2), wq), shape((4, 2, 4), wo), shape((4, 2), wg), shape((4, 2), wu), shape((4, 2), wd)],
        in_specs=[ANY] * 6,
        out_specs=[ANY] * 6,
        scratch_shapes=[dma((3, 3)), dma((3, 3)), dma((15, 5)), dma((15, 5)), dma((15,))],
        compiler_params=pltpu.CompilerParams(collective_id=1, has_side_effects=True, vmem_limit_bytes=48 * 2**20),
        name="gather_weights",
    )(kv, wq, wo, wg, wu, wd)


def xor4(a, m):
    return (a // 2 + m // 2) % 2 * 2 + (a % 2 + m % 2) % 2


def copy_to(src, dst, send_sem, recv_sem, to):
    return pltpu.make_async_remote_copy(src, dst, send_sem, recv_sem, device_id=to, device_id_type=MESH)


def add_low(left, right):
    return (left.astype(F32) + right.astype(F32)).astype(BF)


def mlp_kernel(a2_in, ct_in, wg_in, wu_in, wd_in, da2_out, mo_out, gg_out, gu_out, gd_out, twin_g, twin_u, twin_d, wg, wu, wd, a2_buf, ct_buf, mo_buf, a2_col, ct_col, zt, dg, du, out_buf, in_buf, diag_gu, x_gu, y_gu, diag_d, x_d, y_d, stage_gu, stage_d, load, store, line_send, line_recv, twin_send, twin_recv, send, recv, stage_sem):
    me = Place()
    rows, width = da2_out.shape
    hidden = wg.shape[1]
    cols = width // 8
    weights = [pltpu.make_async_copy(wg_in, wg, load.at[4]), pltpu.make_async_copy(wu_in, wu, load.at[5])]
    weights += [pltpu.make_async_copy(wd_in.at[d], wd.at[:, pl.ds(d * cols, cols)], load.at[6 + d]) for d in range(8)]
    for copy in weights:
        copy.start()

    def chunk_load(j, slot):
        s = xor4(me.t, 3 - j)
        return pltpu.make_async_copy(a2_in.at[s], a2_buf.at[slot], load.at[slot]), pltpu.make_async_copy(ct_in.at[s], ct_buf.at[slot], load.at[2 + slot])

    def chunk_send(j):
        return copy_to(out_buf.at[j], in_buf.at[2 - j], line_send.at[j], line_recv.at[2 - j], me.line(xor4(me.t, 3 - j)))

    def mo_store(j, slot):
        return pltpu.make_async_copy(mo_buf.at[slot], mo_out.at[xor4(me.t, 3 - j)], store.at[slot])

    for copy in chunk_load(0, 0):
        copy.start()
    me.greet()
    for copy in weights:
        copy.wait()

    def chunk(j, _):
        slot = j % 2

        @pl.when(j < 3)
        def _():
            for copy in chunk_load(j + 1, 1 - slot):
                copy.start()

        for copy in chunk_load(j, slot):
            copy.wait()
        where = pl.multiple_of(xor4(me.t, 3 - j) * rows, rows)
        g, u = dot_nn(a2_buf[slot], wg[...]), dot_nn(a2_buf[slot], wu[...])
        dz = dot_nt(ct_buf[slot], wd[...])
        sig = 1.0 / (1.0 + jnp.exp(-g))
        act = g * sig
        z = (act * u).astype(BF)
        zt[:, pl.ds(where, rows)] = z.T
        dg_now = (dz * u * (sig * (1.0 + g * (1.0 - sig)))).astype(BF)
        du_now = (dz * act).astype(BF)
        dg[pl.ds(where, rows)] = dg_now
        du[pl.ds(where, rows)] = du_now
        part = dot_nt(dg_now, wg[...]) + dot_nt(du_now, wu[...])

        @pl.when(j < 3)
        def _():
            out_buf[j] = part.astype(BF)
            chunk_send(j).start()

        @pl.when(j == 3)
        def _():
            da2_out[...] = part

        @pl.when(j >= 2)
        def _():
            mo_store(j - 2, slot).wait()

        mo_buf[slot] = dot_nn(z, wd[...]).astype(BF)
        mo_store(j, slot).start()
        return 0

    lax.fori_loop(0, 4, chunk, 0)
    mo_store(2, 0).wait()
    mo_store(3, 1).wait()

    def owner(i):
        return xor4(me.p, 3 - i % 4) * 2 + (1 - me.c + i // 4) % 2

    def tile_load(i, slot):
        at = pl.ds(pl.multiple_of(owner(i) * cols, cols), cols)
        return pltpu.make_async_copy(a2_in.at[:, :, at], a2_col.at[slot], load.at[slot]), pltpu.make_async_copy(ct_in.at[:, :, at], ct_col.at[slot], load.at[2 + slot])

    def piece(k, p, c):
        at = pl.ds(pl.multiple_of((p * 2 + c) * cols, cols), cols)
        return (wg, wu)[k].at[at] if k < 2 else wd.at[:, at]

    twins = [twin_g, twin_u, twin_d]

    def twin_push(k, i):
        p = xor4(me.p, 3 - i)
        return copy_to(piece(k, p, 1 - me.c), twins[k].at[p], twin_send.at[k, i], twin_recv.at[k, i], me.twin())

    for copy in tile_load(0, 0):
        copy.start()

    def tile(i, _):
        slot = i % 2

        @pl.when(i < 7)
        def _():
            for copy in tile_load(i + 1, 1 - slot):
                copy.start()

        for copy in tile_load(i, slot):
            copy.wait()
        at = pl.ds(pl.multiple_of(owner(i) * cols, cols), cols)
        a2t = a2_col[slot].reshape(4 * rows, cols).T
        wg[at] = dot_nn(a2t, dg[...]).astype(BF)
        wu[at] = dot_nn(a2t, du[...]).astype(BF)
        wd[:, at] = dot_nn(zt[...], ct_col[slot].reshape(4 * rows, cols)).astype(BF)

        @pl.when(i < 4)
        def _():
            for k in range(3):
                twin_push(k, i).start()

        return 0

    lax.fori_loop(0, 8, tile, 0)

    diag = [diag_gu.at[0], diag_gu.at[1], diag_d]
    from_x = [x_gu.at[0], x_gu.at[1], x_d]
    from_y = [y_gu.at[0], y_gu.at[1], y_d]
    stage = [stage_gu.at[0], stage_gu.at[1], stage_d]

    def side(k, kind):
        if kind < 2:
            src, dst = half_of(piece(k, me.pd, me.c), kind), half_of(diag[k], kind)
        else:
            src, dst = (piece(k, me.px, me.c), from_x[k]) if kind == 2 else (piece(k, me.py, me.c), from_y[k])
        return copy_to(src, dst, send.at[k, kind], recv.at[k, kind], me.x_side() if kind % 2 == 0 else me.y_side())

    steps = [(k, i) for i in range(4) for k in range(3)]

    def fetch(n):
        k, i = steps[n]
        twin_push(k, i).wait_recv()
        copy = pltpu.make_async_copy(twins[k].at[xor4(me.p, 3 - i)], stage[k], stage_sem.at[k])
        copy.start()
        return copy

    def add_twin(n, copy):
        k, i = steps[n]
        copy.wait()
        mine = piece(k, xor4(me.p, 3 - i), me.c)
        mine[...] = add_low(mine[...], stage[k][...])
        if i == 0:
            side(k, 0).start()
            side(k, 1).start()

    ahead = fetch(0)
    for n in range(12):
        now = ahead
        if n + 1 < 12:
            ahead = fetch(n + 1)
        add_twin(n, now)
    for k in range(3):
        side(k, 1).wait_recv()
        part, extra = half_of(piece(k, me.px, me.c), 1), half_of(diag[k], 1)
        part[...] = add_low(part[...], extra[...])
        side(k, 2).start()
        side(k, 0).wait_recv()
        part, extra = half_of(piece(k, me.py, me.c), 0), half_of(diag[k], 0)
        part[...] = add_low(part[...], extra[...])
        side(k, 3).start()
    results = []
    for k in range(3):
        side(k, 2).wait_recv()
        side(k, 3).wait_recv()
        mine = piece(k, me.p, me.c)
        mine[...] = (mine[...].astype(F32) + from_x[k][...].astype(F32) + from_y[k][...].astype(F32)).astype(BF)
        results.append(pltpu.make_async_copy(mine, (gg_out, gu_out, gd_out)[k], stage_sem.at[k]))
        results[-1].start()
    for j in range(3):
        chunk_send(j).wait_recv()
    da2_out[...] += in_buf[0].astype(F32) + in_buf[1].astype(F32) + in_buf[2].astype(F32)
    for copy in results:
        copy.wait()
    for j in range(3):
        chunk_send(j).wait_send()
    for k in range(3):
        for i in range(4):
            twin_push(k, i).wait_send()
            side(k, i).wait_send()


def mlp(a2, ct, wg, wu, wd):
    chunks, rows, width = a2.shape
    hidden, cols = wg.shape[1], width // 8
    dma, vmem = pltpu.SemaphoreType.DMA, lambda *shape: pltpu.VMEM(shape, BF)
    shape = lambda *dims: jax.ShapeDtypeStruct(dims, BF)
    return pl.pallas_call(
        mlp_kernel,
        out_shape=[jax.ShapeDtypeStruct((rows, width), F32), shape(4, rows, width), shape(cols, hidden), shape(cols, hidden), shape(hidden, cols), shape(4, cols, hidden), shape(4, cols, hidden), shape(4, hidden, cols)],
        in_specs=[ANY] * 5,
        out_specs=[pl.BlockSpec(memory_space=pltpu.VMEM)] + [ANY] * 7,
        scratch_shapes=[
            vmem(width, hidden), vmem(width, hidden), vmem(hidden, width),
            vmem(2, rows, width), vmem(2, rows, width), vmem(2, rows, width),
            vmem(2, 4, rows, cols), vmem(2, 4, rows, cols),
            vmem(hidden, 4 * rows), vmem(4 * rows, hidden), vmem(4 * rows, hidden),
            vmem(3, rows, width), vmem(3, rows, width),
            vmem(2, cols, hidden), vmem(2, cols, hidden), vmem(2, cols, hidden),
            vmem(hidden, cols), vmem(hidden, cols), vmem(hidden, cols),
            vmem(2, cols, hidden), vmem(hidden, cols),
            dma((14,)), dma((2,)), dma((3,)), dma((3,)), dma((3, 4)), dma((3, 4)), dma((3, 4)), dma((3, 4)), dma((3,)),
        ],
        compiler_params=pltpu.CompilerParams(collective_id=2, has_side_effects=True, vmem_limit_bytes=62 * 2**20),
        name="mlp",
    )(a2, ct, wg, wu, wd)[:5]


def home(v, dim):
    return lax.psum_scatter(v.astype(BF), "dp", scatter_dimension=dim, tiled=True)


def mlp_plain(h, a2, cot, wg, wu, wd):
    g, u = dot_nn(a2, wg), dot_nn(a2, wu)
    sig = jax.nn.sigmoid(g)
    act = g * sig
    z = (act * u).astype(BF)
    scatter = lambda v: lax.psum_scatter(v.astype(BF), "tensor", scatter_dimension=0, tiled=True).astype(F32)
    output = (h + scatter(dot_nn(z, wd))).astype(BF)
    dz = dot_nt(cot, wd)
    dg = (dz * u * (sig * (1.0 + g * (1.0 - sig)))).astype(BF)
    du = (dz * act).astype(BF)
    gd = home(dot_tn(z, cot), 1).astype(F32)
    gg = home(dot_tn(a2, dg), 0).astype(F32)
    gu = home(dot_tn(a2, du), 0).astype(F32)
    da2 = scatter(dot_nt(dg, wg) + dot_nt(du, wu))
    return output, da2, gg, gu, gd


def body(tokens, segments, attn_gain, w_query, w_key, w_value, w_out, mlp_gain, w_gate, w_up, w_down, cotangent):
    rows, width = tokens.shape
    hidden = w_gate.shape[1]
    nt = lax.axis_size("tensor")
    row0 = lax.axis_index("tensor") * rows
    keys = segments.shape[0]

    own_seg = lax.dynamic_slice_in_dim(segments, row0, rows)
    first = jnp.sum((segments[:, None] < own_seg[None, :]).astype(jnp.int32), axis=0)
    index = jnp.arange(rows, dtype=jnp.int32) + row0
    freq = jnp.exp(jnp.arange(HD // 2, dtype=F32) * (-2.0 * math.log(10000.0) / HD))
    angle = freq[:, None] * (index - first).astype(F32)[None, :]
    cos, sin = jnp.cos(angle), jnp.sin(angle)
    cos, sin = jnp.concatenate([cos, cos], 0), jnp.concatenate([sin, sin], 0)
    first = first[None, :]
    row0_s = row0[None].astype(jnp.int32)

    gain1 = lax.all_gather(attn_gain, "dp", axis=0, tiled=True).astype(F32)
    gain2 = lax.all_gather(mlp_gain, "dp", axis=0, tiled=True).astype(F32)
    w_kv = jnp.concatenate([w_key, w_value], 1)
    if lax.axis_size("dp") == 8 and nt == 4:
        wkv, wq, wo, wg, wu, wd = gather_weights(w_kv, w_query, w_out, w_gate, w_up, w_down)
        wkv, wq = wkv.reshape(4, width, -1), wq.reshape(4, width, -1)
        wo = wo.reshape(8, width, -1).transpose(1, 0, 2).reshape(width, width)
        wg, wu = wg.reshape(width, -1), wu.reshape(width, -1)
        wd8 = wd.reshape(8, hidden, -1)
    else:
        full = lambda w, axis: lax.all_gather(lax.all_gather(w, "dp", axis=axis, tiled=True), "tensor", axis=0)
        wq = full(w_query, 0)
        wkv = full(w_kv, 0)
        wo = full(w_out, 1).reshape(width, width)
        wg = lax.all_gather(w_gate, "dp", axis=0, tiled=True)
        wu = lax.all_gather(w_up, "dp", axis=0, tiled=True)
        wd = lax.all_gather(w_down, "dp", axis=1, tiled=True)

    x = tokens.astype(F32)
    n1, r1 = rms_forward(x, gain1)
    a1 = n1.astype(BF)
    kv = jnp.einsum("rd,gdc->grc", a1, wkv, preferred_element_type=F32)
    cos_r, sin_r = cos.T, sin.T
    k = kv[..., :HD]
    k = k * cos_r + jnp.concatenate([-k[..., HD // 2 :], k[..., : HD // 2]], -1) * sin_r
    kv = jnp.concatenate([k, kv[..., HD:]], -1).astype(BF)
    kv = lax.all_gather(kv, "tensor", axis=1, tiled=True)
    o, q, lse = attn_forward(row0_s, a1, wq, kv, cos, sin, first)
    o2 = o.reshape(-1, rows)
    h = x + dot_tn(o2, wo)

    n2, r2 = rms_forward(h, gain2)
    a2 = lax.all_gather(n2.astype(BF), "tensor", axis=0, tiled=True)
    cot = lax.all_gather(cotangent, "tensor", axis=0, tiled=True)
    if lax.axis_size("dp") == 8 and nt == 4:
        da2, mo, gg, gu, gd = mlp(a2.reshape(4, rows, width), cot.reshape(4, rows, width), wg, wu, wd8)
        output = (h + lax.psum_scatter(mo.reshape(4 * rows, width), "tensor", scatter_dimension=0, tiled=True).astype(F32)).astype(BF)
        gg, gu, gd = gg.astype(F32), gu.astype(F32), gd.astype(F32)
    else:
        output, da2, gg, gu, gd = mlp_plain(h, a2, cot, wg, wu, wd)
    dres, gain2_part = rms_backward(h, r2, gain2, da2)
    dh = cotangent.astype(F32) + dres
    dhb = dh.astype(BF)

    do = dot_nt(wo, dhb).astype(BF).reshape(o.shape)
    go_part = dot_nn(o2, dhb)
    dq, dkv = attn_backward(row0_s, q, kv, do, o, lse, cos, sin, first)
    groups = dkv.shape[0]
    dkv = lax.psum_scatter(dkv.astype(BF), "tensor", scatter_dimension=1, tiled=True).astype(F32)
    dk = dkv[..., :HD]
    ws = dk * sin_r
    dk = dk * cos_r + jnp.concatenate([ws[..., HD // 2 :], -ws[..., : HD // 2]], -1)
    dkv = jnp.concatenate([dk, dkv[..., HD:]], -1).astype(BF)
    gq_part = jnp.einsum("rd,gcr->gdc", a1, dq, preferred_element_type=F32)
    gkv_part = jnp.einsum("rd,grc->gdc", a1, dkv, preferred_element_type=F32)
    da1 = jnp.einsum("gcr,gdc->rd", dq, wq, preferred_element_type=F32) + jnp.einsum("grc,gdc->rd", dkv, wkv, preferred_element_type=F32)
    din, gain1_part = rms_backward(x, r1, gain1, da1)
    grad_tokens = dh + din

    def home_all(v, dim):
        return lax.psum_scatter(home(v, dim + 1), "tensor", scatter_dimension=0, tiled=False).astype(F32)

    gq = home_all(gq_part, 0)
    gkv = home_all(gkv_part, 0)
    go = home_all(go_part.reshape(nt, -1, width), 1)
    gains = lax.psum_scatter(jnp.stack([gain1_part, gain2_part]), "dp", scatter_dimension=1, tiled=True)
    gains = lax.psum(gains, "tensor")
    return (output, grad_tokens, gains[0], gq, gkv[:, :HD], gkv[:, HD:], go, gains[1], gg, gu, gd)


def solution(mesh):
    rows, block = P(("dp", "tensor"), None), P("dp", "tensor")
    turned, line = P("tensor", "dp"), P("dp")
    return jax.shard_map(
        body,
        mesh=mesh,
        in_specs=(rows, line, line, block, block, block, turned, line, block, block, turned, rows),
        out_specs=(rows, rows, line, block, block, block, turned, line, block, block, turned),
        check_vma=False,
    )
```

```python
import functools
import math

import jax
import jax.numpy as jnp
from jax import lax
from jax.experimental import pallas as pl
from jax.experimental.pallas import tpu as pltpu
from jax.sharding import PartitionSpec as P

HD = 64
RATIO = 8
EPSILON = 1e-05
MASKED = -1e30
BF = jnp.bfloat16
F32 = jnp.float32


def dot_nn(left, right):
    return lax.dot_general(left, right, (((1,), (0,)), ((), ())), preferred_element_type=F32)


def dot_nt(left, right):
    return lax.dot_general(left, right, (((1,), (1,)), ((), ())), preferred_element_type=F32)


def dot_tn(left, right):
    return lax.dot_general(left, right, (((0,), (0,)), ((), ())), preferred_element_type=F32)


def rms_forward(values_in, gain_row):
    factor = lax.rsqrt(jnp.mean(values_in * values_in, axis=-1, keepdims=True) + EPSILON)
    return (values_in * factor * gain_row, factor)


def rms_backward(values_in, factor, gain_row, gradient):
    scaled = gain_row * gradient
    grad_gain = jnp.sum(gradient * values_in * factor, axis=0)
    grad_input = factor * scaled - values_in * (factor * factor * factor) * jnp.mean(
        scaled * values_in, axis=-1, keepdims=True
    )
    return (grad_input, grad_gain)


def rope_t(u, cos, sin):
    half = HD // 2
    return u * cos + jnp.concatenate([-u[half:], u[:half]], 0) * sin


def rope_back_t(w, cos, sin):
    half = HD // 2
    ws = w * sin
    return w * cos + jnp.concatenate([ws[half:], -ws[:half]], 0)


def bias_of(first, row0, keys, rows):
    key = lax.broadcasted_iota(jnp.int32, (keys, rows), 0)
    row = lax.broadcasted_iota(jnp.int32, (keys, rows), 1) + row0
    return jnp.where((key <= row) & (key >= first), 0.0, MASKED).astype(F32)


def attn_forward_kernel(row0_ref, a1_ref, wq_ref, kv_ref, cos_ref, sin_ref, first_ref, o_ref, q_ref, lse_ref, bias_ref, s_ref, vt_ref):
    keys, rows = bias_ref.shape

    @pl.when(pl.program_id(0) == 0)
    def _():
        bias_ref[...] = bias_of(first_ref[...], row0_ref[0], keys, rows)

    kv = kv_ref[0]
    kvt = kv.T
    vt_ref[...] = jnp.concatenate([kvt[HD:], jnp.ones((16, keys), BF)], 0)
    qt = dot_nn(a1_ref[...], wq_ref[0]).T
    cos, sin = cos_ref[...], sin_ref[...]
    for h in range(RATIO):
        q = (rope_t(qt[h * HD : (h + 1) * HD], cos, sin) * HD ** (-0.5)).astype(BF)
        q_ref[0, h * HD : (h + 1) * HD] = q
        s_ref[...] = dot_nn(kv, jnp.concatenate([q, jnp.zeros_like(q)], 0)) + bias_ref[...]
        peak = jnp.max(s_ref[...], axis=0, keepdims=True)
        e = jnp.exp(s_ref[...] - peak).astype(BF)
        ot = dot_nn(vt_ref[...], e)
        total = ot[HD : HD + 1]
        o_ref[0, h * HD : (h + 1) * HD] = (ot[:HD] / total).astype(BF)
        lse_ref[0, h : h + 1] = peak + jnp.log(total)


def attn_backward_kernel(row0_ref, q_ref, kv_ref, do_ref, o_ref, lse_ref, cos_ref, sin_ref, first_ref, dq_ref, dkv_ref, bias_ref, acc_ref):
    keys, rows = bias_ref.shape

    @pl.when(pl.program_id(0) == 0)
    def _():
        bias_ref[...] = bias_of(first_ref[...], row0_ref[0], keys, rows)

    kv = kv_ref[0]
    kt = kv.T[:HD]
    cos, sin = cos_ref[...], sin_ref[...]
    for h in range(RATIO):
        part = slice(h * HD, (h + 1) * HD)
        q, do, o = q_ref[0, part], do_ref[0, part], o_ref[0, part]
        qz = jnp.concatenate([q, jnp.zeros_like(q)], 0)
        doz = jnp.concatenate([jnp.zeros_like(do), do], 0)
        delta = jnp.sum(do.astype(F32) * o.astype(F32), axis=0, keepdims=True)
        p = jnp.exp(dot_nn(kv, qz) + bias_ref[...] - lse_ref[0, h : h + 1])
        ds = (p * (dot_nn(kv, doz) - delta)).astype(BF)
        grad = dot_nt(ds, qz) + dot_nt(p.astype(BF), doz)
        if h == 0:
            acc_ref[...] = grad
        else:
            acc_ref[...] += grad
        dq = dot_nn(kt, ds) * HD ** (-0.5)
        dq_ref[0, part] = rope_back_t(dq, cos, sin).astype(BF)
    dkv_ref[0] = acc_ref[...]


def params():
    return pltpu.CompilerParams(vmem_limit_bytes=56 * 2**20)


def attn_forward(row0, a1, wq, kv, cos, sin, first):
    groups, width, cols = wq.shape
    rows, keys = a1.shape[0], kv.shape[1]
    whole = lambda *shape: pl.BlockSpec(shape, lambda i: (0,) * len(shape))
    part = lambda *shape: pl.BlockSpec((1,) + shape, lambda i: (i,) + (0,) * len(shape))
    return pl.pallas_call(
        attn_forward_kernel,
        grid=(groups,),
        in_specs=[pl.BlockSpec(memory_space=pltpu.SMEM), whole(rows, width), part(width, cols), part(keys, 2 * HD), whole(HD, rows), whole(HD, rows), whole(1, rows)],
        out_specs=[part(cols, rows), part(cols, rows), part(RATIO, rows)],
        out_shape=[jax.ShapeDtypeStruct((groups, cols, rows), BF), jax.ShapeDtypeStruct((groups, cols, rows), BF), jax.ShapeDtypeStruct((groups, RATIO, rows), F32)],
        scratch_shapes=[pltpu.VMEM((keys, rows), F32), pltpu.VMEM((keys, rows), F32), pltpu.VMEM((HD + 16, keys), BF)],
        compiler_params=params(),
        name="attn_forward",
    )(row0, a1, wq, kv, cos, sin, first)


def attn_backward(row0, q, kv, do, o, lse, cos, sin, first):
    groups, cols, rows = q.shape
    keys = kv.shape[1]
    whole = lambda *shape: pl.BlockSpec(shape, lambda i: (0,) * len(shape))
    part = lambda *shape: pl.BlockSpec((1,) + shape, lambda i: (i,) + (0,) * len(shape))
    return pl.pallas_call(
        attn_backward_kernel,
        grid=(groups,),
        in_specs=[pl.BlockSpec(memory_space=pltpu.SMEM), part(cols, rows), part(keys, 2 * HD), part(cols, rows), part(cols, rows), part(RATIO, rows), whole(HD, rows), whole(HD, rows), whole(1, rows)],
        out_specs=[part(cols, rows), part(keys, 2 * HD)],
        out_shape=[jax.ShapeDtypeStruct((groups, cols, rows), BF), jax.ShapeDtypeStruct((groups, keys, 2 * HD), F32)],
        scratch_shapes=[pltpu.VMEM((keys, rows), F32), pltpu.VMEM((keys, 2 * HD), F32)],
        compiler_params=params(),
        name="attn_backward",
    )(row0, q, kv, do, o, lse, cos, sin, first)


MESH = pl.DeviceIdType.MESH
ANY = pl.BlockSpec(memory_space=pl.ANY)


class Place:
    def __init__(self):
        d, self.t = lax.axis_index("dp"), lax.axis_index("tensor")
        self.c, self.p = d % 2, d // 2
        x, y = self.p % 2, self.p // 2
        self.px, self.py, self.pd = self.p + 1 - 2 * x, self.p + 2 - 4 * y, 3 - self.p
        self.across = [self.t + 1 - 2 * (self.t % 2), (self.t + 2) % 4, 3 - self.t]
        self.order = [self.t] + self.across

    def at(self, p, c, t):
        return {"dp": p * 2 + c, "tensor": t}

    def x_side(self):
        return self.at(self.px, self.c, self.t)

    def y_side(self):
        return self.at(self.py, self.c, self.t)

    def twin(self):
        return self.at(self.p, 1 - self.c, self.t)

    def line(self, t):
        return self.at(self.p, self.c, t)

    def greet(self):
        barrier = pltpu.get_barrier_semaphore()
        others = [self.x_side(), self.y_side(), self.twin()] + [self.line(t) for t in self.across]
        for other in others:
            pl.semaphore_signal(barrier, inc=1, device_id=other, device_id_type=MESH)
        pl.semaphore_wait(barrier, len(others))


def half_of(ref, part):
    rows = ref.shape[0] // 2
    return ref.at[pl.ds(part * rows, rows)]


def gather_kernel(kv, wq, wo, wg, wu, wd, kv_out, q_out, o_out, g_out, u_out, d_out, z_send, z_recv, send, recv, local):
    me = Place()
    me.greet()
    sources = [kv, wq, wo, wg, wu, wd]
    outs = [kv_out, q_out, o_out, g_out, u_out, d_out]

    def piece(k, s, p, c):
        if k == 2:
            return o_out.at[p, c, s]
        return outs[k].at[s, p, c] if k < 2 else outs[k].at[p, c]

    def pair(k, s, c):
        if k == 2:
            return o_out.at[:, c, s]
        return outs[k].at[s, :, c] if k < 2 else outs[k].at[:, c]

    def remote(src, dst, send_sem, recv_sem, to):
        copy = pltpu.make_async_remote_copy(src, dst, send_sem, recv_sem, device_id=to, device_id_type=MESH)
        copy.start()
        return copy

    lines = {}
    for k in range(3):
        for j, z in enumerate(me.across):
            lines[k, j + 1] = remote(sources[k], piece(k, me.t, me.p, me.c), z_send.at[k, j], z_recv.at[k, j], me.line(z))
    items = [(k, j) for k in range(3) for j in range(4)] + [(k, 0) for k in range(3, 6)]
    going = {}

    def push(i, kind, src, dst, to):
        going[i, kind] = remote(src, dst, send.at[i, kind], recv.at[i, kind], to)

    def first(i):
        k, j = items[i]
        s = me.order[j]
        mine = piece(k, s, me.p, me.c)
        if j == 0:
            src = sources[k]
            going[i, "local"] = pltpu.make_async_copy(src, mine, local.at[i])
            going[i, "local"].start()
        else:
            lines[k, j].wait_recv()
            src = mine
        push(i, 0, src, mine, me.x_side())
        push(i, 1, src, mine, me.y_side())

    def second(i):
        k, j = items[i]
        s = me.order[j]
        going[i, 0].wait_recv()
        part = half_of(piece(k, s, me.px, me.c), 0)
        push(i, 2, part, part, me.y_side())
        going[i, 1].wait_recv()
        part = half_of(piece(k, s, me.py, me.c), 1)
        push(i, 3, part, part, me.x_side())

    def third(i):
        k, j = items[i]
        going[i, 2].wait_recv()
        going[i, 3].wait_recv()
        if (i, "local") in going:
            going[i, "local"].wait()
        part = pair(k, me.order[j], me.c)
        push(i, 4, part, part, me.twin())

    count = len(items)
    for tick in range(count + 4):
        if tick < count:
            first(tick)
        if 0 <= tick - 1 < count:
            second(tick - 1)
        if 0 <= tick - 2 < count:
            third(tick - 2)
        if 0 <= tick - 4 < count:
            going[tick - 4, 4].wait_recv()
    for copy in lines.values():
        copy.wait_send()
    for i in range(count):
        for kind in range(5):
            going[i, kind].wait_send()


def gather_weights(kv, wq, wo, wg, wu, wd):
    dma = pltpu.SemaphoreType.DMA
    shape = lambda lead, w: jax.ShapeDtypeStruct(lead + w.shape, BF)
    return pl.pallas_call(
        gather_kernel,
        out_shape=[shape((4, 4, 2), kv), shape((4, 4, 2), wq), shape((4, 2, 4), wo), shape((4, 2), wg), shape((4, 2), wu), shape((4, 2), wd)],
        in_specs=[ANY] * 6,
        out_specs=[ANY] * 6,
        scratch_shapes=[dma((3, 3)), dma((3, 3)), dma((15, 5)), dma((15, 5)), dma((15,))],
        compiler_params=pltpu.CompilerParams(collective_id=1, has_side_effects=True, vmem_limit_bytes=48 * 2**20),
        name="gather_weights",
    )(kv, wq, wo, wg, wu, wd)


def xor4(a, m):
    return (a // 2 + m // 2) % 2 * 2 + (a % 2 + m % 2) % 2


def copy_to(src, dst, send_sem, recv_sem, to):
    return pltpu.make_async_remote_copy(src, dst, send_sem, recv_sem, device_id=to, device_id_type=MESH)


def add_low(left, right):
    return (left.astype(F32) + right.astype(F32)).astype(BF)


def mlp_kernel(a2_in, ct_in, wg_in, wu_in, wd_in, da2_out, mo_out, mo_got, gg_out, gu_out, gd_out, twin_g, twin_u, twin_d, wg, wu, wd, a2_buf, ct_buf, mo_buf, a2_col, ct_col, zt, dg, du, out_buf, in_buf, diag_gu, x_gu, y_gu, diag_d, x_d, y_d, stage_gu, stage_d, load, store, line_send, line_recv, mo_send, mo_recv, twin_send, twin_recv, send, recv, stage_sem):
    me = Place()
    rows, width = da2_out.shape
    hidden = wg.shape[1]
    cols = width // 8
    weights = [pltpu.make_async_copy(wg_in, wg, load.at[4]), pltpu.make_async_copy(wu_in, wu, load.at[5])]
    weights += [pltpu.make_async_copy(wd_in.at[d], wd.at[:, pl.ds(d * cols, cols)], load.at[6 + d]) for d in range(8)]
    for copy in weights:
        copy.start()

    def chunk_load(j, slot):
        s = xor4(me.t, 3 - j)
        return pltpu.make_async_copy(a2_in.at[s], a2_buf.at[slot], load.at[slot]), pltpu.make_async_copy(ct_in.at[s], ct_buf.at[slot], load.at[2 + slot])

    def chunk_send(j):
        return copy_to(out_buf.at[j], in_buf.at[2 - j], line_send.at[j], line_recv.at[2 - j], me.line(xor4(me.t, 3 - j)))

    def mo_store(j, slot):
        return pltpu.make_async_copy(mo_buf.at[slot], mo_out.at[xor4(me.t, 3 - j)], store.at[slot])

    for copy in chunk_load(0, 0):
        copy.start()
    me.greet()
    for copy in weights:
        copy.wait()

    def chunk(j, _):
        slot = j % 2

        @pl.when(j < 3)
        def _():
            for copy in chunk_load(j + 1, 1 - slot):
                copy.start()

        for copy in chunk_load(j, slot):
            copy.wait()
        where = pl.multiple_of(xor4(me.t, 3 - j) * rows, rows)
        g, u = dot_nn(a2_buf[slot], wg[...]), dot_nn(a2_buf[slot], wu[...])
        dz = dot_nt(ct_buf[slot], wd[...])
        sig = 1.0 / (1.0 + jnp.exp(-g))
        act = g * sig
        z = (act * u).astype(BF)
        zt[:, pl.ds(where, rows)] = z.T
        dg_now = (dz * u * (sig * (1.0 + g * (1.0 - sig)))).astype(BF)
        du_now = (dz * act).astype(BF)
        dg[pl.ds(where, rows)] = dg_now
        du[pl.ds(where, rows)] = du_now
        part = dot_nt(dg_now, wg[...]) + dot_nt(du_now, wu[...])

        @pl.when(j < 3)
        def _():
            out_buf[j] = part.astype(BF)
            chunk_send(j).start()

        @pl.when(j == 3)
        def _():
            da2_out[...] = part

        @pl.when(j >= 2)
        def _():
            mo_store(j - 2, slot).wait()

        mo_buf[slot] = dot_nn(z, wd[...]).astype(BF)
        mo_store(j, slot).start()
        return 0

    lax.fori_loop(0, 4, chunk, 0)
    mo_store(2, 0).wait()
    mo_store(3, 1).wait()

    def mo_push(m):
        return copy_to(mo_out.at[xor4(me.t, m)], mo_got.at[m - 1], mo_send.at[m - 1], mo_recv.at[m - 1], me.line(xor4(me.t, m)))

    for m in (1, 2):
        mo_push(m).start()

    def owner(i):
        return xor4(me.p, 3 - i % 4) * 2 + (1 - me.c + i // 4) % 2

    def tile_load(i, slot):
        at = pl.ds(pl.multiple_of(owner(i) * cols, cols), cols)
        return pltpu.make_async_copy(a2_in.at[:, :, at], a2_col.at[slot], load.at[slot]), pltpu.make_async_copy(ct_in.at[:, :, at], ct_col.at[slot], load.at[2 + slot])

    def piece(k, p, c):
        at = pl.ds(pl.multiple_of((p * 2 + c) * cols, cols), cols)
        return (wg, wu)[k].at[at] if k < 2 else wd.at[:, at]

    twins = [twin_g, twin_u, twin_d]

    def twin_push(k, i):
        p = xor4(me.p, 3 - i)
        return copy_to(piece(k, p, 1 - me.c), twins[k].at[p], twin_send.at[k, i], twin_recv.at[k, i], me.twin())

    for copy in tile_load(0, 0):
        copy.start()

    def tile(i, _):
        slot = i % 2

        @pl.when(i < 7)
        def _():
            for copy in tile_load(i + 1, 1 - slot):
                copy.start()

        for copy in tile_load(i, slot):
            copy.wait()
        at = pl.ds(pl.multiple_of(owner(i) * cols, cols), cols)
        a2t = a2_col[slot].reshape(4 * rows, cols).T
        wg[at] = dot_nn(a2t, dg[...]).astype(BF)
        wu[at] = dot_nn(a2t, du[...]).astype(BF)
        wd[:, at] = dot_nn(zt[...], ct_col[slot].reshape(4 * rows, cols)).astype(BF)

        @pl.when(i < 4)
        def _():
            for k in range(3):
                twin_push(k, i).start()

        return 0

    lax.fori_loop(0, 8, tile, 0)

    diag = [diag_gu.at[0], diag_gu.at[1], diag_d]
    from_x = [x_gu.at[0], x_gu.at[1], x_d]
    from_y = [y_gu.at[0], y_gu.at[1], y_d]
    stage = [stage_gu.at[0], stage_gu.at[1], stage_d]

    def side(k, kind):
        if kind < 2:
            src, dst = half_of(piece(k, me.pd, me.c), kind), half_of(diag[k], kind)
        else:
            src, dst = (piece(k, me.px, me.c), from_x[k]) if kind == 2 else (piece(k, me.py, me.c), from_y[k])
        return copy_to(src, dst, send.at[k, kind], recv.at[k, kind], me.x_side() if kind % 2 == 0 else me.y_side())

    steps = [(k, i) for i in range(4) for k in range(3)]

    def fetch(n):
        k, i = steps[n]
        twin_push(k, i).wait_recv()
        copy = pltpu.make_async_copy(twins[k].at[xor4(me.p, 3 - i)], stage[k], stage_sem.at[k])
        copy.start()
        return copy

    def add_twin(n, copy):
        k, i = steps[n]
        copy.wait()
        mine = piece(k, xor4(me.p, 3 - i), me.c)
        mine[...] = add_low(mine[...], stage[k][...])
        if i == 0:
            side(k, 0).start()
            side(k, 1).start()

    ahead = fetch(0)
    for n in range(12):
        now = ahead
        if n + 1 < 12:
            ahead = fetch(n + 1)
        add_twin(n, now)
    for k in range(3):
        side(k, 1).wait_recv()
        part, extra = half_of(piece(k, me.px, me.c), 1), half_of(diag[k], 1)
        part[...] = add_low(part[...], extra[...])
        side(k, 2).start()
        side(k, 0).wait_recv()
        part, extra = half_of(piece(k, me.py, me.c), 0), half_of(diag[k], 0)
        part[...] = add_low(part[...], extra[...])
        side(k, 3).start()
    results = []
    for k in range(3):
        side(k, 2).wait_recv()
        side(k, 3).wait_recv()
        mine = piece(k, me.p, me.c)
        mine[...] = (mine[...].astype(F32) + from_x[k][...].astype(F32) + from_y[k][...].astype(F32)).astype(BF)
        results.append(pltpu.make_async_copy(mine, (gg_out, gu_out, gd_out)[k], stage_sem.at[k]))
        results[-1].start()
    for j in range(3):
        chunk_send(j).wait_recv()
    da2_out[...] += in_buf[0].astype(F32) + in_buf[1].astype(F32) + in_buf[2].astype(F32)
    for copy in results:
        copy.wait()
    for m in (1, 2):
        mo_push(m).wait()
    for j in range(3):
        chunk_send(j).wait_send()
    for k in range(3):
        for i in range(4):
            twin_push(k, i).wait_send()
            side(k, i).wait_send()


def mlp(a2, ct, wg, wu, wd):
    chunks, rows, width = a2.shape
    hidden, cols = wg.shape[1], width // 8
    dma, vmem = pltpu.SemaphoreType.DMA, lambda *shape: pltpu.VMEM(shape, BF)
    shape = lambda *dims: jax.ShapeDtypeStruct(dims, BF)
    return pl.pallas_call(
        mlp_kernel,
        out_shape=[jax.ShapeDtypeStruct((rows, width), F32), shape(4, rows, width), shape(2, rows, width), shape(cols, hidden), shape(cols, hidden), shape(hidden, cols), shape(4, cols, hidden), shape(4, cols, hidden), shape(4, hidden, cols)],
        in_specs=[ANY] * 5,
        out_specs=[pl.BlockSpec(memory_space=pltpu.VMEM)] + [ANY] * 8,
        scratch_shapes=[
            vmem(width, hidden), vmem(width, hidden), vmem(hidden, width),
            vmem(2, rows, width), vmem(2, rows, width), vmem(2, rows, width),
            vmem(2, 4, rows, cols), vmem(2, 4, rows, cols),
            vmem(hidden, 4 * rows), vmem(4 * rows, hidden), vmem(4 * rows, hidden),
            vmem(3, rows, width), vmem(3, rows, width),
            vmem(2, cols, hidden), vmem(2, cols, hidden), vmem(2, cols, hidden),
            vmem(hidden, cols), vmem(hidden, cols), vmem(hidden, cols),
            vmem(2, cols, hidden), vmem(hidden, cols),
            dma((14,)), dma((2,)), dma((3,)), dma((3,)), dma((2,)), dma((2,)), dma((3, 4)), dma((3, 4)), dma((3, 4)), dma((3, 4)), dma((3,)),
        ],
        compiler_params=pltpu.CompilerParams(collective_id=2, has_side_effects=True, vmem_limit_bytes=62 * 2**20),
        name="mlp",
    )(a2, ct, wg, wu, wd)[:6]


def home(v, dim):
    return lax.psum_scatter(v.astype(BF), "dp", scatter_dimension=dim, tiled=True)


def mlp_plain(h, a2, cot, wg, wu, wd):
    g, u = dot_nn(a2, wg), dot_nn(a2, wu)
    sig = jax.nn.sigmoid(g)
    act = g * sig
    z = (act * u).astype(BF)
    scatter = lambda v: lax.psum_scatter(v.astype(BF), "tensor", scatter_dimension=0, tiled=True).astype(F32)
    output = (h + scatter(dot_nn(z, wd))).astype(BF)
    dz = dot_nt(cot, wd)
    dg = (dz * u * (sig * (1.0 + g * (1.0 - sig)))).astype(BF)
    du = (dz * act).astype(BF)
    gd = home(dot_tn(z, cot), 1).astype(F32)
    gg = home(dot_tn(a2, dg), 0).astype(F32)
    gu = home(dot_tn(a2, du), 0).astype(F32)
    da2 = scatter(dot_nt(dg, wg) + dot_nt(du, wu))
    return output, da2, gg, gu, gd


def attn_back_kernel(wo_in, wq_in, wkv_in, mo_in, q_ref, o_ref, kv_ref, lse_ref, dh_ref, a1_ref, x_ref, r1_ref, gain2_ref, cos_ref, sin_ref, first_ref, da1_ref, go_ref, gq_ref, gkv_ref, mo_got, twin_o, twin_q, twin_kv, grad_o, grad_q, grad_kv, diag_o, diag_q, diag_kv, x_o, x_q, x_kv, y_o, y_q, y_kv, z_o, z_q, z_kv, stage_o, stage_q, stage_kv, wo, wq, wkv, a1t, do_ref, bias_ref, acc_ref, dqt_ref, dkv_own, dkv_out, dkv_got, load, mo_sem, dkv_send, dkv_recv, twin_send, twin_recv, send, recv, line_send, line_recv):
    me = Place()
    rows, width = dh_ref.shape
    keys, cols = kv_ref.shape[1], width // 8
    head_of = [xor4(me.t, 3 - j) for j in range(4)]

    def wo_load(j):
        return pltpu.make_async_copy(wo_in.at[:, head_of[j]], wo.at[j % 2], load.at[j % 2])

    def wq_load(j):
        return pltpu.make_async_copy(wq_in.at[head_of[j]], wq, load.at[2])

    wkv_load = pltpu.make_async_copy(wkv_in, wkv, load.at[3])
    mo_push = copy_to(mo_in.at[xor4(me.t, 3)], mo_got, mo_sem.at[0], mo_sem.at[1], me.line(xor4(me.t, 3)))
    wo_load(0).start()
    wo_load(1).start()
    wq_load(0).start()
    wkv_load.start()
    me.greet()
    mo_push.start()
    a1t[...] = a1_ref[...].T
    bias_ref[...] = bias_of(first_ref[...], me.t * rows, keys, rows)

    grads, twins, diags = [grad_o, grad_q, grad_kv], [twin_o, twin_q, twin_kv], [diag_o, diag_q, diag_kv]
    from_x, from_y, from_z = [x_o, x_q, x_kv], [y_o, y_q, y_kv], [z_o, z_q, z_kv]
    stages = [stage_o, stage_q, stage_kv]

    def twin_push(k, j):
        i = k * 4 + j
        return copy_to(grads[k].at[j, :, 1 - me.c], twins[k].at[j], twin_send.at[i], twin_recv.at[i], me.twin())

    def side(k, j, kind):
        i = k * 4 + j
        piece = lambda p: grads[k].at[j, p, me.c]
        if kind < 2:
            src, dst = half_of(piece(me.pd), kind), half_of(diags[k].at[j], kind)
        else:
            src, dst = (piece(me.px), from_x[k].at[j]) if kind == 2 else (piece(me.py), from_y[k].at[j])
        return copy_to(src, dst, send.at[i, kind], recv.at[i, kind], me.x_side() if kind % 2 == 0 else me.y_side())

    def line_push(k, j):
        return copy_to(grads[k].at[j, me.p, me.c], from_z[k].at[2 - j], line_send.at[k, j], line_recv.at[k, 2 - j], me.line(head_of[j]))

    def first(k, j):
        twin_push(k, j).wait_recv()
        copy = pltpu.make_async_copy(twins[k].at[j], stages[k], load.at[4])
        copy.start()
        copy.wait()
        for p in (me.pd, me.px, me.py, me.p):
            mine = grads[k].at[j, p, me.c]
            mine[...] = add_low(mine[...], stages[k][p])
            if p is me.pd:
                side(k, j, 0).start()
                side(k, j, 1).start()

    def second(k, j):
        for kind, p, to in ((1, me.px, 2), (0, me.py, 3)):
            side(k, j, kind).wait_recv()
            part, extra = half_of(grads[k].at[j, p, me.c], kind), half_of(diags[k].at[j], kind)
            part[...] = add_low(part[...], extra[...])
            side(k, j, to).start()

    def third(k, j):
        side(k, j, 2).wait_recv()
        side(k, j, 3).wait_recv()
        mine = grads[k].at[j, me.p, me.c]
        total = mine[...].astype(F32) + from_x[k][j].astype(F32) + from_y[k][j].astype(F32)
        if j < 3:
            mine[...] = total.astype(BF)
            line_push(k, j).start()
        else:
            (go_ref, gq_ref, gkv_ref)[k][...] = total

    def out_group(j):
        g = head_of[j]
        wo_load(j).wait()
        do = jnp.zeros((wo.shape[2], rows), F32)
        for d in range(8):
            part = slice(d * cols, (d + 1) * cols)
            do += dot_nt(wo[j % 2, d], dh_ref[:, part])
            grad_o[j, d // 2, d % 2] = dot_nn(o_ref[g], dh_ref[:, part]).astype(BF)
        twin_push(0, j).start()
        do_ref[j] = do.astype(BF)
        if j + 2 < 4:
            wo_load(j + 2).start()

    def dkv_push(j, m):
        z = xor4(me.t, m)
        there = 3 - ((3 - j) ^ m)
        src = dkv_out.at[j, pl.ds(pl.multiple_of(z * rows, rows), rows)]
        return copy_to(src, dkv_got.at[m - 1, there], dkv_send.at[m - 1, j], dkv_recv.at[m - 1, there], me.line(z))

    def back_group(j):
        g = head_of[j]
        kv = kv_ref[g]
        kt = kv.T[:HD]
        cos, sin = cos_ref[...], sin_ref[...]

        def head(h, _):
            part = pl.ds(pl.multiple_of(h * HD, HD), HD)
            q, do, o = q_ref[g, part], do_ref[j, part], o_ref[g, part]
            qz = jnp.concatenate([q, jnp.zeros_like(q)], 0)
            doz = jnp.concatenate([jnp.zeros_like(do), do], 0)
            delta = jnp.sum(do.astype(F32) * o.astype(F32), axis=0, keepdims=True)
            p = jnp.exp(dot_nn(kv, qz) + bias_ref[...] - lse_ref[g, pl.ds(h, 1)])
            ds = (p * (dot_nn(kv, doz) - delta)).astype(BF)
            acc_ref[...] += dot_nt(ds, qz) + dot_nt(p.astype(BF), doz)
            dqt_ref[part] = rope_back_t(dot_nn(kt, ds) * HD ** (-0.5), cos, sin).astype(BF)
            return 0

        acc_ref[...] = jnp.zeros_like(acc_ref)
        lax.fori_loop(0, RATIO, head, 0, unroll=2)
        dkv_out[j] = acc_ref[...].astype(BF)
        dkv_own[j] = acc_ref[pl.ds(pl.multiple_of(me.t * rows, rows), rows)]
        for m in (3, 2, 1):
            dkv_push(j, m).start()
        for d in range(8):
            grad_q[j, d // 2, d % 2] = dot_nt(a1t[d * cols : (d + 1) * cols], dqt_ref[...]).astype(BF)
        twin_push(1, j).start()
        wq_load(j).wait()
        part = dot_nt(dqt_ref[...].T, wq[...])
        if j == 0:
            da1_ref[...] = part
        else:
            da1_ref[...] += part
        if j < 3:
            wq_load(j + 1).start()

    def keys_back():
        wkv_load.wait()
        turned = []
        for j in range(4):
            total = dkv_own[j]
            for m in (3, 2, 1):
                dkv_push(3 - ((3 - j) ^ m), m).wait_recv()
                total += dkv_got[m - 1, j].astype(F32)
            total = total.T
            dkvt = jnp.concatenate([rope_back_t(total[:HD], cos_ref[...], sin_ref[...]), total[HD:]], 0)
            turned.append(dkvt.astype(BF))
            da1_ref[...] += dot_nt(dkvt.T.astype(BF), wkv[head_of[j]])
        gain1 = jnp.sum(da1_ref[...] * (x_ref[...].astype(F32) * r1_ref[...]), axis=0, keepdims=True)
        gain2 = gain2_ref[...]
        for j in range(4):
            for d in range(8):
                at = d * cols
                grad_kv[j, d // 2, d % 2, :cols] = dot_nt(a1t[at : at + cols], turned[j]).astype(BF)
                extra = [gain1[:, at : at + 128], gain1[:, at + 128 : at + 256], gain2[:, at : at + 128], gain2[:, at + 128 : at + 256], jnp.zeros((28, 128), F32)]
                grad_kv[j, d // 2, d % 2, cols:] = jnp.concatenate(extra, 0).astype(BF)
            twin_push(2, j).start()

    for j in range(4):
        out_group(j)
    for j in range(4):
        first(0, j)
    second(0, 0)
    second(0, 1)
    back_group(0)
    second(0, 2)
    second(0, 3)
    first(1, 0)
    back_group(1)
    third(0, 0)
    third(0, 1)
    second(1, 0)
    first(1, 1)
    back_group(2)
    third(0, 2)
    third(0, 3)
    second(1, 1)
    first(1, 2)
    third(1, 0)
    back_group(3)
    second(1, 2)
    first(1, 3)
    third(1, 1)
    keys_back()
    second(1, 3)
    third(1, 2)
    for j in range(4):
        first(2, j)
    third(1, 3)
    for j in range(4):
        second(2, j)
    for j in range(4):
        third(2, j)
    for k in range(3):
        for j in range(3):
            line_push(k, j).wait()
        total = (go_ref, gq_ref, gkv_ref)[k]
        total[...] += from_z[k][0].astype(F32) + from_z[k][1].astype(F32) + from_z[k][2].astype(F32)
    mo_push.wait()
    for j in range(4):
        for m in (1, 2, 3):
            dkv_push(j, m).wait_send()
        for k in range(3):
            twin_push(k, j).wait_send()
            for kind in range(4):
                side(k, j, kind).wait_send()


def attn_back(wo, wq, wkv, mo, q, o, kv, lse, dh, a1, x, r1, gain2, cos, sin, first):
    rows, width = dh.shape
    groups, heads, _ = q.shape
    keys, cols = kv.shape[1], width // 8
    dma, vmem = pltpu.SemaphoreType.DMA, lambda *shape: pltpu.VMEM(shape, BF)
    low = lambda *dims: jax.ShapeDtypeStruct(dims, BF)
    full = lambda *dims: jax.ShapeDtypeStruct(dims, F32)
    inside = pl.BlockSpec(memory_space=pltpu.VMEM)
    pieces = ((heads, cols), (cols, heads), (cols + 32, 2 * HD))
    return pl.pallas_call(
        attn_back_kernel,
        out_shape=[full(rows, width)] + [full(*p) for p in pieces] + [low(rows, width)] + [low(4, 4, *p) for p in pieces],
        in_specs=[ANY] * 4 + [inside] * 12,
        out_specs=[inside] * 4 + [ANY] * 4,
        scratch_shapes=[vmem(4, 4, 2, *p) for p in pieces]
        + [vmem(4, *p) for _ in range(3) for p in pieces]
        + [vmem(3, *p) for p in pieces]
        + [vmem(4, *p) for p in pieces]
        + [
            vmem(2, 8, heads, cols), vmem(width, heads), vmem(4, width, 2 * HD), vmem(width, rows), vmem(4, heads, rows),
            pltpu.VMEM((keys, rows), F32), pltpu.VMEM((keys, 2 * HD), F32), vmem(heads, rows),
            pltpu.VMEM((4, rows, 2 * HD), F32), vmem(4, keys, 2 * HD), vmem(3, 4, rows, 2 * HD),
            dma((5,)), dma((2,)), dma((3, 4)), dma((3, 4)), dma((12,)), dma((12,)), dma((12, 4)), dma((12, 4)), dma((3, 3)), dma((3, 3)),
        ],
        compiler_params=pltpu.CompilerParams(collective_id=3, has_side_effects=True, vmem_limit_bytes=63 * 2**20),
        name="attn_back",
    )(wo, wq, wkv, mo, q, o, kv, lse, dh, a1, x, r1, gain2, cos, sin, first)[:5]


def body(tokens, segments, attn_gain, w_query, w_key, w_value, w_out, mlp_gain, w_gate, w_up, w_down, cotangent):
    rows, width = tokens.shape
    hidden = w_gate.shape[1]
    nt = lax.axis_size("tensor")
    row0 = lax.axis_index("tensor") * rows
    keys = segments.shape[0]

    own_seg = lax.dynamic_slice_in_dim(segments, row0, rows)
    first = jnp.sum((segments[:, None] < own_seg[None, :]).astype(jnp.int32), axis=0)
    index = jnp.arange(rows, dtype=jnp.int32) + row0
    freq = jnp.exp(jnp.arange(HD // 2, dtype=F32) * (-2.0 * math.log(10000.0) / HD))
    angle = freq[:, None] * (index - first).astype(F32)[None, :]
    cos, sin = jnp.cos(angle), jnp.sin(angle)
    cos, sin = jnp.concatenate([cos, cos], 0), jnp.concatenate([sin, sin], 0)
    first = first[None, :]
    row0_s = row0[None].astype(jnp.int32)

    gain1 = lax.all_gather(attn_gain, "dp", axis=0, tiled=True).astype(F32)
    gain2 = lax.all_gather(mlp_gain, "dp", axis=0, tiled=True).astype(F32)
    w_kv = jnp.concatenate([w_key, w_value], 1)
    if lax.axis_size("dp") == 8 and nt == 4:
        wkv, wq, wo, wg, wu, wd = gather_weights(w_kv, w_query, w_out, w_gate, w_up, w_down)
        wkv, wq = wkv.reshape(4, width, -1), wq.reshape(4, width, -1)
        wo_raw = wo.reshape(8, 4, -1, width // 8)
        wo = wo.reshape(8, width, -1).transpose(1, 0, 2).reshape(width, width)
        wg, wu = wg.reshape(width, -1), wu.reshape(width, -1)
        wd8 = wd.reshape(8, hidden, -1)
    else:
        full = lambda w, axis: lax.all_gather(lax.all_gather(w, "dp", axis=axis, tiled=True), "tensor", axis=0)
        wq = full(w_query, 0)
        wkv = full(w_kv, 0)
        wo = full(w_out, 1).reshape(width, width)
        wg = lax.all_gather(w_gate, "dp", axis=0, tiled=True)
        wu = lax.all_gather(w_up, "dp", axis=0, tiled=True)
        wd = lax.all_gather(w_down, "dp", axis=1, tiled=True)

    x = tokens.astype(F32)
    n1, r1 = rms_forward(x, gain1)
    a1 = n1.astype(BF)
    kv = jnp.einsum("rd,gdc->grc", a1, wkv, preferred_element_type=F32)
    cos_r, sin_r = cos.T, sin.T
    k = kv[..., :HD]
    k = k * cos_r + jnp.concatenate([-k[..., HD // 2 :], k[..., : HD // 2]], -1) * sin_r
    kv = jnp.concatenate([k, kv[..., HD:]], -1).astype(BF)
    kv = lax.all_gather(kv, "tensor", axis=1, tiled=True)
    o, q, lse = attn_forward(row0_s, a1, wq, kv, cos, sin, first)
    o2 = o.reshape(-1, rows)
    h = x + dot_tn(o2, wo)

    n2, r2 = rms_forward(h, gain2)
    a2 = lax.all_gather(n2.astype(BF), "tensor", axis=0, tiled=True)
    cot = lax.all_gather(cotangent, "tensor", axis=0, tiled=True)
    if lax.axis_size("dp") == 8 and nt == 4:
        da2, mo, mo_near, gg, gu, gd = mlp(a2.reshape(4, rows, width), cot.reshape(4, rows, width), wg, wu, wd8)
        gg, gu, gd = gg.astype(F32), gu.astype(F32), gd.astype(F32)
    else:
        output, da2, gg, gu, gd = mlp_plain(h, a2, cot, wg, wu, wd)
    dres, gain2_part = rms_backward(h, r2, gain2, da2)
    dh = cotangent.astype(F32) + dres
    dhb = dh.astype(BF)

    if lax.axis_size("dp") == 8 and nt == 4:
        da1, go, gq, gkv, mo_far = attn_back(wo_raw, wq, wkv, mo, q, o, kv, lse, dhb, a1, tokens, r1, gain2_part[None, :], cos, sin, first)
        mo_own = lax.dynamic_index_in_dim(mo, lax.axis_index("tensor"), 0, keepdims=False)
        output = (h + mo_own.astype(F32) + mo_near[0].astype(F32) + mo_near[1].astype(F32) + mo_far.astype(F32)).astype(BF)
        din, _ = rms_backward(x, r1, gain1, da1)
        grad_tokens = dh + din
        cols = w_key.shape[0]
        gains = gkv[cols : cols + 4].reshape(2, -1)
        gkv = gkv[:cols]
        return (output, grad_tokens, gains[0], gq, gkv[:, :HD], gkv[:, HD:], go, gains[1], gg, gu, gd)

    do = dot_nt(wo, dhb).astype(BF).reshape(o.shape)
    go_part = dot_nn(o2, dhb)
    dq, dkv = attn_backward(row0_s, q, kv, do, o, lse, cos, sin, first)
    groups = dkv.shape[0]
    dkv = lax.psum_scatter(dkv.astype(BF), "tensor", scatter_dimension=1, tiled=True).astype(F32)
    dk = dkv[..., :HD]
    ws = dk * sin_r
    dk = dk * cos_r + jnp.concatenate([ws[..., HD // 2 :], -ws[..., : HD // 2]], -1)
    dkv = jnp.concatenate([dk, dkv[..., HD:]], -1).astype(BF)
    gq_part = jnp.einsum("rd,gcr->gdc", a1, dq, preferred_element_type=F32)
    gkv_part = jnp.einsum("rd,grc->gdc", a1, dkv, preferred_element_type=F32)
    da1 = jnp.einsum("gcr,gdc->rd", dq, wq, preferred_element_type=F32) + jnp.einsum("grc,gdc->rd", dkv, wkv, preferred_element_type=F32)
    din, gain1_part = rms_backward(x, r1, gain1, da1)
    grad_tokens = dh + din

    def home_all(v, dim):
        return lax.psum_scatter(home(v, dim + 1), "tensor", scatter_dimension=0, tiled=False).astype(F32)

    gq = home_all(gq_part, 0)
    gkv = home_all(gkv_part, 0)
    go = home_all(go_part.reshape(nt, -1, width), 1)
    gains = lax.psum_scatter(jnp.stack([gain1_part, gain2_part]), "dp", scatter_dimension=1, tiled=True)
    gains = lax.psum(gains, "tensor")
    return (output, grad_tokens, gains[0], gq, gkv[:, :HD], gkv[:, HD:], go, gains[1], gg, gu, gd)


def solution(mesh):
    rows, block = P(("dp", "tensor"), None), P("dp", "tensor")
    turned, line = P("tensor", "dp"), P("dp")
    return jax.shard_map(
        body,
        mesh=mesh,
        in_specs=(rows, line, line, block, block, block, turned, line, block, block, turned, rows),
        out_specs=(rows, rows, line, block, block, block, turned, line, block, block, turned),
        check_vma=False,
    )
```

```python
import functools
import math

import jax
import jax.numpy as jnp
from jax import lax
from jax.experimental import pallas as pl
from jax.experimental.pallas import tpu as pltpu
from jax.sharding import PartitionSpec as P

HD = 64
RATIO = 8
EPSILON = 1e-05
MASKED = -1e30
BF = jnp.bfloat16
F32 = jnp.float32


def dot_nn(left, right):
    return lax.dot_general(left, right, (((1,), (0,)), ((), ())), preferred_element_type=F32)


def dot_nt(left, right):
    return lax.dot_general(left, right, (((1,), (1,)), ((), ())), preferred_element_type=F32)


def dot_tn(left, right):
    return lax.dot_general(left, right, (((0,), (0,)), ((), ())), preferred_element_type=F32)


def rms_forward(values_in, gain_row):
    factor = lax.rsqrt(jnp.mean(values_in * values_in, axis=-1, keepdims=True) + EPSILON)
    return (values_in * factor * gain_row, factor)


def rms_backward(values_in, factor, gain_row, gradient):
    scaled = gain_row * gradient
    grad_gain = jnp.sum(gradient * values_in * factor, axis=0)
    grad_input = factor * scaled - values_in * (factor * factor * factor) * jnp.mean(
        scaled * values_in, axis=-1, keepdims=True
    )
    return (grad_input, grad_gain)


def rope_t(u, cos, sin):
    half = HD // 2
    return u * cos + jnp.concatenate([-u[half:], u[:half]], 0) * sin


def rope_back_t(w, cos, sin):
    half = HD // 2
    ws = w * sin
    return w * cos + jnp.concatenate([ws[half:], -ws[:half]], 0)


def bias_of(first, row0, keys, rows):
    key = lax.broadcasted_iota(jnp.int32, (keys, rows), 0)
    row = lax.broadcasted_iota(jnp.int32, (keys, rows), 1) + row0
    return jnp.where((key <= row) & (key >= first), 0.0, MASKED).astype(F32)


def attn_forward_kernel(row0_ref, a1_ref, wq_ref, kv_ref, cos_ref, sin_ref, first_ref, o_ref, q_ref, lse_ref, bias_ref, s_ref, vt_ref):
    keys, rows = bias_ref.shape

    @pl.when(pl.program_id(0) == 0)
    def _():
        bias_ref[...] = bias_of(first_ref[...], row0_ref[0], keys, rows)

    kv = kv_ref[0]
    kvt = kv.T
    vt_ref[...] = jnp.concatenate([kvt[HD:], jnp.ones((16, keys), BF)], 0)
    qt = dot_nn(a1_ref[...], wq_ref[0]).T
    cos, sin = cos_ref[...], sin_ref[...]
    for h in range(RATIO):
        q = (rope_t(qt[h * HD : (h + 1) * HD], cos, sin) * HD ** (-0.5)).astype(BF)
        q_ref[0, h * HD : (h + 1) * HD] = q
        s_ref[...] = dot_nn(kv, jnp.concatenate([q, jnp.zeros_like(q)], 0)) + bias_ref[...]
        peak = jnp.max(s_ref[...], axis=0, keepdims=True)
        e = jnp.exp(s_ref[...] - peak).astype(BF)
        ot = dot_nn(vt_ref[...], e)
        total = ot[HD : HD + 1]
        o_ref[0, h * HD : (h + 1) * HD] = (ot[:HD] / total).astype(BF)
        lse_ref[0, h : h + 1] = peak + jnp.log(total)


def attn_backward_kernel(row0_ref, q_ref, kv_ref, do_ref, o_ref, lse_ref, cos_ref, sin_ref, first_ref, dq_ref, dkv_ref, bias_ref, acc_ref):
    keys, rows = bias_ref.shape

    @pl.when(pl.program_id(0) == 0)
    def _():
        bias_ref[...] = bias_of(first_ref[...], row0_ref[0], keys, rows)

    kv = kv_ref[0]
    kt = kv.T[:HD]
    cos, sin = cos_ref[...], sin_ref[...]
    for h in range(RATIO):
        part = slice(h * HD, (h + 1) * HD)
        q, do, o = q_ref[0, part], do_ref[0, part], o_ref[0, part]
        qz = jnp.concatenate([q, jnp.zeros_like(q)], 0)
        doz = jnp.concatenate([jnp.zeros_like(do), do], 0)
        delta = jnp.sum(do.astype(F32) * o.astype(F32), axis=0, keepdims=True)
        p = jnp.exp(dot_nn(kv, qz) + bias_ref[...] - lse_ref[0, h : h + 1])
        ds = (p * (dot_nn(kv, doz) - delta)).astype(BF)
        grad = dot_nt(ds, qz) + dot_nt(p.astype(BF), doz)
        if h == 0:
            acc_ref[...] = grad
        else:
            acc_ref[...] += grad
        dq = dot_nn(kt, ds) * HD ** (-0.5)
        dq_ref[0, part] = rope_back_t(dq, cos, sin).astype(BF)
    dkv_ref[0] = acc_ref[...]


def params():
    return pltpu.CompilerParams(vmem_limit_bytes=56 * 2**20)


def attn_forward(row0, a1, wq, kv, cos, sin, first):
    groups, width, cols = wq.shape
    rows, keys = a1.shape[0], kv.shape[1]
    whole = lambda *shape: pl.BlockSpec(shape, lambda i: (0,) * len(shape))
    part = lambda *shape: pl.BlockSpec((1,) + shape, lambda i: (i,) + (0,) * len(shape))
    return pl.pallas_call(
        attn_forward_kernel,
        grid=(groups,),
        in_specs=[pl.BlockSpec(memory_space=pltpu.SMEM), whole(rows, width), part(width, cols), part(keys, 2 * HD), whole(HD, rows), whole(HD, rows), whole(1, rows)],
        out_specs=[part(cols, rows), part(cols, rows), part(RATIO, rows)],
        out_shape=[jax.ShapeDtypeStruct((groups, cols, rows), BF), jax.ShapeDtypeStruct((groups, cols, rows), BF), jax.ShapeDtypeStruct((groups, RATIO, rows), F32)],
        scratch_shapes=[pltpu.VMEM((keys, rows), F32), pltpu.VMEM((keys, rows), F32), pltpu.VMEM((HD + 16, keys), BF)],
        compiler_params=params(),
        name="attn_forward",
    )(row0, a1, wq, kv, cos, sin, first)


def attn_backward(row0, q, kv, do, o, lse, cos, sin, first):
    groups, cols, rows = q.shape
    keys = kv.shape[1]
    whole = lambda *shape: pl.BlockSpec(shape, lambda i: (0,) * len(shape))
    part = lambda *shape: pl.BlockSpec((1,) + shape, lambda i: (i,) + (0,) * len(shape))
    return pl.pallas_call(
        attn_backward_kernel,
        grid=(groups,),
        in_specs=[pl.BlockSpec(memory_space=pltpu.SMEM), part(cols, rows), part(keys, 2 * HD), part(cols, rows), part(cols, rows), part(RATIO, rows), whole(HD, rows), whole(HD, rows), whole(1, rows)],
        out_specs=[part(cols, rows), part(keys, 2 * HD)],
        out_shape=[jax.ShapeDtypeStruct((groups, cols, rows), BF), jax.ShapeDtypeStruct((groups, keys, 2 * HD), F32)],
        scratch_shapes=[pltpu.VMEM((keys, rows), F32), pltpu.VMEM((keys, 2 * HD), F32)],
        compiler_params=params(),
        name="attn_backward",
    )(row0, q, kv, do, o, lse, cos, sin, first)


MESH = pl.DeviceIdType.MESH
ANY = pl.BlockSpec(memory_space=pl.ANY)


class Place:
    def __init__(self):
        d, self.t = lax.axis_index("dp"), lax.axis_index("tensor")
        self.c, self.p = d % 2, d // 2
        x, y = self.p % 2, self.p // 2
        self.px, self.py, self.pd = self.p + 1 - 2 * x, self.p + 2 - 4 * y, 3 - self.p
        self.across = [self.t + 1 - 2 * (self.t % 2), (self.t + 2) % 4, 3 - self.t]
        self.order = [self.t] + self.across

    def at(self, p, c, t):
        return {"dp": p * 2 + c, "tensor": t}

    def x_side(self):
        return self.at(self.px, self.c, self.t)

    def y_side(self):
        return self.at(self.py, self.c, self.t)

    def twin(self):
        return self.at(self.p, 1 - self.c, self.t)

    def line(self, t):
        return self.at(self.p, self.c, t)

    def greet(self):
        barrier = pltpu.get_barrier_semaphore()
        others = [self.x_side(), self.y_side(), self.twin()] + [self.line(t) for t in self.across]
        for other in others:
            pl.semaphore_signal(barrier, inc=1, device_id=other, device_id_type=MESH)
        pl.semaphore_wait(barrier, len(others))


def half_of(ref, part):
    rows = ref.shape[0] // 2
    return ref.at[pl.ds(part * rows, rows)]


def attn_gather_kernel(kv_in, wq_in, wo_in, wg_in, wu_in, wd_in, ct_in, x_ref, cos_ref, sin_ref, first_ref, h_ref, a1_ref, r1_ref, r2_ref, gains_ref, q_ref, o_ref, lse_ref, kv_ref, kv_out, q_out, o_out, g_out, u_out, d_out, a2_all, ct_all, wkv, wq, wo, rows_kv, bias_ref, s_ref, vt_ref, qt_ref, o_rows, a2_ref, z_send, z_recv, send, recv, local, load, kv_send, kv_recv, line_send, line_recv):
    me = Place()
    rows, width = x_ref.shape
    keys, cols = kv_ref.shape[1], width // 8
    me.greet()
    sources = [kv_in, wq_in, wo_in, wg_in, wu_in, wd_in]
    outs = [kv_out, q_out, o_out, g_out, u_out, d_out]

    def piece(k, s, p, c):
        if k == 2:
            return o_out.at[p, c, s]
        return outs[k].at[s, p, c] if k < 2 else outs[k].at[p, c]

    def pair(k, s, c):
        if k == 2:
            return o_out.at[:, c, s]
        return outs[k].at[s, :, c] if k < 2 else outs[k].at[:, c]

    def line_push(k, j):
        return copy_to(sources[k], piece(k, me.t, me.p, me.c), z_send.at[k, j - 1], z_recv.at[k, j - 1], me.line(me.order[j]))

    def push(k, j, kind):
        s, i = me.order[j], k * 4 + j if k < 3 else k + 9
        if kind < 2:
            dst = piece(k, s, me.p, me.c)
            src = sources[k] if j == 0 else dst
        elif kind < 4:
            src = dst = half_of(piece(k, s, me.px if kind == 2 else me.py, me.c), kind - 2)
        else:
            src = dst = pair(k, s, me.c)
        to = [me.x_side, me.y_side, me.y_side, me.x_side, me.twin][kind]()
        return copy_to(src, dst, send.at[i, kind], recv.at[i, kind], to)

    def keep(k):
        return pltpu.make_async_copy(sources[k], piece(k, me.t, me.p, me.c), local.at[k])

    def first(k, j):
        if j == 0:
            keep(k).start()
        else:
            line_push(k, j).wait_recv()
        push(k, j, 0).start()
        push(k, j, 1).start()

    def second(k, j):
        push(k, j, 0).wait_recv()
        push(k, j, 2).start()
        push(k, j, 1).wait_recv()
        push(k, j, 3).start()

    def third(k, j):
        push(k, j, 2).wait_recv()
        push(k, j, 3).wait_recv()
        if j == 0:
            keep(k).wait()
        push(k, j, 4).start()

    def last(k, j):
        push(k, j, 4).wait_recv()

    def step(n, k, action):
        t, out, own = me.t, (ct_all, a2_all)[n], (ct_in, a2_ref)[n]
        for way, chunk, can in ((0, t - k + 1, (t < 3) & (t - k + 1 >= 0)), (1, t + k - 1, (t > 0) & (t + k - 1 <= 3))):

            @pl.when(can)
            def _():
                src = own if k == 1 else out.at[chunk]
                copy = copy_to(src, out.at[chunk], line_send.at[n, way, k - 1], line_recv.at[n, way, k - 1], me.line(t + 1 - 2 * way))
                copy.start() if action == "start" else copy.wait_send()

    def got(n, k):
        t, out = me.t, (ct_all, a2_all)[n]
        for way, chunk, can in ((0, t - k, t - k >= 0), (1, t + k, t + k <= 3)):

            @pl.when(can)
            def _():
                copy_to(out.at[chunk], out.at[chunk], line_send.at[n, way, k - 1], line_recv.at[n, way, k - 1], me.line(t + 1 - 2 * way)).wait_recv()

    def own_rows(n):
        return pltpu.make_async_copy((ct_in, a2_ref)[n], (ct_all, a2_all)[n].at[me.t], local.at[6 + n])

    kv_load = pltpu.make_async_copy(kv_out, wkv, load.at[0])
    kv_keep = pltpu.make_async_copy(rows_kv, kv_ref, load.at[1])

    def wq_load(j):
        return pltpu.make_async_copy(q_out.at[me.order[j]], wq.at[j % 2], load.at[2 + j % 2])

    def wo_load(j):
        s = me.order[j]
        return pltpu.make_async_copy(o_out.at[:, :, s], wo.at[:, :, pl.ds(pl.multiple_of(s * 2 * cols, cols), 2 * cols)], load.at[4 + j])

    own = pl.ds(pl.multiple_of(me.t * rows, rows), rows)

    def kv_push(j):
        part = rows_kv.at[:, own]
        return copy_to(part, part, kv_send.at[j - 1], kv_recv.at[j - 1], me.line(me.order[j]))

    def gain(n):
        parts = [wkv[0, d // 2, d % 2, cols + 2 * n + e : cols + 2 * n + e + 1] for d in range(8) for e in range(2)]
        return jnp.concatenate(parts, 1).astype(F32)

    def norm(value):
        return lax.rsqrt(jnp.mean(value * value, axis=-1, keepdims=True) + EPSILON)

    def project_keys():
        x = x_ref[...].astype(F32)
        r1_ref[...] = norm(x)
        gains_ref[0:1] = gain(0)
        gains_ref[1:2] = gain(1)
        a1_ref[...] = (x * r1_ref[...] * gains_ref[0:1]).astype(BF)
        for s in range(4):
            weights = wkv[s, :, :, :cols].reshape(width, 2 * HD)
            kvt = dot_nn(a1_ref[...], weights).T
            kvt = jnp.concatenate([rope_t(kvt[:HD], cos_ref[...], sin_ref[...]), kvt[HD:]], 0).astype(BF)
            rows_kv[s, own] = kvt.T

    def attend(j):
        g = me.order[j]
        qt_ref[...] = dot_nn(a1_ref[...], wq[j % 2].reshape(width, -1)).T
        kv = rows_kv[g]
        vt_ref[...] = jnp.concatenate([kv.T[HD:], jnp.ones((16, keys), BF)], 0)
        cos, sin = cos_ref[...], sin_ref[...]

        def head(h, _):
            part = pl.ds(pl.multiple_of(h * HD, HD), HD)
            q = (rope_t(qt_ref[part], cos, sin) * HD ** (-0.5)).astype(BF)
            q_ref[g, part] = q
            s_ref[...] = dot_nn(kv, jnp.concatenate([q, jnp.zeros_like(q)], 0)) + bias_ref[...]
            peak = jnp.max(s_ref[...], axis=0, keepdims=True)
            e = jnp.exp(s_ref[...] - peak).astype(BF)
            ot = dot_nn(vt_ref[...], e)
            total = ot[HD : HD + 1]
            o_ref[g, part] = (ot[:HD] / total).astype(BF)
            lse_ref[g, pl.ds(h, 1)] = peak + jnp.log(total)
            return 0

        lax.fori_loop(0, RATIO, head, 0, unroll=2)
        o_rows[:, pl.ds(pl.multiple_of(g * 2 * cols, cols), 2 * cols)] = o_ref[g].T

    def mix():
        for d in range(8):
            part = slice(d * cols, (d + 1) * cols)
            h_ref[:, part] = x_ref[:, part].astype(F32) + dot_nn(o_rows[...], wo[d // 2, d % 2])
        h = h_ref[...]
        r2_ref[...] = norm(h)
        a2_ref[...] = (h * r2_ref[...] * gains_ref[1:2]).astype(BF)

    KV, Q, O, G, U, D = range(6)
    for k in (KV, Q, O):
        for j in (1, 2, 3):
            line_push(k, j).start()
    own_rows(0).start()
    first(KV, 0)
    first(Q, 0)
    bias_ref[...] = bias_of(first_ref[...], me.t * rows, keys, rows)
    for j in (1, 2, 3):
        first(KV, j)
    for j in range(4):
        second(KV, j)
    first(Q, 1)
    for j in range(4):
        third(KV, j)
    second(Q, 0)
    for j in range(4):
        last(KV, j)
    kv_load.start()
    kv_load.wait()
    project_keys()
    for j in (1, 2, 3):
        kv_push(j).start()
    step(0, 1, "start")
    first(Q, 2)
    second(Q, 1)
    third(Q, 0)
    first(Q, 3)
    second(Q, 2)
    third(Q, 1)
    last(Q, 0)
    wq_load(0).start()
    first(O, 0)
    for j in (1, 2, 3):
        kv_push(j).wait_recv()
    kv_keep.start()
    wq_load(0).wait()
    attend(0)
    second(Q, 3)
    third(Q, 2)
    first(O, 1)
    last(Q, 1)
    wq_load(1).start()
    second(O, 0)
    got(0, 1)
    step(0, 2, "start")
    wq_load(1).wait()
    attend(1)
    third(Q, 3)
    first(O, 2)
    last(Q, 2)
    wq_load(2).start()
    second(O, 1)
    third(O, 0)
    wq_load(2).wait()
    attend(2)
    first(O, 3)
    last(Q, 3)
    wq_load(3).start()
    second(O, 2)
    third(O, 1)
    got(0, 2)
    step(0, 3, "start")
    wq_load(3).wait()
    attend(3)
    first(G, 0)
    second(O, 3)
    third(O, 2)
    last(O, 0)
    wo_load(0).start()
    last(O, 1)
    wo_load(1).start()
    third(O, 3)
    first(U, 0)
    last(O, 2)
    wo_load(2).start()
    last(O, 3)
    wo_load(3).start()
    for j in range(4):
        wo_load(j).wait()
    mix()
    own_rows(1).start()
    step(1, 1, "start")
    second(G, 0)
    first(D, 0)
    third(G, 0)
    second(U, 0)
    got(1, 1)
    step(1, 2, "start")
    third(U, 0)
    second(D, 0)
    got(1, 2)
    step(1, 3, "start")
    third(D, 0)
    for k in (G, U, D):
        last(k, 0)
    got(0, 3)
    got(1, 3)
    kv_keep.wait()
    for n in range(2):
        own_rows(n).wait()
        for k in (1, 2, 3):
            step(n, k, "wait")
    for j in (1, 2, 3):
        kv_push(j).wait_send()
        for k in (KV, Q, O):
            line_push(k, j).wait_send()
    for k in range(6):
        for j in range(4 if k < 3 else 1):
            for kind in range(5):
                push(k, j, kind).wait_send()


def attn_gather(kv, wq, wo, wg, wu, wd, ct, x, cos, sin, first):
    rows, width = x.shape
    heads, cols, keys = wq.shape[1], wq.shape[0], 4 * rows
    dma, vmem = pltpu.SemaphoreType.DMA, lambda *shape: pltpu.VMEM(shape, BF)
    low = lambda *dims: jax.ShapeDtypeStruct(dims, BF)
    full = lambda *dims: jax.ShapeDtypeStruct(dims, F32)
    inside = pl.BlockSpec(memory_space=pltpu.VMEM)
    return pl.pallas_call(
        attn_gather_kernel,
        out_shape=[
            full(rows, width), low(rows, width), full(rows, 1), full(rows, 1), full(2, width), low(4, heads, rows), low(4, heads, rows), full(4, RATIO, rows),
            low(4, keys, 2 * HD), low(4, 4, 2, *kv.shape), low(4, 4, 2, *wq.shape), low(4, 2, 4, *wo.shape),
            low(4, 2, *wg.shape), low(4, 2, *wu.shape), low(4, 2, *wd.shape), low(4, rows, width), low(4, rows, width),
        ],
        in_specs=[ANY] * 7 + [inside] * 4,
        out_specs=[inside] * 8 + [ANY] * 9,
        scratch_shapes=[
            vmem(4, 4, 2, *kv.shape), vmem(2, 4, 2, cols, heads), vmem(4, 2, width, cols), vmem(4, keys, 2 * HD),
            pltpu.VMEM((keys, rows), F32), pltpu.VMEM((keys, rows), F32), vmem(HD + 16, keys), pltpu.VMEM((heads, rows), F32), vmem(rows, width), vmem(rows, width),
            dma((3, 3)), dma((3, 3)), dma((15, 5)), dma((15, 5)), dma((8,)), dma((8,)), dma((3,)), dma((3,)), dma((2, 2, 3)), dma((2, 2, 3)),
        ],
        compiler_params=pltpu.CompilerParams(collective_id=1, has_side_effects=True, vmem_limit_bytes=56 * 2**20),
        name="attn_gather",
    )(kv, wq, wo, wg, wu, wd, ct, x, cos, sin, first)


def xor4(a, m):
    return (a // 2 + m // 2) % 2 * 2 + (a % 2 + m % 2) % 2


def copy_to(src, dst, send_sem, recv_sem, to):
    return pltpu.make_async_remote_copy(src, dst, send_sem, recv_sem, device_id=to, device_id_type=MESH)


def add_low(left, right):
    return (left.astype(F32) + right.astype(F32)).astype(BF)


def mlp_kernel(a2_in, ct_in, wg_in, wu_in, wd_in, da2_out, mo_out, mo_got, gg_out, gu_out, gd_out, twin_g, twin_u, twin_d, wg, wu, wd, a2_buf, ct_buf, mo_buf, a2_col, ct_col, zt, dg, du, out_buf, in_buf, diag_gu, x_gu, y_gu, diag_d, x_d, y_d, stage_gu, stage_d, load, store, line_send, line_recv, mo_send, mo_recv, twin_send, twin_recv, send, recv, stage_sem):
    me = Place()
    rows, width = da2_out.shape
    hidden = wg.shape[1]
    cols = width // 8
    weights = [pltpu.make_async_copy(wg_in, wg, load.at[4]), pltpu.make_async_copy(wu_in, wu, load.at[5])]
    weights += [pltpu.make_async_copy(wd_in.at[d], wd.at[:, pl.ds(d * cols, cols)], load.at[6 + d]) for d in range(8)]
    for copy in weights:
        copy.start()

    def chunk_load(j, slot):
        s = xor4(me.t, 3 - j)
        return pltpu.make_async_copy(a2_in.at[s], a2_buf.at[slot], load.at[slot]), pltpu.make_async_copy(ct_in.at[s], ct_buf.at[slot], load.at[2 + slot])

    def chunk_send(j):
        return copy_to(out_buf.at[j], in_buf.at[2 - j], line_send.at[j], line_recv.at[2 - j], me.line(xor4(me.t, 3 - j)))

    def mo_store(j, slot):
        return pltpu.make_async_copy(mo_buf.at[slot], mo_out.at[xor4(me.t, 3 - j)], store.at[slot])

    for copy in chunk_load(0, 0):
        copy.start()
    me.greet()
    for copy in weights:
        copy.wait()

    def chunk(j, _):
        slot = j % 2

        @pl.when(j < 3)
        def _():
            for copy in chunk_load(j + 1, 1 - slot):
                copy.start()

        for copy in chunk_load(j, slot):
            copy.wait()
        where = pl.multiple_of(xor4(me.t, 3 - j) * rows, rows)
        g, u = dot_nn(a2_buf[slot], wg[...]), dot_nn(a2_buf[slot], wu[...])
        dz = dot_nt(ct_buf[slot], wd[...])
        sig = 1.0 / (1.0 + jnp.exp(-g))
        act = g * sig
        z = (act * u).astype(BF)
        zt[:, pl.ds(where, rows)] = z.T
        dg_now = (dz * u * (sig * (1.0 + g * (1.0 - sig)))).astype(BF)
        du_now = (dz * act).astype(BF)
        dg[pl.ds(where, rows)] = dg_now
        du[pl.ds(where, rows)] = du_now
        part = dot_nt(dg_now, wg[...]) + dot_nt(du_now, wu[...])

        @pl.when(j < 3)
        def _():
            out_buf[j] = part.astype(BF)
            chunk_send(j).start()

        @pl.when(j == 3)
        def _():
            da2_out[...] = part

        @pl.when(j >= 2)
        def _():
            mo_store(j - 2, slot).wait()

        mo_buf[slot] = dot_nn(z, wd[...]).astype(BF)
        mo_store(j, slot).start()
        return 0

    lax.fori_loop(0, 4, chunk, 0)
    mo_store(2, 0).wait()
    mo_store(3, 1).wait()

    def mo_push(m):
        return copy_to(mo_out.at[xor4(me.t, m)], mo_got.at[m - 1], mo_send.at[m - 1], mo_recv.at[m - 1], me.line(xor4(me.t, m)))

    for m in (1, 2):
        mo_push(m).start()

    def owner(i):
        return xor4(me.p, 3 - i % 4) * 2 + (1 - me.c + i // 4) % 2

    def tile_load(i, slot):
        at = pl.ds(pl.multiple_of(owner(i) * cols, cols), cols)
        return pltpu.make_async_copy(a2_in.at[:, :, at], a2_col.at[slot], load.at[slot]), pltpu.make_async_copy(ct_in.at[:, :, at], ct_col.at[slot], load.at[2 + slot])

    def piece(k, p, c):
        at = pl.ds(pl.multiple_of((p * 2 + c) * cols, cols), cols)
        return (wg, wu)[k].at[at] if k < 2 else wd.at[:, at]

    twins = [twin_g, twin_u, twin_d]

    def twin_push(k, i):
        p = xor4(me.p, 3 - i)
        return copy_to(piece(k, p, 1 - me.c), twins[k].at[p], twin_send.at[k, i], twin_recv.at[k, i], me.twin())

    for copy in tile_load(0, 0):
        copy.start()

    def tile(i, _):
        slot = i % 2

        @pl.when(i < 7)
        def _():
            for copy in tile_load(i + 1, 1 - slot):
                copy.start()

        for copy in tile_load(i, slot):
            copy.wait()
        at = pl.ds(pl.multiple_of(owner(i) * cols, cols), cols)
        a2t = a2_col[slot].reshape(4 * rows, cols).T
        wg[at] = dot_nn(a2t, dg[...]).astype(BF)
        wu[at] = dot_nn(a2t, du[...]).astype(BF)
        wd[:, at] = dot_nn(zt[...], ct_col[slot].reshape(4 * rows, cols)).astype(BF)

        @pl.when(i < 4)
        def _():
            for k in range(3):
                twin_push(k, i).start()

        return 0

    lax.fori_loop(0, 8, tile, 0)

    diag = [diag_gu.at[0], diag_gu.at[1], diag_d]
    from_x = [x_gu.at[0], x_gu.at[1], x_d]
    from_y = [y_gu.at[0], y_gu.at[1], y_d]
    stage = [stage_gu.at[0], stage_gu.at[1], stage_d]

    def side(k, kind):
        if kind < 2:
            src, dst = half_of(piece(k, me.pd, me.c), kind), half_of(diag[k], kind)
        else:
            src, dst = (piece(k, me.px, me.c), from_x[k]) if kind == 2 else (piece(k, me.py, me.c), from_y[k])
        return copy_to(src, dst, send.at[k, kind], recv.at[k, kind], me.x_side() if kind % 2 == 0 else me.y_side())

    steps = [(k, i) for i in range(4) for k in range(3)]

    def fetch(n):
        k, i = steps[n]
        twin_push(k, i).wait_recv()
        copy = pltpu.make_async_copy(twins[k].at[xor4(me.p, 3 - i)], stage[k], stage_sem.at[k])
        copy.start()
        return copy

    def add_twin(n, copy):
        k, i = steps[n]
        copy.wait()
        mine = piece(k, xor4(me.p, 3 - i), me.c)
        mine[...] = add_low(mine[...], stage[k][...])
        if i == 0:
            side(k, 0).start()
            side(k, 1).start()

    ahead = fetch(0)
    for n in range(12):
        now = ahead
        if n + 1 < 12:
            ahead = fetch(n + 1)
        add_twin(n, now)
    for k in range(3):
        side(k, 1).wait_recv()
        part, extra = half_of(piece(k, me.px, me.c), 1), half_of(diag[k], 1)
        part[...] = add_low(part[...], extra[...])
        side(k, 2).start()
        side(k, 0).wait_recv()
        part, extra = half_of(piece(k, me.py, me.c), 0), half_of(diag[k], 0)
        part[...] = add_low(part[...], extra[...])
        side(k, 3).start()
    results = []
    for k in range(3):
        side(k, 2).wait_recv()
        side(k, 3).wait_recv()
        mine = piece(k, me.p, me.c)
        mine[...] = (mine[...].astype(F32) + from_x[k][...].astype(F32) + from_y[k][...].astype(F32)).astype(BF)
        results.append(pltpu.make_async_copy(mine, (gg_out, gu_out, gd_out)[k], stage_sem.at[k]))
        results[-1].start()
    for j in range(3):
        chunk_send(j).wait_recv()
    da2_out[...] += in_buf[0].astype(F32) + in_buf[1].astype(F32) + in_buf[2].astype(F32)
    for copy in results:
        copy.wait()
    for m in (1, 2):
        mo_push(m).wait()
    for j in range(3):
        chunk_send(j).wait_send()
    for k in range(3):
        for i in range(4):
            twin_push(k, i).wait_send()
            side(k, i).wait_send()


def mlp(a2, ct, wg, wu, wd):
    chunks, rows, width = a2.shape
    hidden, cols = wg.shape[1], width // 8
    dma, vmem = pltpu.SemaphoreType.DMA, lambda *shape: pltpu.VMEM(shape, BF)
    shape = lambda *dims: jax.ShapeDtypeStruct(dims, BF)
    return pl.pallas_call(
        mlp_kernel,
        out_shape=[jax.ShapeDtypeStruct((rows, width), F32), shape(4, rows, width), shape(2, rows, width), shape(cols, hidden), shape(cols, hidden), shape(hidden, cols), shape(4, cols, hidden), shape(4, cols, hidden), shape(4, hidden, cols)],
        in_specs=[ANY] * 5,
        out_specs=[pl.BlockSpec(memory_space=pltpu.VMEM)] + [ANY] * 8,
        scratch_shapes=[
            vmem(width, hidden), vmem(width, hidden), vmem(hidden, width),
            vmem(2, rows, width), vmem(2, rows, width), vmem(2, rows, width),
            vmem(2, 4, rows, cols), vmem(2, 4, rows, cols),
            vmem(hidden, 4 * rows), vmem(4 * rows, hidden), vmem(4 * rows, hidden),
            vmem(3, rows, width), vmem(3, rows, width),
            vmem(2, cols, hidden), vmem(2, cols, hidden), vmem(2, cols, hidden),
            vmem(hidden, cols), vmem(hidden, cols), vmem(hidden, cols),
            vmem(2, cols, hidden), vmem(hidden, cols),
            dma((14,)), dma((2,)), dma((3,)), dma((3,)), dma((2,)), dma((2,)), dma((3, 4)), dma((3, 4)), dma((3, 4)), dma((3, 4)), dma((3,)),
        ],
        compiler_params=pltpu.CompilerParams(collective_id=2, has_side_effects=True, vmem_limit_bytes=62 * 2**20),
        name="mlp",
    )(a2, ct, wg, wu, wd)[:6]


def home(v, dim):
    return lax.psum_scatter(v.astype(BF), "dp", scatter_dimension=dim, tiled=True)


def mlp_plain(h, a2, cot, wg, wu, wd):
    g, u = dot_nn(a2, wg), dot_nn(a2, wu)
    sig = jax.nn.sigmoid(g)
    act = g * sig
    z = (act * u).astype(BF)
    scatter = lambda v: lax.psum_scatter(v.astype(BF), "tensor", scatter_dimension=0, tiled=True).astype(F32)
    output = (h + scatter(dot_nn(z, wd))).astype(BF)
    dz = dot_nt(cot, wd)
    dg = (dz * u * (sig * (1.0 + g * (1.0 - sig)))).astype(BF)
    du = (dz * act).astype(BF)
    gd = home(dot_tn(z, cot), 1).astype(F32)
    gg = home(dot_tn(a2, dg), 0).astype(F32)
    gu = home(dot_tn(a2, du), 0).astype(F32)
    da2 = scatter(dot_nt(dg, wg) + dot_nt(du, wu))
    return output, da2, gg, gu, gd


def attn_back_kernel(wo_in, wq_in, wkv_in, mo_in, q_ref, o_ref, kv_ref, lse_ref, dh_ref, a1_ref, x_ref, r1_ref, gain2_ref, cos_ref, sin_ref, first_ref, da1_ref, go_ref, gq_ref, gkv_ref, mo_got, twin_o, twin_q, twin_kv, grad_o, grad_q, grad_kv, diag_o, diag_q, diag_kv, x_o, x_q, x_kv, y_o, y_q, y_kv, z_o, z_q, z_kv, stage_o, stage_q, stage_kv, wo, wq, wkv, a1t, do_ref, bias_ref, acc_ref, dqt_ref, dkv_own, dkv_out, dkv_got, load, mo_sem, dkv_send, dkv_recv, twin_send, twin_recv, send, recv, line_send, line_recv):
    me = Place()
    rows, width = dh_ref.shape
    keys, cols = kv_ref.shape[1], width // 8
    head_of = [xor4(me.t, 3 - j) for j in range(4)]

    def wo_load(j):
        return pltpu.make_async_copy(wo_in.at[:, head_of[j]], wo.at[j % 2], load.at[j % 2])

    def wq_load(j):
        return pltpu.make_async_copy(wq_in.at[head_of[j]], wq, load.at[2])

    wkv_load = pltpu.make_async_copy(wkv_in, wkv, load.at[3])
    mo_push = copy_to(mo_in.at[xor4(me.t, 3)], mo_got, mo_sem.at[0], mo_sem.at[1], me.line(xor4(me.t, 3)))
    wo_load(0).start()
    wo_load(1).start()
    wq_load(0).start()
    wkv_load.start()
    me.greet()
    mo_push.start()
    a1t[...] = a1_ref[...].T
    bias_ref[...] = bias_of(first_ref[...], me.t * rows, keys, rows)

    grads, twins, diags = [grad_o, grad_q, grad_kv], [twin_o, twin_q, twin_kv], [diag_o, diag_q, diag_kv]
    from_x, from_y, from_z = [x_o, x_q, x_kv], [y_o, y_q, y_kv], [z_o, z_q, z_kv]
    stages = [stage_o, stage_q, stage_kv]

    def twin_push(k, j):
        i = k * 4 + j
        return copy_to(grads[k].at[j, :, 1 - me.c], twins[k].at[j], twin_send.at[i], twin_recv.at[i], me.twin())

    def side(k, j, kind):
        i = k * 4 + j
        piece = lambda p: grads[k].at[j, p, me.c]
        if kind < 2:
            src, dst = half_of(piece(me.pd), kind), half_of(diags[k].at[j], kind)
        else:
            src, dst = (piece(me.px), from_x[k].at[j]) if kind == 2 else (piece(me.py), from_y[k].at[j])
        return copy_to(src, dst, send.at[i, kind], recv.at[i, kind], me.x_side() if kind % 2 == 0 else me.y_side())

    def line_push(k, j):
        return copy_to(grads[k].at[j, me.p, me.c], from_z[k].at[2 - j], line_send.at[k, j], line_recv.at[k, 2 - j], me.line(head_of[j]))

    def first(k, j):
        twin_push(k, j).wait_recv()
        copy = pltpu.make_async_copy(twins[k].at[j], stages[k], load.at[4])
        copy.start()
        copy.wait()
        for p in (me.pd, me.px, me.py, me.p):
            mine = grads[k].at[j, p, me.c]
            mine[...] = add_low(mine[...], stages[k][p])
            if p is me.pd:
                side(k, j, 0).start()
                side(k, j, 1).start()

    def second(k, j):
        for kind, p, to in ((1, me.px, 2), (0, me.py, 3)):
            side(k, j, kind).wait_recv()
            part, extra = half_of(grads[k].at[j, p, me.c], kind), half_of(diags[k].at[j], kind)
            part[...] = add_low(part[...], extra[...])
            side(k, j, to).start()

    def third(k, j):
        side(k, j, 2).wait_recv()
        side(k, j, 3).wait_recv()
        mine = grads[k].at[j, me.p, me.c]
        total = mine[...].astype(F32) + from_x[k][j].astype(F32) + from_y[k][j].astype(F32)
        if j < 3:
            mine[...] = total.astype(BF)
            line_push(k, j).start()
        else:
            (go_ref, gq_ref, gkv_ref)[k][...] = total

    def out_group(j):
        g = head_of[j]
        wo_load(j).wait()
        do = jnp.zeros((wo.shape[2], rows), F32)
        for d in range(8):
            part = slice(d * cols, (d + 1) * cols)
            do += dot_nt(wo[j % 2, d], dh_ref[:, part])
            grad_o[j, d // 2, d % 2] = dot_nn(o_ref[g], dh_ref[:, part]).astype(BF)
        twin_push(0, j).start()
        do_ref[j] = do.astype(BF)
        if j + 2 < 4:
            wo_load(j + 2).start()

    def dkv_push(j, m):
        z = xor4(me.t, m)
        there = 3 - ((3 - j) ^ m)
        src = dkv_out.at[j, pl.ds(pl.multiple_of(z * rows, rows), rows)]
        return copy_to(src, dkv_got.at[m - 1, there], dkv_send.at[m - 1, j], dkv_recv.at[m - 1, there], me.line(z))

    def back_group(j):
        g = head_of[j]
        kv = kv_ref[g]
        kt = kv.T[:HD]
        cos, sin = cos_ref[...], sin_ref[...]

        def head(h, _):
            part = pl.ds(pl.multiple_of(h * HD, HD), HD)
            q, do, o = q_ref[g, part], do_ref[j, part], o_ref[g, part]
            qz = jnp.concatenate([q, jnp.zeros_like(q)], 0)
            doz = jnp.concatenate([jnp.zeros_like(do), do], 0)
            delta = jnp.sum(do.astype(F32) * o.astype(F32), axis=0, keepdims=True)
            p = jnp.exp(dot_nn(kv, qz) + bias_ref[...] - lse_ref[g, pl.ds(h, 1)])
            ds = (p * (dot_nn(kv, doz) - delta)).astype(BF)
            acc_ref[...] += dot_nt(ds, qz) + dot_nt(p.astype(BF), doz)
            dqt_ref[part] = rope_back_t(dot_nn(kt, ds) * HD ** (-0.5), cos, sin).astype(BF)
            return 0

        acc_ref[...] = jnp.zeros_like(acc_ref)
        lax.fori_loop(0, RATIO, head, 0, unroll=2)
        dkv_out[j] = acc_ref[...].astype(BF)
        dkv_own[j] = acc_ref[pl.ds(pl.multiple_of(me.t * rows, rows), rows)]
        for m in (3, 2, 1):
            dkv_push(j, m).start()
        for d in range(8):
            grad_q[j, d // 2, d % 2] = dot_nt(a1t[d * cols : (d + 1) * cols], dqt_ref[...]).astype(BF)
        twin_push(1, j).start()
        wq_load(j).wait()
        part = dot_nt(dqt_ref[...].T, wq[...])
        if j == 0:
            da1_ref[...] = part
        else:
            da1_ref[...] += part
        if j < 3:
            wq_load(j + 1).start()

    def keys_back():
        wkv_load.wait()
        turned = []
        for j in range(4):
            total = dkv_own[j]
            for m in (3, 2, 1):
                dkv_push(3 - ((3 - j) ^ m), m).wait_recv()
                total += dkv_got[m - 1, j].astype(F32)
            total = total.T
            dkvt = jnp.concatenate([rope_back_t(total[:HD], cos_ref[...], sin_ref[...]), total[HD:]], 0)
            turned.append(dkvt.astype(BF))
            da1_ref[...] += dot_nt(dkvt.T.astype(BF), wkv[head_of[j], :, :cols].reshape(width, 2 * HD))
        gain1 = jnp.sum(da1_ref[...] * (x_ref[...].astype(F32) * r1_ref[...]), axis=0, keepdims=True)
        gain2 = gain2_ref[...]
        for j in range(4):
            for d in range(8):
                at = d * cols
                grad_kv[j, d // 2, d % 2, :cols] = dot_nt(a1t[at : at + cols], turned[j]).astype(BF)
                extra = [gain1[:, at : at + 128], gain1[:, at + 128 : at + 256], gain2[:, at : at + 128], gain2[:, at + 128 : at + 256], jnp.zeros((28, 128), F32)]
                grad_kv[j, d // 2, d % 2, cols:] = jnp.concatenate(extra, 0).astype(BF)
            twin_push(2, j).start()

    for j in range(4):
        out_group(j)
    for j in range(4):
        first(0, j)
    second(0, 0)
    second(0, 1)
    back_group(0)
    second(0, 2)
    second(0, 3)
    first(1, 0)
    back_group(1)
    third(0, 0)
    third(0, 1)
    second(1, 0)
    first(1, 1)
    back_group(2)
    third(0, 2)
    third(0, 3)
    second(1, 1)
    first(1, 2)
    third(1, 0)
    back_group(3)
    second(1, 2)
    first(1, 3)
    third(1, 1)
    keys_back()
    second(1, 3)
    third(1, 2)
    for j in range(4):
        first(2, j)
    third(1, 3)
    for j in range(4):
        second(2, j)
    for j in range(4):
        third(2, j)
    for k in range(3):
        for j in range(3):
            line_push(k, j).wait()
        total = (go_ref, gq_ref, gkv_ref)[k]
        total[...] += from_z[k][0].astype(F32) + from_z[k][1].astype(F32) + from_z[k][2].astype(F32)
    mo_push.wait()
    for j in range(4):
        for m in (1, 2, 3):
            dkv_push(j, m).wait_send()
        for k in range(3):
            twin_push(k, j).wait_send()
            for kind in range(4):
                side(k, j, kind).wait_send()


def attn_back(wo, wq, wkv, mo, q, o, kv, lse, dh, a1, x, r1, gain2, cos, sin, first):
    rows, width = dh.shape
    groups, heads, _ = q.shape
    keys, cols = kv.shape[1], width // 8
    dma, vmem = pltpu.SemaphoreType.DMA, lambda *shape: pltpu.VMEM(shape, BF)
    low = lambda *dims: jax.ShapeDtypeStruct(dims, BF)
    full = lambda *dims: jax.ShapeDtypeStruct(dims, F32)
    inside = pl.BlockSpec(memory_space=pltpu.VMEM)
    pieces = ((heads, cols), (cols, heads), (cols + 32, 2 * HD))
    return pl.pallas_call(
        attn_back_kernel,
        out_shape=[full(rows, width)] + [full(*p) for p in pieces] + [low(rows, width)] + [low(4, 4, *p) for p in pieces],
        in_specs=[ANY] * 4 + [inside] * 12,
        out_specs=[inside] * 4 + [ANY] * 4,
        scratch_shapes=[vmem(4, 4, 2, *p) for p in pieces]
        + [vmem(4, *p) for _ in range(3) for p in pieces]
        + [vmem(3, *p) for p in pieces]
        + [vmem(4, *p) for p in pieces]
        + [
            vmem(2, 8, heads, cols), vmem(width, heads), vmem(4, 8, cols + 32, 2 * HD), vmem(width, rows), vmem(4, heads, rows),
            pltpu.VMEM((keys, rows), F32), pltpu.VMEM((keys, 2 * HD), F32), vmem(heads, rows),
            pltpu.VMEM((4, rows, 2 * HD), F32), vmem(4, keys, 2 * HD), vmem(3, 4, rows, 2 * HD),
            dma((5,)), dma((2,)), dma((3, 4)), dma((3, 4)), dma((12,)), dma((12,)), dma((12, 4)), dma((12, 4)), dma((3, 3)), dma((3, 3)),
        ],
        compiler_params=pltpu.CompilerParams(collective_id=3, has_side_effects=True, vmem_limit_bytes=63 * 2**20),
        name="attn_back",
    )(wo, wq, wkv, mo, q, o, kv, lse, dh, a1, x, r1, gain2, cos, sin, first)[:5]


def rope_tables(segments, rows, row0):
    own = lax.dynamic_slice_in_dim(segments, row0, rows)
    first = jnp.sum((segments[:, None] < own[None, :]).astype(jnp.int32), axis=0)
    index = jnp.arange(rows, dtype=jnp.int32) + row0
    freq = jnp.exp(jnp.arange(HD // 2, dtype=F32) * (-2.0 * math.log(10000.0) / HD))
    angle = freq[:, None] * (index - first).astype(F32)[None, :]
    cos, sin = jnp.cos(angle), jnp.sin(angle)
    return jnp.concatenate([cos, cos], 0), jnp.concatenate([sin, sin], 0), first[None, :]


def body(tokens, segments, attn_gain, w_query, w_key, w_value, w_out, mlp_gain, w_gate, w_up, w_down, cotangent):
    rows, width = tokens.shape
    cols, hidden = w_gate.shape
    t = lax.axis_index("tensor")
    cos, sin, first = rope_tables(segments, rows, t * rows)
    extra = jnp.concatenate([attn_gain.reshape(2, -1), mlp_gain.reshape(2, -1), jnp.zeros((28, 2 * HD), BF)], 0)
    w_kv = jnp.concatenate([jnp.concatenate([w_key, w_value], 1), extra], 0)
    h, a1, r1, r2, gains, q, o, lse, kv, wkv, wq, wo, wg, wu, wd, a2, ct = attn_gather(w_kv, w_query, w_out, w_gate, w_up, w_down, cotangent, tokens, cos, sin, first)
    wkv, wq, wo = wkv.reshape(4, 8, -1, 2 * HD), wq.reshape(4, width, -1), wo.reshape(8, 4, -1, cols)
    da2, mo, mo_near, gg, gu, gd = mlp(a2, ct, wg.reshape(width, -1), wu.reshape(width, -1), wd.reshape(8, hidden, -1))
    dres, gain2_part = rms_backward(h, r2, gains[1:2], da2)
    dh = cotangent.astype(F32) + dres
    da1, go, gq, gkv, mo_far = attn_back(wo, wq, wkv, mo, q, o, kv, lse, dh.astype(BF), a1, tokens, r1, gain2_part[None, :], cos, sin, first)
    mo_own = lax.dynamic_index_in_dim(mo, t, 0, keepdims=False)
    output = (h + mo_own.astype(F32) + mo_near[0].astype(F32) + mo_near[1].astype(F32) + mo_far.astype(F32)).astype(BF)
    din, _ = rms_backward(tokens.astype(F32), r1, gains[0:1], da1)
    grad_tokens = dh + din
    gain_grads = gkv[cols : cols + 4].reshape(2, -1)
    gkv = gkv[:cols]
    return (output, grad_tokens, gain_grads[0], gq, gkv[:, :HD], gkv[:, HD:], go, gain_grads[1], gg.astype(F32), gu.astype(F32), gd.astype(F32))


def body_plain(tokens, segments, attn_gain, w_query, w_key, w_value, w_out, mlp_gain, w_gate, w_up, w_down, cotangent):
    rows, width = tokens.shape
    hidden = w_gate.shape[1]
    nt = lax.axis_size("tensor")
    row0 = lax.axis_index("tensor") * rows
    cos, sin, first = rope_tables(segments, rows, row0)
    row0_s = row0[None].astype(jnp.int32)

    gain1 = lax.all_gather(attn_gain, "dp", axis=0, tiled=True).astype(F32)
    gain2 = lax.all_gather(mlp_gain, "dp", axis=0, tiled=True).astype(F32)
    w_kv = jnp.concatenate([w_key, w_value], 1)
    full = lambda w, axis: lax.all_gather(lax.all_gather(w, "dp", axis=axis, tiled=True), "tensor", axis=0)
    wq = full(w_query, 0)
    wkv = full(w_kv, 0)
    wo = full(w_out, 1).reshape(width, width)
    wg = lax.all_gather(w_gate, "dp", axis=0, tiled=True)
    wu = lax.all_gather(w_up, "dp", axis=0, tiled=True)
    wd = lax.all_gather(w_down, "dp", axis=1, tiled=True)

    x = tokens.astype(F32)
    n1, r1 = rms_forward(x, gain1)
    a1 = n1.astype(BF)
    kv = jnp.einsum("rd,gdc->grc", a1, wkv, preferred_element_type=F32)
    cos_r, sin_r = cos.T, sin.T
    k = kv[..., :HD]
    k = k * cos_r + jnp.concatenate([-k[..., HD // 2 :], k[..., : HD // 2]], -1) * sin_r
    kv = jnp.concatenate([k, kv[..., HD:]], -1).astype(BF)
    kv = lax.all_gather(kv, "tensor", axis=1, tiled=True)
    o, q, lse = attn_forward(row0_s, a1, wq, kv, cos, sin, first)
    o2 = o.reshape(-1, rows)
    h = x + dot_tn(o2, wo)

    n2, r2 = rms_forward(h, gain2)
    a2 = lax.all_gather(n2.astype(BF), "tensor", axis=0, tiled=True)
    cot = lax.all_gather(cotangent, "tensor", axis=0, tiled=True)
    output, da2, gg, gu, gd = mlp_plain(h, a2, cot, wg, wu, wd)
    dres, gain2_part = rms_backward(h, r2, gain2, da2)
    dh = cotangent.astype(F32) + dres
    dhb = dh.astype(BF)

    do = dot_nt(wo, dhb).astype(BF).reshape(o.shape)
    go_part = dot_nn(o2, dhb)
    dq, dkv = attn_backward(row0_s, q, kv, do, o, lse, cos, sin, first)
    groups = dkv.shape[0]
    dkv = lax.psum_scatter(dkv.astype(BF), "tensor", scatter_dimension=1, tiled=True).astype(F32)
    dk = dkv[..., :HD]
    ws = dk * sin_r
    dk = dk * cos_r + jnp.concatenate([ws[..., HD // 2 :], -ws[..., : HD // 2]], -1)
    dkv = jnp.concatenate([dk, dkv[..., HD:]], -1).astype(BF)
    gq_part = jnp.einsum("rd,gcr->gdc", a1, dq, preferred_element_type=F32)
    gkv_part = jnp.einsum("rd,grc->gdc", a1, dkv, preferred_element_type=F32)
    da1 = jnp.einsum("gcr,gdc->rd", dq, wq, preferred_element_type=F32) + jnp.einsum("grc,gdc->rd", dkv, wkv, preferred_element_type=F32)
    din, gain1_part = rms_backward(x, r1, gain1, da1)
    grad_tokens = dh + din

    def home_all(v, dim):
        return lax.psum_scatter(home(v, dim + 1), "tensor", scatter_dimension=0, tiled=False).astype(F32)

    gq = home_all(gq_part, 0)
    gkv = home_all(gkv_part, 0)
    go = home_all(go_part.reshape(nt, -1, width), 1)
    gains = lax.psum_scatter(jnp.stack([gain1_part, gain2_part]), "dp", scatter_dimension=1, tiled=True)
    gains = lax.psum(gains, "tensor")
    return (output, grad_tokens, gains[0], gq, gkv[:, :HD], gkv[:, HD:], go, gains[1], gg, gu, gd)


def solution(mesh):
    rows, block = P(("dp", "tensor"), None), P("dp", "tensor")
    turned, line = P("tensor", "dp"), P("dp")
    return jax.shard_map(
        body if (mesh.shape["dp"], mesh.shape["tensor"]) == (8, 4) else body_plain,
        mesh=mesh,
        in_specs=(rows, line, line, block, block, block, turned, line, block, block, turned, rows),
        out_specs=(rows, rows, line, block, block, block, turned, line, block, block, turned),
        check_vma=False,
    )
```

```python
import functools
import math

import jax
import jax.numpy as jnp
from jax import lax
from jax.experimental import pallas as pl
from jax.experimental.pallas import tpu as pltpu
from jax.sharding import PartitionSpec as P

HD = 64
RATIO = 8
EPSILON = 1e-05
MASKED = -1e30
BF = jnp.bfloat16
F32 = jnp.float32


def dot_nn(left, right):
    return lax.dot_general(left, right, (((1,), (0,)), ((), ())), preferred_element_type=F32)


def dot_nt(left, right):
    return lax.dot_general(left, right, (((1,), (1,)), ((), ())), preferred_element_type=F32)


def dot_tn(left, right):
    return lax.dot_general(left, right, (((0,), (0,)), ((), ())), preferred_element_type=F32)


def rms_forward(values_in, gain_row):
    factor = lax.rsqrt(jnp.mean(values_in * values_in, axis=-1, keepdims=True) + EPSILON)
    return (values_in * factor * gain_row, factor)


def rms_backward(values_in, factor, gain_row, gradient):
    scaled = gain_row * gradient
    grad_gain = jnp.sum(gradient * values_in * factor, axis=0)
    grad_input = factor * scaled - values_in * (factor * factor * factor) * jnp.mean(
        scaled * values_in, axis=-1, keepdims=True
    )
    return (grad_input, grad_gain)


def rope_t(u, cos, sin):
    half = HD // 2
    return u * cos + jnp.concatenate([-u[half:], u[:half]], 0) * sin


def rope_back_t(w, cos, sin):
    half = HD // 2
    ws = w * sin
    return w * cos + jnp.concatenate([ws[half:], -ws[:half]], 0)


def bias_of(first, row0, keys, rows):
    key = lax.broadcasted_iota(jnp.int32, (keys, rows), 0)
    row = lax.broadcasted_iota(jnp.int32, (keys, rows), 1) + row0
    return jnp.where((key <= row) & (key >= first), 0.0, MASKED).astype(F32)


def attn_forward_kernel(row0_ref, a1_ref, wq_ref, kv_ref, cos_ref, sin_ref, first_ref, o_ref, q_ref, lse_ref, bias_ref, s_ref, vt_ref):
    keys, rows = bias_ref.shape

    @pl.when(pl.program_id(0) == 0)
    def _():
        bias_ref[...] = bias_of(first_ref[...], row0_ref[0], keys, rows)

    kv = kv_ref[0]
    kvt = kv.T
    vt_ref[...] = jnp.concatenate([kvt[HD:], jnp.ones((16, keys), BF)], 0)
    qt = dot_nn(a1_ref[...], wq_ref[0]).T
    cos, sin = cos_ref[...], sin_ref[...]
    for h in range(RATIO):
        q = (rope_t(qt[h * HD : (h + 1) * HD], cos, sin) * HD ** (-0.5)).astype(BF)
        q_ref[0, h * HD : (h + 1) * HD] = q
        s_ref[...] = dot_nn(kv, jnp.concatenate([q, jnp.zeros_like(q)], 0)) + bias_ref[...]
        peak = jnp.max(s_ref[...], axis=0, keepdims=True)
        e = jnp.exp(s_ref[...] - peak).astype(BF)
        ot = dot_nn(vt_ref[...], e)
        total = ot[HD : HD + 1]
        o_ref[0, h * HD : (h + 1) * HD] = (ot[:HD] / total).astype(BF)
        lse_ref[0, h : h + 1] = peak + jnp.log(total)


def attn_backward_kernel(row0_ref, q_ref, kv_ref, do_ref, o_ref, lse_ref, cos_ref, sin_ref, first_ref, dq_ref, dkv_ref, bias_ref, acc_ref):
    keys, rows = bias_ref.shape

    @pl.when(pl.program_id(0) == 0)
    def _():
        bias_ref[...] = bias_of(first_ref[...], row0_ref[0], keys, rows)

    kv = kv_ref[0]
    kt = kv.T[:HD]
    cos, sin = cos_ref[...], sin_ref[...]
    for h in range(RATIO):
        part = slice(h * HD, (h + 1) * HD)
        q, do, o = q_ref[0, part], do_ref[0, part], o_ref[0, part]
        qz = jnp.concatenate([q, jnp.zeros_like(q)], 0)
        doz = jnp.concatenate([jnp.zeros_like(do), do], 0)
        delta = jnp.sum(do.astype(F32) * o.astype(F32), axis=0, keepdims=True)
        p = jnp.exp(dot_nn(kv, qz) + bias_ref[...] - lse_ref[0, h : h + 1])
        ds = (p * (dot_nn(kv, doz) - delta)).astype(BF)
        grad = dot_nt(ds, qz) + dot_nt(p.astype(BF), doz)
        if h == 0:
            acc_ref[...] = grad
        else:
            acc_ref[...] += grad
        dq = dot_nn(kt, ds) * HD ** (-0.5)
        dq_ref[0, part] = rope_back_t(dq, cos, sin).astype(BF)
    dkv_ref[0] = acc_ref[...]


def params():
    return pltpu.CompilerParams(vmem_limit_bytes=56 * 2**20)


def attn_forward(row0, a1, wq, kv, cos, sin, first):
    groups, width, cols = wq.shape
    rows, keys = a1.shape[0], kv.shape[1]
    whole = lambda *shape: pl.BlockSpec(shape, lambda i: (0,) * len(shape))
    part = lambda *shape: pl.BlockSpec((1,) + shape, lambda i: (i,) + (0,) * len(shape))
    return pl.pallas_call(
        attn_forward_kernel,
        grid=(groups,),
        in_specs=[pl.BlockSpec(memory_space=pltpu.SMEM), whole(rows, width), part(width, cols), part(keys, 2 * HD), whole(HD, rows), whole(HD, rows), whole(1, rows)],
        out_specs=[part(cols, rows), part(cols, rows), part(RATIO, rows)],
        out_shape=[jax.ShapeDtypeStruct((groups, cols, rows), BF), jax.ShapeDtypeStruct((groups, cols, rows), BF), jax.ShapeDtypeStruct((groups, RATIO, rows), F32)],
        scratch_shapes=[pltpu.VMEM((keys, rows), F32), pltpu.VMEM((keys, rows), F32), pltpu.VMEM((HD + 16, keys), BF)],
        compiler_params=params(),
        name="attn_forward",
    )(row0, a1, wq, kv, cos, sin, first)


def attn_backward(row0, q, kv, do, o, lse, cos, sin, first):
    groups, cols, rows = q.shape
    keys = kv.shape[1]
    whole = lambda *shape: pl.BlockSpec(shape, lambda i: (0,) * len(shape))
    part = lambda *shape: pl.BlockSpec((1,) + shape, lambda i: (i,) + (0,) * len(shape))
    return pl.pallas_call(
        attn_backward_kernel,
        grid=(groups,),
        in_specs=[pl.BlockSpec(memory_space=pltpu.SMEM), part(cols, rows), part(keys, 2 * HD), part(cols, rows), part(cols, rows), part(RATIO, rows), whole(HD, rows), whole(HD, rows), whole(1, rows)],
        out_specs=[part(cols, rows), part(keys, 2 * HD)],
        out_shape=[jax.ShapeDtypeStruct((groups, cols, rows), BF), jax.ShapeDtypeStruct((groups, keys, 2 * HD), F32)],
        scratch_shapes=[pltpu.VMEM((keys, rows), F32), pltpu.VMEM((keys, 2 * HD), F32)],
        compiler_params=params(),
        name="attn_backward",
    )(row0, q, kv, do, o, lse, cos, sin, first)


MESH = pl.DeviceIdType.MESH
ANY = pl.BlockSpec(memory_space=pl.ANY)


class Place:
    def __init__(self):
        d, self.t = lax.axis_index("dp"), lax.axis_index("tensor")
        self.c, self.p = d % 2, d // 2
        x, y = self.p % 2, self.p // 2
        self.px, self.py, self.pd = self.p + 1 - 2 * x, self.p + 2 - 4 * y, 3 - self.p
        self.across = [self.t + 1 - 2 * (self.t % 2), (self.t + 2) % 4, 3 - self.t]
        self.inner = (self.t == 1) | (self.t == 2)
        self.outer = (self.t == 0) | (self.t == 3)
        inner = self.t * (3 - self.t) // 2
        self.order = [self.t, self.across[0], 2 - self.t // 2, 3 - self.t // 2 * 3]
        self.far = [0, 1, 2 - inner, 3 - inner]
        self.way = [0, 1 - self.t % 2, 1 - self.t // 2, 1 - self.t // 2]

    def at(self, p, c, t):
        return {"dp": p * 2 + c, "tensor": t}

    def x_side(self):
        return self.at(self.px, self.c, self.t)

    def y_side(self):
        return self.at(self.py, self.c, self.t)

    def twin(self):
        return self.at(self.p, 1 - self.c, self.t)

    def line(self, t):
        return self.at(self.p, self.c, t)

    def greet(self):
        barrier = pltpu.get_barrier_semaphore()
        others = [self.x_side(), self.y_side(), self.twin()] + [self.line(t) for t in self.across]
        for other in others:
            pl.semaphore_signal(barrier, inc=1, device_id=other, device_id_type=MESH)
        pl.semaphore_wait(barrier, len(others))


def half_of(ref, part):
    rows = ref.shape[0] // 2
    return ref.at[pl.ds(part * rows, rows)]


def attn_gather_kernel(kv_in, wq_in, wo_in, wg_in, wu_in, wd_in, ct_in, x_ref, cos_ref, sin_ref, first_ref, h_ref, a1_ref, r1_ref, r2_ref, gains_ref, q_ref, o_ref, lse_ref, kv_ref, kv_out, q_out, o_out, g_out, u_out, d_out, a2_all, ct_all, wkv, wq, wo, rows_kv, bias_ref, s_ref, vt_ref, qt_ref, o_rows, a2_ref, z_send, z_recv, send, recv, local, load, kv_send, kv_recv, line_send, line_recv):
    me = Place()
    rows, width = x_ref.shape
    keys, cols = kv_ref.shape[1], width // 8
    me.greet()
    sources = [kv_in, wq_in, wo_in, wg_in, wu_in, wd_in]
    outs = [kv_out, q_out, o_out, g_out, u_out, d_out]

    def piece(k, s, p, c):
        if k == 2:
            return o_out.at[p, c, s]
        return outs[k].at[s, p, c] if k < 2 else outs[k].at[p, c]

    def pair(k, s, c):
        if k == 2:
            return o_out.at[:, c, s]
        if k == 0:
            return kv_out.at[:, :, c]
        return q_out.at[s, :, c] if k == 1 else outs[k].at[:, c]

    def line_copy(k, chunk, way, step, own=False):
        dst = piece(k, chunk, me.p, me.c)
        src = sources[k] if own else dst
        at = (k, way, step - 1)
        return copy_to(src, dst, z_send.at[at], z_recv.at[at], me.line(me.t + 1 - 2 * way))

    def line_first(k, action):
        for way in range(2):

            @pl.when(me.t < 3 if way == 0 else me.t > 0)
            def _():
                copy = line_copy(k, me.t, way, 1, True)
                copy.start() if action == "start" else copy.wait_send()

    def line_next(k, j, action):
        target = me.t + 1 - 2 * me.way[j]

        @pl.when((target >= 0) & (target <= 3))
        def _():
            copy = line_copy(k, me.order[j], me.way[j], me.far[j] + 1)
            copy.start() if action == "start" else copy.wait_send()

    def push(k, j, kind):
        s, i = me.order[j], (0, 1 + j, 5 + j, 9, 10, 11)[k]
        part = (lambda p: kv_out.at[:, p, me.c]) if k == 0 else (lambda p: piece(k, s, p, me.c))
        if kind < 2:
            dst = part(me.p)
            src = sources[k] if j == 0 and k > 0 else dst
        elif kind < 4:
            src = dst = half_of(part(me.px if kind == 2 else me.py), kind - 2)
        else:
            src = dst = pair(k, s, me.c)
        to = [me.x_side, me.y_side, me.y_side, me.x_side, me.twin][kind]()
        return copy_to(src, dst, send.at[i, kind], recv.at[i, kind], to)

    def keep(k):
        return pltpu.make_async_copy(sources[k], piece(k, me.t, me.p, me.c), local.at[k])

    def arrive(k, j):
        line_copy(k, me.order[j], me.way[j], me.far[j]).wait_recv()
        line_next(k, j, "start")

    def first(k, j):
        if k == 0:
            keep(k).wait()
        elif j == 0:
            keep(k).start()
        push(k, j, 0).start()
        push(k, j, 1).start()

    def second(k, j):
        push(k, j, 0).wait_recv()
        push(k, j, 2).start()
        push(k, j, 1).wait_recv()
        push(k, j, 3).start()

    def third(k, j):
        push(k, j, 2).wait_recv()
        push(k, j, 3).wait_recv()
        if j == 0 and k > 0:
            keep(k).wait()
        push(k, j, 4).start()

    def last(k, j):
        push(k, j, 4).wait_recv()

    def step(n, k, action):
        t, out, own = me.t, (ct_all, a2_all)[n], (ct_in, a2_ref)[n]
        for way, chunk, can in ((0, t - k + 1, (t < 3) & (t - k + 1 >= 0)), (1, t + k - 1, (t > 0) & (t + k - 1 <= 3))):

            @pl.when(can)
            def _():
                src = own if k == 1 else out.at[chunk]
                copy = copy_to(src, out.at[chunk], line_send.at[n, way, k - 1], line_recv.at[n, way, k - 1], me.line(t + 1 - 2 * way))
                copy.start() if action == "start" else copy.wait_send()

    def got(n, k):
        t, out = me.t, (ct_all, a2_all)[n]
        for way, chunk, can in ((0, t - k, t - k >= 0), (1, t + k, t + k <= 3)):

            @pl.when(can)
            def _():
                copy_to(out.at[chunk], out.at[chunk], line_send.at[n, way, k - 1], line_recv.at[n, way, k - 1], me.line(t + 1 - 2 * way)).wait_recv()

    def own_rows(n):
        return pltpu.make_async_copy((ct_in, a2_ref)[n], (ct_all, a2_all)[n].at[me.t], local.at[6 + n])

    kv_load = pltpu.make_async_copy(kv_out, wkv, load.at[0])
    kv_keep = pltpu.make_async_copy(rows_kv, kv_ref, load.at[1])

    def wq_load(j):
        return pltpu.make_async_copy(q_out.at[me.order[j]], wq.at[j % 2], load.at[2 + j % 2])

    def wo_load(j):
        s = me.order[j]
        return pltpu.make_async_copy(o_out.at[:, :, s], wo.at[:, :, pl.ds(pl.multiple_of(s * 2 * cols, cols), 2 * cols)], load.at[4 + j])

    own = pl.ds(pl.multiple_of(me.t * rows, rows), rows)

    def kv_push(j):
        part = rows_kv.at[:, own]
        return copy_to(part, part, kv_send.at[j - 1], kv_recv.at[j - 1], me.line(me.across[j - 1]))

    def gain(n):
        parts = [wkv[0, d // 2, d % 2, cols + 2 * n + e : cols + 2 * n + e + 1] for d in range(8) for e in range(2)]
        return jnp.concatenate(parts, 1).astype(F32)

    def norm(value):
        return lax.rsqrt(jnp.mean(value * value, axis=-1, keepdims=True) + EPSILON)

    def project_keys():
        x = x_ref[...].astype(F32)
        r1_ref[...] = norm(x)
        gains_ref[0:1] = gain(0)
        gains_ref[1:2] = gain(1)
        a1_ref[...] = (x * r1_ref[...] * gains_ref[0:1]).astype(BF)
        for s in range(4):
            weights = wkv[s, :, :, :cols].reshape(width, 2 * HD)
            kvt = dot_nn(a1_ref[...], weights).T
            kvt = jnp.concatenate([rope_t(kvt[:HD], cos_ref[...], sin_ref[...]), kvt[HD:]], 0).astype(BF)
            rows_kv[s, own] = kvt.T

    def attend(j):
        g = me.order[j]
        qt_ref[...] = dot_nn(a1_ref[...], wq[j % 2].reshape(width, -1)).T
        kv = rows_kv[g]
        vt_ref[...] = jnp.concatenate([kv.T[HD:], jnp.ones((16, keys), BF)], 0)
        cos, sin = cos_ref[...], sin_ref[...]

        def head(h, _):
            part = pl.ds(pl.multiple_of(h * HD, HD), HD)
            q = (rope_t(qt_ref[part], cos, sin) * HD ** (-0.5)).astype(BF)
            q_ref[g, part] = q
            s_ref[...] = dot_nn(kv, jnp.concatenate([q, jnp.zeros_like(q)], 0)) + bias_ref[...]
            peak = jnp.max(s_ref[...], axis=0, keepdims=True)
            e = jnp.exp(s_ref[...] - peak).astype(BF)
            ot = dot_nn(vt_ref[...], e)
            total = ot[HD : HD + 1]
            o_ref[g, part] = (ot[:HD] / total).astype(BF)
            lse_ref[g, pl.ds(h, 1)] = peak + jnp.log(total)
            return 0

        lax.fori_loop(0, RATIO, head, 0, unroll=2)
        o_rows[:, pl.ds(pl.multiple_of(g * 2 * cols, cols), 2 * cols)] = o_ref[g].T

    def mix():
        for d in range(8):
            part = slice(d * cols, (d + 1) * cols)
            h_ref[:, part] = x_ref[:, part].astype(F32) + dot_nn(o_rows[...], wo[d // 2, d % 2])
        h = h_ref[...]
        r2_ref[...] = norm(h)
        a2_ref[...] = (h * r2_ref[...] * gains_ref[1:2]).astype(BF)

    KV, Q, O, G, U, D = range(6)
    keep(KV).start()
    line_first(KV, "start")
    line_first(Q, "start")
    first(Q, 0)
    first(O, 0)
    own_rows(0).start()
    for j in (1, 2, 3):
        arrive(KV, j)
    first(KV, 0)
    bias_ref[...] = bias_of(first_ref[...], me.t * rows, keys, rows)
    second(Q, 0)
    arrive(Q, 1)
    first(Q, 1)
    line_first(O, "start")
    second(KV, 0)
    second(O, 0)
    arrive(Q, 2)
    first(Q, 2)
    third(KV, 0)
    third(Q, 0)
    arrive(Q, 3)
    second(Q, 1)
    last(KV, 0)
    kv_load.start()
    last(Q, 0)
    wq_load(0).start()
    first(Q, 3)
    kv_load.wait()
    project_keys()
    for j in (1, 2, 3):
        kv_push(j).start()
    arrive(O, 1)
    third(Q, 1)
    second(Q, 2)
    step(0, 1, "start")
    first(O, 1)
    arrive(O, 2)
    second(Q, 3)
    third(Q, 2)
    first(O, 2)
    last(Q, 1)
    wq_load(1).start()
    arrive(O, 3)
    for j in (1, 2, 3):
        kv_push(j).wait_recv()
    kv_keep.start()
    wq_load(0).wait()
    attend(0)
    first(O, 3)
    third(Q, 3)
    second(O, 1)
    third(O, 0)
    got(0, 1)
    step(0, 2, "start")
    wq_load(1).wait()
    attend(1)
    last(Q, 2)
    wq_load(2).start()
    second(O, 2)
    third(O, 1)
    first(G, 0)
    wq_load(2).wait()
    attend(2)
    last(Q, 3)
    wq_load(3).start()
    second(O, 3)
    third(O, 2)
    last(O, 0)
    wo_load(0).start()
    last(O, 1)
    wo_load(1).start()
    wq_load(3).wait()
    attend(3)
    third(O, 3)
    first(U, 0)
    last(O, 2)
    wo_load(2).start()
    last(O, 3)
    wo_load(3).start()
    for j in range(4):
        wo_load(j).wait()
    mix()
    own_rows(1).start()
    step(1, 1, "start")
    second(G, 0)
    first(D, 0)
    third(G, 0)
    second(U, 0)
    got(1, 1)
    step(1, 2, "start")
    third(U, 0)
    second(D, 0)
    got(1, 2)
    step(1, 3, "start")
    third(D, 0)
    for k in (G, U, D):
        last(k, 0)
    got(0, 2)
    got(1, 3)
    kv_keep.wait()
    for n in range(2):
        own_rows(n).wait()
        for k in (1, 2, 3)[: 2 + n]:
            step(n, k, "wait")
    for j in (1, 2, 3):
        kv_push(j).wait_send()
        for k in (KV, Q, O):
            line_next(k, j, "wait")
    for k in (KV, Q, O):
        line_first(k, "wait")
    for k in range(6):
        for j in range(4 if k in (Q, O) else 1):
            for kind in range(5):
                push(k, j, kind).wait_send()


def attn_gather(kv, wq, wo, wg, wu, wd, ct, x, cos, sin, first):
    rows, width = x.shape
    heads, cols, keys = wq.shape[1], wq.shape[0], 4 * rows
    dma, vmem = pltpu.SemaphoreType.DMA, lambda *shape: pltpu.VMEM(shape, BF)
    low = lambda *dims: jax.ShapeDtypeStruct(dims, BF)
    full = lambda *dims: jax.ShapeDtypeStruct(dims, F32)
    inside = pl.BlockSpec(memory_space=pltpu.VMEM)
    return pl.pallas_call(
        attn_gather_kernel,
        out_shape=[
            full(rows, width), low(rows, width), full(rows, 1), full(rows, 1), full(2, width), low(4, heads, rows), low(4, heads, rows), full(4, RATIO, rows),
            low(4, keys, 2 * HD), low(4, 4, 2, *kv.shape), low(4, 4, 2, *wq.shape), low(4, 2, 4, *wo.shape),
            low(4, 2, *wg.shape), low(4, 2, *wu.shape), low(4, 2, *wd.shape), low(4, rows, width), low(4, rows, width),
        ],
        in_specs=[ANY] * 7 + [inside] * 4,
        out_specs=[inside] * 8 + [ANY] * 9,
        scratch_shapes=[
            vmem(4, 4, 2, *kv.shape), vmem(2, 4, 2, cols, heads), vmem(4, 2, width, cols), vmem(4, keys, 2 * HD),
            pltpu.VMEM((keys, rows), F32), pltpu.VMEM((keys, rows), F32), vmem(HD + 16, keys), pltpu.VMEM((heads, rows), F32), vmem(rows, width), vmem(rows, width),
            dma((3, 2, 3)), dma((3, 2, 3)), dma((12, 5)), dma((12, 5)), dma((8,)), dma((8,)), dma((3,)), dma((3,)), dma((2, 2, 3)), dma((2, 2, 3)),
        ],
        compiler_params=pltpu.CompilerParams(collective_id=1, has_side_effects=True, vmem_limit_bytes=56 * 2**20),
        name="attn_gather",
    )(kv, wq, wo, wg, wu, wd, ct, x, cos, sin, first)


def xor4(a, m):
    return (a // 2 + m // 2) % 2 * 2 + (a % 2 + m % 2) % 2


def copy_to(src, dst, send_sem, recv_sem, to):
    return pltpu.make_async_remote_copy(src, dst, send_sem, recv_sem, device_id=to, device_id_type=MESH)


def add_low(left, right):
    return (left.astype(F32) + right.astype(F32)).astype(BF)


def mlp_kernel(a2_in, ct_old, wg_in, wu_in, wd_in, ct_in, da2_out, mo_out, mo_got, gg_out, gu_out, gd_out, twin_g, twin_u, twin_d, wg, wu, wd, a2_buf, ct_buf, mo_buf, a2_col, ct_col, zt, dg, du, out_buf, in_buf, diag_gu, x_gu, y_gu, diag_d, x_d, y_d, stage_gu, stage_d, load, store, line_send, line_recv, ct_send, ct_recv, mo_send, mo_recv, twin_send, twin_recv, send, recv, stage_sem):
    me = Place()
    rows, width = da2_out.shape
    hidden = wg.shape[1]
    cols = width // 8
    weights = [pltpu.make_async_copy(wg_in, wg, load.at[4]), pltpu.make_async_copy(wu_in, wu, load.at[5])]
    weights += [pltpu.make_async_copy(wd_in.at[d], wd.at[:, pl.ds(d * cols, cols)], load.at[6 + d]) for d in range(8)]
    for copy in weights:
        copy.start()

    def away(j):
        return 2 * (1 - j % 2) + (j % 2 + j // 2) % 2

    ct_push = copy_to(ct_in.at[xor4(me.t, 2)], ct_in.at[xor4(me.t, 2)], ct_send.at[0], ct_recv.at[0], me.line(xor4(me.t, 1)))

    def chunk_load(j, slot):
        s = xor4(me.t, away(j))
        return pltpu.make_async_copy(a2_in.at[s], a2_buf.at[slot], load.at[slot]), pltpu.make_async_copy(ct_in.at[s], ct_buf.at[slot], load.at[2 + slot])

    near, cross, both = in_buf.at[0], in_buf.at[1], in_buf.at[pl.ds(2, 2)]

    def near_send():
        return copy_to(out_buf.at[0], near, line_send.at[0], line_recv.at[0], me.line(xor4(me.t, 1)))

    def both_send(m):
        s = xor4(me.t, m)
        return copy_to(out_buf.at[m - 1], both.at[s % 2], line_send.at[m - 1], line_recv.at[2 + s % 2], me.line(xor4(me.t, 1)))

    def cross_send(m):
        return copy_to(out_buf.at[m - 1], cross, line_send.at[m - 1], line_recv.at[1], me.line(xor4(me.t, m)))

    def cross_add(m):
        s = xor4(me.t, m)
        copy_to(both.at[s % 2], both.at[s % 2], line_send.at[0], line_recv.at[2 + s % 2], me.line(xor4(me.t, 1))).wait_recv()
        out_buf[m - 1] = add_low(out_buf[m - 1], both[s % 2])
        cross_send(m).start()

    def mo_store(j, slot):
        return pltpu.make_async_copy(mo_buf.at[slot], mo_out.at[xor4(me.t, away(j))], store.at[slot])

    for copy in chunk_load(0, 0):
        copy.start()
    me.greet()

    @pl.when(me.inner)
    def _():
        ct_push.start()

    def chunk(j, _):
        slot = j % 2

        for copy in chunk_load(j, slot):
            copy.wait()
        where = pl.multiple_of(xor4(me.t, away(j)) * rows, rows)

        @pl.when(j == 0)
        def _():
            weights[0].wait()

        g = dot_nn(a2_buf[slot], wg[...])

        @pl.when(j == 0)
        def _():
            for copy in weights[1:]:
                copy.wait()

        u = dot_nn(a2_buf[slot], wu[...])
        dz = dot_nt(ct_buf[slot], wd[...])
        sig = 1.0 / (1.0 + jnp.exp(-g))
        act = g * sig
        z = (act * u).astype(BF)
        zt[:, pl.ds(where, rows)] = z.T
        dg_now = (dz * u * (sig * (1.0 + g * (1.0 - sig)))).astype(BF)
        du_now = (dz * act).astype(BF)
        dg[pl.ds(where, rows)] = dg_now
        du[pl.ds(where, rows)] = du_now
        part = dot_nt(dg_now, wg[...]) + dot_nt(du_now, wu[...])

        @pl.when(j < 3)
        def _():
            out_buf[away(j) - 1] = part.astype(BF)

        @pl.when((j == 1) & me.inner)
        def _():
            near_send().start()

        for at, m in ((0, 2), (2, 3)):

            @pl.when((j == at) & me.outer)
            def _():
                both_send(m).start()

        @pl.when(j == 3)
        def _():
            da2_out[...] = part

        @pl.when((j == 1) & me.outer)
        def _():
            ct_push.wait_recv()

        @pl.when(j < 3)
        def _():
            for copy in chunk_load(j + 1, 1 - slot):
                copy.start()

        @pl.when(j >= 2)
        def _():
            mo_store(j - 2, slot).wait()

        mo_buf[slot] = dot_nn(z, wd[...]).astype(BF)
        mo_store(j, slot).start()
        return 0

    lax.fori_loop(0, 4, chunk, 0)
    mo_store(2, 0).wait()
    mo_store(3, 1).wait()

    def mo_push(m):
        return copy_to(mo_out.at[xor4(me.t, m)], mo_got.at[m - 1], mo_send.at[m - 1], mo_recv.at[m - 1], me.line(xor4(me.t, m)))

    @pl.when(me.inner)
    def _():
        cross_add(3)

    def owner(i):
        return xor4(me.p, 3 - i % 4) * 2 + (1 - me.c + i // 4) % 2

    def tile_load(i, slot):
        at = pl.ds(pl.multiple_of(owner(i) * cols, cols), cols)
        return pltpu.make_async_copy(a2_in.at[:, :, at], a2_col.at[slot], load.at[slot]), pltpu.make_async_copy(ct_in.at[:, :, at], ct_col.at[slot], load.at[2 + slot])

    def piece(k, p, c):
        at = pl.ds(pl.multiple_of((p * 2 + c) * cols, cols), cols)
        return (wg, wu)[k].at[at] if k < 2 else wd.at[:, at]

    twins = [twin_g, twin_u, twin_d]

    def twin_push(k, i):
        p = xor4(me.p, 3 - i)
        return copy_to(piece(k, p, 1 - me.c), twins[k].at[p], twin_send.at[k, i], twin_recv.at[k, i], me.twin())

    diag = [diag_gu.at[0], diag_gu.at[1], diag_d]
    from_x = [x_gu.at[0], x_gu.at[1], x_d]
    from_y = [y_gu.at[0], y_gu.at[1], y_d]
    stage = [stage_gu.at[0], stage_gu.at[1], stage_d]

    def side(k, kind):
        if kind < 2:
            src, dst = half_of(piece(k, me.pd, me.c), kind), half_of(diag[k], kind)
        else:
            src, dst = (piece(k, me.px, me.c), from_x[k]) if kind == 2 else (piece(k, me.py, me.c), from_y[k])
        return copy_to(src, dst, send.at[k, kind], recv.at[k, kind], me.x_side() if kind % 2 == 0 else me.y_side())

    def fetch(k, p):
        return pltpu.make_async_copy(twins[k].at[p], stage[k], stage_sem.at[k])

    for copy in tile_load(0, 0):
        copy.start()

    def tile(i, _):
        slot = i % 2

        @pl.when(i < 7)
        def _():
            for copy in tile_load(i + 1, 1 - slot):
                copy.start()

        for copy in tile_load(i, slot):
            copy.wait()
        at = pl.ds(pl.multiple_of(owner(i) * cols, cols), cols)
        a2t = a2_col[slot].reshape(4 * rows, cols).T
        wg[at] = dot_nn(a2t, dg[...]).astype(BF)
        wu[at] = dot_nn(a2t, du[...]).astype(BF)
        wd[:, at] = dot_nn(zt[...], ct_col[slot].reshape(4 * rows, cols)).astype(BF)

        @pl.when(i < 4)
        def _():
            for k in range(3):
                twin_push(k, i).start()

        @pl.when(i >= 4)
        def _():
            p = xor4(me.p, 7 - i)
            for k in range(3):
                twin_push(k, i - 4).wait_recv()
                fetch(k, p).start()
            for k in range(3):
                fetch(k, p).wait()
                mine = piece(k, p, me.c)
                mine[...] = add_low(mine[...], stage[k][...])

        @pl.when(i == 4)
        def _():
            for k in range(3):
                side(k, 0).start()
                side(k, 1).start()

        @pl.when((i == 5) & me.inner)
        def _():
            cross_add(2)

        @pl.when((i == 5) & me.outer)
        def _():
            near_send().start()

        @pl.when(i == 5)
        def _():
            for m in (1, 2):
                mo_push(m).start()

        return 0

    lax.fori_loop(0, 8, tile, 0)
    for k in range(3):
        side(k, 1).wait_recv()
        part, extra = half_of(piece(k, me.px, me.c), 1), half_of(diag[k], 1)
        part[...] = add_low(part[...], extra[...])
        side(k, 2).start()
        side(k, 0).wait_recv()
        part, extra = half_of(piece(k, me.py, me.c), 0), half_of(diag[k], 0)
        part[...] = add_low(part[...], extra[...])
        side(k, 3).start()
    results = []
    for k in range(3):
        side(k, 2).wait_recv()
        side(k, 3).wait_recv()
        mine = piece(k, me.p, me.c)
        mine[...] = (mine[...].astype(F32) + from_x[k][...].astype(F32) + from_y[k][...].astype(F32)).astype(BF)
        results.append(pltpu.make_async_copy(mine, (gg_out, gu_out, gd_out)[k], stage_sem.at[k]))
        results[-1].start()
    near_send().wait_recv()
    cross_send(2).wait_recv()
    da2_out[...] += in_buf[0].astype(F32) + in_buf[1].astype(F32)
    for copy in results:
        copy.wait()
    for m in (1, 2):
        mo_push(m).wait()

    @pl.when(me.inner)
    def _():
        ct_push.wait_send()

    near_send().wait_send()
    for m in (2, 3):
        cross_send(m).wait_send()
    for k in range(3):
        for i in range(4):
            twin_push(k, i).wait_send()
            side(k, i).wait_send()


def mlp(a2, ct, wg, wu, wd):
    chunks, rows, width = a2.shape
    hidden, cols = wg.shape[1], width // 8
    dma, vmem = pltpu.SemaphoreType.DMA, lambda *shape: pltpu.VMEM(shape, BF)
    shape = lambda *dims: jax.ShapeDtypeStruct(dims, BF)
    return pl.pallas_call(
        mlp_kernel,
        out_shape=[shape(4, rows, width), jax.ShapeDtypeStruct((rows, width), F32), shape(4, rows, width), shape(2, rows, width), shape(cols, hidden), shape(cols, hidden), shape(hidden, cols), shape(4, cols, hidden), shape(4, cols, hidden), shape(4, hidden, cols)],
        in_specs=[ANY] * 5,
        out_specs=[ANY, pl.BlockSpec(memory_space=pltpu.VMEM)] + [ANY] * 8,
        input_output_aliases={1: 0},
        scratch_shapes=[
            vmem(width, hidden), vmem(width, hidden), vmem(hidden, width),
            vmem(2, rows, width), vmem(2, rows, width), vmem(2, rows, width),
            vmem(2, 4, rows, cols), vmem(2, 4, rows, cols),
            vmem(hidden, 4 * rows), vmem(4 * rows, hidden), vmem(4 * rows, hidden),
            vmem(3, rows, width), vmem(4, rows, width),
            vmem(2, cols, hidden), vmem(2, cols, hidden), vmem(2, cols, hidden),
            vmem(hidden, cols), vmem(hidden, cols), vmem(hidden, cols),
            vmem(2, cols, hidden), vmem(hidden, cols),
            dma((14,)), dma((2,)), dma((3,)), dma((4,)), dma((1,)), dma((1,)), dma((2,)), dma((2,)), dma((3, 4)), dma((3, 4)), dma((3, 4)), dma((3, 4)), dma((3,)),
        ],
        compiler_params=pltpu.CompilerParams(collective_id=2, has_side_effects=True, vmem_limit_bytes=62 * 2**20),
        name="mlp",
    )(a2, ct, wg, wu, wd)[1:7]


def home(v, dim):
    return lax.psum_scatter(v.astype(BF), "dp", scatter_dimension=dim, tiled=True)


def mlp_plain(h, a2, cot, wg, wu, wd):
    g, u = dot_nn(a2, wg), dot_nn(a2, wu)
    sig = jax.nn.sigmoid(g)
    act = g * sig
    z = (act * u).astype(BF)
    scatter = lambda v: lax.psum_scatter(v.astype(BF), "tensor", scatter_dimension=0, tiled=True).astype(F32)
    output = (h + scatter(dot_nn(z, wd))).astype(BF)
    dz = dot_nt(cot, wd)
    dg = (dz * u * (sig * (1.0 + g * (1.0 - sig)))).astype(BF)
    du = (dz * act).astype(BF)
    gd = home(dot_tn(z, cot), 1).astype(F32)
    gg = home(dot_tn(a2, dg), 0).astype(F32)
    gu = home(dot_tn(a2, du), 0).astype(F32)
    da2 = scatter(dot_nt(dg, wg) + dot_nt(du, wu))
    return output, da2, gg, gu, gd


def attn_back_kernel(wo_in, wq_in, wkv_in, mo_in, q_ref, o_ref, kv_ref, lse_ref, dh_ref, a1_ref, x_ref, r1_ref, gain2_ref, cos_ref, sin_ref, first_ref, da1_ref, go_ref, gq_ref, gkv_ref, mo_got, twin_o, twin_q, twin_kv, grad_o, grad_q, grad_kv, diag_o, diag_q, diag_kv, x_o, x_q, x_kv, y_o, y_q, y_kv, z_o, z_q, z_kv, stage_o, stage_q, stage_kv, wo, wq, wkv, a1t, do_ref, bias_ref, acc_ref, dqt_ref, dkv_own, dkv_out, dkv_got, load, mo_sem, dkv_send, dkv_recv, twin_send, twin_recv, send, recv, line_send, line_recv):
    me = Place()
    rows, width = dh_ref.shape
    keys, cols = kv_ref.shape[1], width // 8
    head_of = [3 - me.t // 2 * 3, 2 - me.t // 2, xor4(me.t, 1), me.t]

    def wo_load(j):
        return pltpu.make_async_copy(wo_in.at[:, head_of[j]], wo.at[j % 2], load.at[j % 2])

    def wq_load(j):
        return pltpu.make_async_copy(wq_in.at[head_of[j]], wq, load.at[2])

    wkv_load = pltpu.make_async_copy(wkv_in, wkv, load.at[3])
    mo_push = copy_to(mo_in.at[xor4(me.t, 3)], mo_got, mo_sem.at[0], mo_sem.at[1], me.line(xor4(me.t, 3)))
    wo_load(0).start()
    wo_load(1).start()
    wq_load(0).start()
    wkv_load.start()
    me.greet()
    mo_push.start()
    a1t[...] = a1_ref[...].T
    bias_ref[...] = bias_of(first_ref[...], me.t * rows, keys, rows)

    grads, twins, diags = [grad_o, grad_q, grad_kv], [twin_o, twin_q, twin_kv], [diag_o, diag_q, diag_kv]
    from_x, from_y, from_z = [x_o, x_q, x_kv], [y_o, y_q, y_kv], [z_o, z_q, z_kv]
    stages = [stage_o, stage_q, stage_kv]

    def twin_push(k, j):
        i = k * 4 + j
        return copy_to(grads[k].at[j, :, 1 - me.c], twins[k].at[j], twin_send.at[i], twin_recv.at[i], me.twin())

    def side(k, j, kind):
        i = k * 4 + j
        piece = lambda p: grads[k].at[j, p, me.c]
        if kind < 2:
            src, dst = half_of(piece(me.pd), kind), half_of(diags[k].at[j], kind)
        else:
            src, dst = (piece(me.px), from_x[k].at[j]) if kind == 2 else (piece(me.py), from_y[k].at[j])
        return copy_to(src, dst, send.at[i, kind], recv.at[i, kind], me.x_side() if kind % 2 == 0 else me.y_side())

    def line_push(k, j, slot):
        to = xor4(me.t, 1) if slot != 1 else head_of[j]
        return copy_to(grads[k].at[j, me.p, me.c], from_z[k].at[slot], line_send.at[k, j], line_recv.at[k, slot], me.line(to))

    def fourth(k, j):
        @pl.when(me.inner)
        def _():
            line_push(k, j, 2 + j).wait_recv()
            mine = grads[k].at[j, me.p, me.c]
            mine[...] = add_low(mine[...], from_z[k][2 + j])
            line_push(k, j, 1).start()

    def first(k, j):
        twin_push(k, j).wait_recv()
        copy = pltpu.make_async_copy(twins[k].at[j], stages[k], load.at[4])
        copy.start()
        copy.wait()
        for p in (me.pd, me.px, me.py, me.p):
            mine = grads[k].at[j, p, me.c]
            mine[...] = add_low(mine[...], stages[k][p])
            if p is me.pd:
                side(k, j, 0).start()
                side(k, j, 1).start()

    def second(k, j):
        for kind, p, to in ((1, me.px, 2), (0, me.py, 3)):
            side(k, j, kind).wait_recv()
            part, extra = half_of(grads[k].at[j, p, me.c], kind), half_of(diags[k].at[j], kind)
            part[...] = add_low(part[...], extra[...])
            side(k, j, to).start()

    def third(k, j):
        side(k, j, 2).wait_recv()
        side(k, j, 3).wait_recv()
        mine = grads[k].at[j, me.p, me.c]
        total = mine[...].astype(F32) + from_x[k][j].astype(F32) + from_y[k][j].astype(F32)
        if j < 3:
            mine[...] = total.astype(BF)
            if j == 2:
                line_push(k, j, 0).start()
            else:

                @pl.when(me.outer)
                def _():
                    line_push(k, j, 2 + j).start()
        else:
            (go_ref, gq_ref, gkv_ref)[k][...] = total

    def out_group(j):
        g = head_of[j]
        wo_load(j).wait()
        do = jnp.zeros((wo.shape[2], rows), F32)
        for d in range(8):
            part = slice(d * cols, (d + 1) * cols)
            do += dot_nt(wo[j % 2, d], dh_ref[:, part])
            grad_o[j, d // 2, d % 2] = dot_nn(o_ref[g], dh_ref[:, part]).astype(BF)
        twin_push(0, j).start()
        do_ref[j] = do.astype(BF)
        if j + 2 < 4:
            wo_load(j + 2).start()

    def dkv_push(j, m):
        z, s = xor4(me.t, m), head_of[j]
        src = dkv_out.at[j, pl.ds(pl.multiple_of(z * rows, rows), rows)]
        return copy_to(src, dkv_got.at[m - 1, s], dkv_send.at[m - 1, j], dkv_recv.at[m - 1, s], me.line(z))

    def back_group(j):
        g = head_of[j]
        kv = kv_ref[g]
        kt = kv.T[:HD]
        cos, sin = cos_ref[...], sin_ref[...]

        def head(h, _):
            part = pl.ds(pl.multiple_of(h * HD, HD), HD)
            q, do, o = q_ref[g, part], do_ref[j, part], o_ref[g, part]
            qz = jnp.concatenate([q, jnp.zeros_like(q)], 0)
            doz = jnp.concatenate([jnp.zeros_like(do), do], 0)
            delta = jnp.sum(do.astype(F32) * o.astype(F32), axis=0, keepdims=True)
            p = jnp.exp(dot_nn(kv, qz) + bias_ref[...] - lse_ref[g, pl.ds(h, 1)])
            ds = (p * (dot_nn(kv, doz) - delta)).astype(BF)
            acc_ref[...] += dot_nt(ds, qz) + dot_nt(p.astype(BF), doz)
            dqt_ref[part] = rope_back_t(dot_nn(kt, ds) * HD ** (-0.5), cos, sin).astype(BF)
            return 0

        acc_ref[...] = jnp.zeros_like(acc_ref)
        lax.fori_loop(0, RATIO, head, 0, unroll=2)
        dkv_out[j] = acc_ref[...].astype(BF)
        dkv_own[j] = acc_ref[pl.ds(pl.multiple_of(me.t * rows, rows), rows)]
        for m in (3, 2, 1):
            dkv_push(j, m).start()
        for d in range(8):
            grad_q[j, d // 2, d % 2] = dot_nt(a1t[d * cols : (d + 1) * cols], dqt_ref[...]).astype(BF)
        twin_push(1, j).start()
        wq_load(j).wait()
        part = dot_nt(dqt_ref[...].T, wq[...])
        if j == 0:
            da1_ref[...] = part
        else:
            da1_ref[...] += part
        if j < 3:
            wq_load(j + 1).start()

    def keys_back():
        wkv_load.wait()
        turned = []
        for j in range(4):
            total = dkv_own[j]
            for m in (3, 2, 1):
                dkv_push(j, m).wait_recv()
                total += dkv_got[m - 1, head_of[j]].astype(F32)
            total = total.T
            dkvt = jnp.concatenate([rope_back_t(total[:HD], cos_ref[...], sin_ref[...]), total[HD:]], 0)
            turned.append(dkvt.astype(BF))
            da1_ref[...] += dot_nt(dkvt.T.astype(BF), wkv[head_of[j], :, :cols].reshape(width, 2 * HD))
        gain1 = jnp.sum(da1_ref[...] * (x_ref[...].astype(F32) * r1_ref[...]), axis=0, keepdims=True)
        gain2 = gain2_ref[...]
        for j in range(4):
            for d in range(8):
                at = d * cols
                grad_kv[j, d // 2, d % 2, :cols] = dot_nt(a1t[at : at + cols], turned[j]).astype(BF)
                extra = [gain1[:, at : at + 128], gain1[:, at + 128 : at + 256], gain2[:, at : at + 128], gain2[:, at + 128 : at + 256], jnp.zeros((28, 128), F32)]
                grad_kv[j, d // 2, d % 2, cols:] = jnp.concatenate(extra, 0).astype(BF)
            twin_push(2, j).start()

    O, Q, KV = range(3)
    for j in range(4):
        out_group(j)
    for j in range(4):
        first(O, j)
    second(O, 0)
    second(O, 1)
    back_group(0)
    second(O, 2)
    second(O, 3)
    first(Q, 0)
    third(O, 0)
    back_group(1)
    third(O, 1)
    second(Q, 0)
    first(Q, 1)
    third(O, 2)
    fourth(O, 0)
    back_group(2)
    third(O, 3)
    second(Q, 1)
    first(Q, 2)
    third(Q, 0)
    fourth(O, 1)
    back_group(3)
    second(Q, 2)
    first(Q, 3)
    third(Q, 1)
    fourth(Q, 0)
    keys_back()
    second(Q, 3)
    third(Q, 2)
    fourth(Q, 1)
    for j in range(4):
        first(KV, j)
    third(Q, 3)
    for j in range(4):
        second(KV, j)
    for j in range(4):
        third(KV, j)
    for j in range(2):
        fourth(KV, j)
    for k in range(3):
        line_push(k, 2, 0).wait()
        line_push(k, 0, 1).wait()
        line_push(k, 1, 1).wait_send()
        total = (go_ref, gq_ref, gkv_ref)[k]
        total[...] += from_z[k][0].astype(F32) + from_z[k][1].astype(F32)
    mo_push.wait()
    for j in range(4):
        for m in (1, 2, 3):
            dkv_push(j, m).wait_send()
        for k in range(3):
            twin_push(k, j).wait_send()
            for kind in range(4):
                side(k, j, kind).wait_send()


def attn_back(wo, wq, wkv, mo, q, o, kv, lse, dh, a1, x, r1, gain2, cos, sin, first):
    rows, width = dh.shape
    groups, heads, _ = q.shape
    keys, cols = kv.shape[1], width // 8
    dma, vmem = pltpu.SemaphoreType.DMA, lambda *shape: pltpu.VMEM(shape, BF)
    low = lambda *dims: jax.ShapeDtypeStruct(dims, BF)
    full = lambda *dims: jax.ShapeDtypeStruct(dims, F32)
    inside = pl.BlockSpec(memory_space=pltpu.VMEM)
    pieces = ((heads, cols), (cols, heads), (cols + 32, 2 * HD))
    return pl.pallas_call(
        attn_back_kernel,
        out_shape=[full(rows, width)] + [full(*p) for p in pieces] + [low(rows, width)] + [low(4, 4, *p) for p in pieces],
        in_specs=[ANY] * 4 + [inside] * 12,
        out_specs=[inside] * 4 + [ANY] * 4,
        scratch_shapes=[vmem(4, 4, 2, *p) for p in pieces]
        + [vmem(4, *p) for _ in range(3) for p in pieces]
        + [vmem(4, *p) for p in pieces]
        + [vmem(4, *p) for p in pieces]
        + [
            vmem(2, 8, heads, cols), vmem(width, heads), vmem(4, 8, cols + 32, 2 * HD), vmem(width, rows), vmem(4, heads, rows),
            pltpu.VMEM((keys, rows), F32), pltpu.VMEM((keys, 2 * HD), F32), vmem(heads, rows),
            pltpu.VMEM((4, rows, 2 * HD), F32), vmem(4, keys, 2 * HD), vmem(3, 4, rows, 2 * HD),
            dma((5,)), dma((2,)), dma((3, 4)), dma((3, 4)), dma((12,)), dma((12,)), dma((12, 4)), dma((12, 4)), dma((3, 3)), dma((3, 4)),
        ],
        compiler_params=pltpu.CompilerParams(collective_id=3, has_side_effects=True, vmem_limit_bytes=63 * 2**20),
        name="attn_back",
    )(wo, wq, wkv, mo, q, o, kv, lse, dh, a1, x, r1, gain2, cos, sin, first)[:5]


def rope_tables(segments, rows, row0):
    own = lax.dynamic_slice_in_dim(segments, row0, rows)
    first = jnp.sum((segments[:, None] < own[None, :]).astype(jnp.int32), axis=0)
    index = jnp.arange(rows, dtype=jnp.int32) + row0
    freq = jnp.exp(jnp.arange(HD // 2, dtype=F32) * (-2.0 * math.log(10000.0) / HD))
    angle = freq[:, None] * (index - first).astype(F32)[None, :]
    cos, sin = jnp.cos(angle), jnp.sin(angle)
    return jnp.concatenate([cos, cos], 0), jnp.concatenate([sin, sin], 0), first[None, :]


def body(tokens, segments, attn_gain, w_query, w_key, w_value, w_out, mlp_gain, w_gate, w_up, w_down, cotangent):
    rows, width = tokens.shape
    cols, hidden = w_gate.shape
    t = lax.axis_index("tensor")
    cos, sin, first = rope_tables(segments, rows, t * rows)
    extra = jnp.concatenate([attn_gain.reshape(2, -1), mlp_gain.reshape(2, -1), jnp.zeros((28, 2 * HD), BF)], 0)
    w_kv = jnp.concatenate([jnp.concatenate([w_key, w_value], 1), extra], 0)
    h, a1, r1, r2, gains, q, o, lse, kv, wkv, wq, wo, wg, wu, wd, a2, ct = attn_gather(w_kv, w_query, w_out, w_gate, w_up, w_down, cotangent, tokens, cos, sin, first)
    wkv, wq, wo = wkv.reshape(4, 8, -1, 2 * HD), wq.reshape(4, width, -1), wo.reshape(8, 4, -1, cols)
    da2, mo, mo_near, gg, gu, gd = mlp(a2, ct, wg.reshape(width, -1), wu.reshape(width, -1), wd.reshape(8, hidden, -1))
    dres, gain2_part = rms_backward(h, r2, gains[1:2], da2)
    dh = cotangent.astype(F32) + dres
    da1, go, gq, gkv, mo_far = attn_back(wo, wq, wkv, mo, q, o, kv, lse, dh.astype(BF), a1, tokens, r1, gain2_part[None, :], cos, sin, first)
    mo_own = lax.dynamic_index_in_dim(mo, t, 0, keepdims=False)
    output = (h + mo_own.astype(F32) + mo_near[0].astype(F32) + mo_near[1].astype(F32) + mo_far.astype(F32)).astype(BF)
    din, _ = rms_backward(tokens.astype(F32), r1, gains[0:1], da1)
    grad_tokens = dh + din
    gain_grads = gkv[cols : cols + 4].reshape(2, -1)
    gkv = gkv[:cols]
    return (output, grad_tokens, gain_grads[0], gq, gkv[:, :HD], gkv[:, HD:], go, gain_grads[1], gg.astype(F32), gu.astype(F32), gd.astype(F32))


def body_plain(tokens, segments, attn_gain, w_query, w_key, w_value, w_out, mlp_gain, w_gate, w_up, w_down, cotangent):
    rows, width = tokens.shape
    hidden = w_gate.shape[1]
    nt = lax.axis_size("tensor")
    row0 = lax.axis_index("tensor") * rows
    cos, sin, first = rope_tables(segments, rows, row0)
    row0_s = row0[None].astype(jnp.int32)

    gain1 = lax.all_gather(attn_gain, "dp", axis=0, tiled=True).astype(F32)
    gain2 = lax.all_gather(mlp_gain, "dp", axis=0, tiled=True).astype(F32)
    w_kv = jnp.concatenate([w_key, w_value], 1)
    full = lambda w, axis: lax.all_gather(lax.all_gather(w, "dp", axis=axis, tiled=True), "tensor", axis=0)
    wq = full(w_query, 0)
    wkv = full(w_kv, 0)
    wo = full(w_out, 1).reshape(width, width)
    wg = lax.all_gather(w_gate, "dp", axis=0, tiled=True)
    wu = lax.all_gather(w_up, "dp", axis=0, tiled=True)
    wd = lax.all_gather(w_down, "dp", axis=1, tiled=True)

    x = tokens.astype(F32)
    n1, r1 = rms_forward(x, gain1)
    a1 = n1.astype(BF)
    kv = jnp.einsum("rd,gdc->grc", a1, wkv, preferred_element_type=F32)
    cos_r, sin_r = cos.T, sin.T
    k = kv[..., :HD]
    k = k * cos_r + jnp.concatenate([-k[..., HD // 2 :], k[..., : HD // 2]], -1) * sin_r
    kv = jnp.concatenate([k, kv[..., HD:]], -1).astype(BF)
    kv = lax.all_gather(kv, "tensor", axis=1, tiled=True)
    o, q, lse = attn_forward(row0_s, a1, wq, kv, cos, sin, first)
    o2 = o.reshape(-1, rows)
    h = x + dot_tn(o2, wo)

    n2, r2 = rms_forward(h, gain2)
    a2 = lax.all_gather(n2.astype(BF), "tensor", axis=0, tiled=True)
    cot = lax.all_gather(cotangent, "tensor", axis=0, tiled=True)
    output, da2, gg, gu, gd = mlp_plain(h, a2, cot, wg, wu, wd)
    dres, gain2_part = rms_backward(h, r2, gain2, da2)
    dh = cotangent.astype(F32) + dres
    dhb = dh.astype(BF)

    do = dot_nt(wo, dhb).astype(BF).reshape(o.shape)
    go_part = dot_nn(o2, dhb)
    dq, dkv = attn_backward(row0_s, q, kv, do, o, lse, cos, sin, first)
    groups = dkv.shape[0]
    dkv = lax.psum_scatter(dkv.astype(BF), "tensor", scatter_dimension=1, tiled=True).astype(F32)
    dk = dkv[..., :HD]
    ws = dk * sin_r
    dk = dk * cos_r + jnp.concatenate([ws[..., HD // 2 :], -ws[..., : HD // 2]], -1)
    dkv = jnp.concatenate([dk, dkv[..., HD:]], -1).astype(BF)
    gq_part = jnp.einsum("rd,gcr->gdc", a1, dq, preferred_element_type=F32)
    gkv_part = jnp.einsum("rd,grc->gdc", a1, dkv, preferred_element_type=F32)
    da1 = jnp.einsum("gcr,gdc->rd", dq, wq, preferred_element_type=F32) + jnp.einsum("grc,gdc->rd", dkv, wkv, preferred_element_type=F32)
    din, gain1_part = rms_backward(x, r1, gain1, da1)
    grad_tokens = dh + din

    def home_all(v, dim):
        return lax.psum_scatter(home(v, dim + 1), "tensor", scatter_dimension=0, tiled=False).astype(F32)

    gq = home_all(gq_part, 0)
    gkv = home_all(gkv_part, 0)
    go = home_all(go_part.reshape(nt, -1, width), 1)
    gains = lax.psum_scatter(jnp.stack([gain1_part, gain2_part]), "dp", scatter_dimension=1, tiled=True)
    gains = lax.psum(gains, "tensor")
    return (output, grad_tokens, gains[0], gq, gkv[:, :HD], gkv[:, HD:], go, gains[1], gg, gu, gd)


def solution(mesh):
    rows, block = P(("dp", "tensor"), None), P("dp", "tensor")
    turned, line = P("tensor", "dp"), P("dp")
    return jax.shard_map(
        body if (mesh.shape["dp"], mesh.shape["tensor"]) == (8, 4) else body_plain,
        mesh=mesh,
        in_specs=(rows, line, line, block, block, block, turned, line, block, block, turned, rows),
        out_specs=(rows, rows, line, block, block, block, turned, line, block, block, turned),
        check_vma=False,
    )
```

```python
import functools
import math

import jax
import jax.numpy as jnp
from jax import lax
from jax.experimental import pallas as pl
from jax.experimental.pallas import tpu as pltpu
from jax.sharding import PartitionSpec as P

HD = 64
RATIO = 8
EPSILON = 1e-05
MASKED = -1e30
BF = jnp.bfloat16
F32 = jnp.float32


def dot_nn(left, right):
    return lax.dot_general(left, right, (((1,), (0,)), ((), ())), preferred_element_type=F32)


def dot_nt(left, right):
    return lax.dot_general(left, right, (((1,), (1,)), ((), ())), preferred_element_type=F32)


def dot_tn(left, right):
    return lax.dot_general(left, right, (((0,), (0,)), ((), ())), preferred_element_type=F32)


def rms_forward(values_in, gain_row):
    factor = lax.rsqrt(jnp.mean(values_in * values_in, axis=-1, keepdims=True) + EPSILON)
    return (values_in * factor * gain_row, factor)


def rms_backward(values_in, factor, gain_row, gradient):
    scaled = gain_row * gradient
    grad_gain = jnp.sum(gradient * values_in * factor, axis=0)
    grad_input = factor * scaled - values_in * (factor * factor * factor) * jnp.mean(
        scaled * values_in, axis=-1, keepdims=True
    )
    return (grad_input, grad_gain)


def rope_t(u, cos, sin):
    half = HD // 2
    return u * cos + jnp.concatenate([-u[half:], u[:half]], 0) * sin


def rope_back_t(w, cos, sin):
    half = HD // 2
    ws = w * sin
    return w * cos + jnp.concatenate([ws[half:], -ws[:half]], 0)


def bias_of(first, row0, keys, rows):
    key = lax.broadcasted_iota(jnp.int32, (keys, rows), 0)
    row = lax.broadcasted_iota(jnp.int32, (keys, rows), 1) + row0
    return jnp.where((key <= row) & (key >= first), 0.0, MASKED).astype(F32)


def attn_forward_kernel(row0_ref, a1_ref, wq_ref, kv_ref, cos_ref, sin_ref, first_ref, o_ref, q_ref, lse_ref, bias_ref, s_ref, vt_ref):
    keys, rows = bias_ref.shape

    @pl.when(pl.program_id(0) == 0)
    def _():
        bias_ref[...] = bias_of(first_ref[...], row0_ref[0], keys, rows)

    kv = kv_ref[0]
    kvt = kv.T
    vt_ref[...] = jnp.concatenate([kvt[HD:], jnp.ones((16, keys), BF)], 0)
    qt = dot_nn(a1_ref[...], wq_ref[0]).T
    cos, sin = cos_ref[...], sin_ref[...]
    for h in range(RATIO):
        q = (rope_t(qt[h * HD : (h + 1) * HD], cos, sin) * HD ** (-0.5)).astype(BF)
        q_ref[0, h * HD : (h + 1) * HD] = q
        s_ref[...] = dot_nn(kv, jnp.concatenate([q, jnp.zeros_like(q)], 0)) + bias_ref[...]
        peak = jnp.max(s_ref[...], axis=0, keepdims=True)
        e = jnp.exp(s_ref[...] - peak).astype(BF)
        ot = dot_nn(vt_ref[...], e)
        total = ot[HD : HD + 1]
        o_ref[0, h * HD : (h + 1) * HD] = (ot[:HD] / total).astype(BF)
        lse_ref[0, h : h + 1] = peak + jnp.log(total)


def attn_backward_kernel(row0_ref, q_ref, kv_ref, do_ref, o_ref, lse_ref, cos_ref, sin_ref, first_ref, dq_ref, dkv_ref, bias_ref, acc_ref):
    keys, rows = bias_ref.shape

    @pl.when(pl.program_id(0) == 0)
    def _():
        bias_ref[...] = bias_of(first_ref[...], row0_ref[0], keys, rows)

    kv = kv_ref[0]
    kt = kv.T[:HD]
    cos, sin = cos_ref[...], sin_ref[...]
    for h in range(RATIO):
        part = slice(h * HD, (h + 1) * HD)
        q, do, o = q_ref[0, part], do_ref[0, part], o_ref[0, part]
        qz = jnp.concatenate([q, jnp.zeros_like(q)], 0)
        doz = jnp.concatenate([jnp.zeros_like(do), do], 0)
        delta = jnp.sum(do.astype(F32) * o.astype(F32), axis=0, keepdims=True)
        p = jnp.exp(dot_nn(kv, qz) + bias_ref[...] - lse_ref[0, h : h + 1])
        ds = (p * (dot_nn(kv, doz) - delta)).astype(BF)
        grad = dot_nt(ds, qz) + dot_nt(p.astype(BF), doz)
        if h == 0:
            acc_ref[...] = grad
        else:
            acc_ref[...] += grad
        dq = dot_nn(kt, ds) * HD ** (-0.5)
        dq_ref[0, part] = rope_back_t(dq, cos, sin).astype(BF)
    dkv_ref[0] = acc_ref[...]


def params():
    return pltpu.CompilerParams(vmem_limit_bytes=56 * 2**20)


def attn_forward(row0, a1, wq, kv, cos, sin, first):
    groups, width, cols = wq.shape
    rows, keys = a1.shape[0], kv.shape[1]
    whole = lambda *shape: pl.BlockSpec(shape, lambda i: (0,) * len(shape))
    part = lambda *shape: pl.BlockSpec((1,) + shape, lambda i: (i,) + (0,) * len(shape))
    return pl.pallas_call(
        attn_forward_kernel,
        grid=(groups,),
        in_specs=[pl.BlockSpec(memory_space=pltpu.SMEM), whole(rows, width), part(width, cols), part(keys, 2 * HD), whole(HD, rows), whole(HD, rows), whole(1, rows)],
        out_specs=[part(cols, rows), part(cols, rows), part(RATIO, rows)],
        out_shape=[jax.ShapeDtypeStruct((groups, cols, rows), BF), jax.ShapeDtypeStruct((groups, cols, rows), BF), jax.ShapeDtypeStruct((groups, RATIO, rows), F32)],
        scratch_shapes=[pltpu.VMEM((keys, rows), F32), pltpu.VMEM((keys, rows), F32), pltpu.VMEM((HD + 16, keys), BF)],
        compiler_params=params(),
        name="attn_forward",
    )(row0, a1, wq, kv, cos, sin, first)


def attn_backward(row0, q, kv, do, o, lse, cos, sin, first):
    groups, cols, rows = q.shape
    keys = kv.shape[1]
    whole = lambda *shape: pl.BlockSpec(shape, lambda i: (0,) * len(shape))
    part = lambda *shape: pl.BlockSpec((1,) + shape, lambda i: (i,) + (0,) * len(shape))
    return pl.pallas_call(
        attn_backward_kernel,
        grid=(groups,),
        in_specs=[pl.BlockSpec(memory_space=pltpu.SMEM), part(cols, rows), part(keys, 2 * HD), part(cols, rows), part(cols, rows), part(RATIO, rows), whole(HD, rows), whole(HD, rows), whole(1, rows)],
        out_specs=[part(cols, rows), part(keys, 2 * HD)],
        out_shape=[jax.ShapeDtypeStruct((groups, cols, rows), BF), jax.ShapeDtypeStruct((groups, keys, 2 * HD), F32)],
        scratch_shapes=[pltpu.VMEM((keys, rows), F32), pltpu.VMEM((keys, 2 * HD), F32)],
        compiler_params=params(),
        name="attn_backward",
    )(row0, q, kv, do, o, lse, cos, sin, first)


MESH = pl.DeviceIdType.MESH
ANY = pl.BlockSpec(memory_space=pl.ANY)


class Place:
    def __init__(self):
        d, self.t = lax.axis_index("dp"), lax.axis_index("tensor")
        self.c, self.p = d % 2, d // 2
        x, y = self.p % 2, self.p // 2
        self.px, self.py, self.pd = self.p + 1 - 2 * x, self.p + 2 - 4 * y, 3 - self.p
        self.across = [self.t + 1 - 2 * (self.t % 2), (self.t + 2) % 4, 3 - self.t]
        self.inner = (self.t == 1) | (self.t == 2)
        self.outer = (self.t == 0) | (self.t == 3)
        inner = self.t * (3 - self.t) // 2
        self.order = [self.t, self.across[0], 2 - self.t // 2, 3 - self.t // 2 * 3]
        self.away = [0, 1, 2 + inner, 3 - inner]

    def at(self, p, c, t):
        return {"dp": p * 2 + c, "tensor": t}

    def x_side(self):
        return self.at(self.px, self.c, self.t)

    def y_side(self):
        return self.at(self.py, self.c, self.t)

    def twin(self):
        return self.at(self.p, 1 - self.c, self.t)

    def line(self, t):
        return self.at(self.p, self.c, t)

    def greet(self):
        barrier = pltpu.get_barrier_semaphore()
        others = [self.x_side(), self.y_side(), self.twin()] + [self.line(t) for t in self.across]
        for other in others:
            pl.semaphore_signal(barrier, inc=1, device_id=other, device_id_type=MESH)
        pl.semaphore_wait(barrier, len(others))


def half_of(ref, part):
    rows = ref.shape[0] // 2
    return ref.at[pl.ds(part * rows, rows)]


def attn_gather_kernel(kv_in, wq_in, wo_in, wg_in, wu_in, wd_in, ct_in, x_ref, cos_ref, sin_ref, first_ref, h_ref, a1_ref, r1_ref, r2_ref, gains_ref, q_ref, o_ref, lse_ref, kv_ref, kv_out, q_out, o_out, g_out, u_out, d_out, a2_all, ct_all, wkv, wq, wo, rows_kv, bias_ref, s_ref, vt_ref, qt_ref, o_rows, a2_ref, z_send, z_recv, send, recv, local, load, kv_send, kv_recv, line_send, line_recv):
    me = Place()
    rows, width = x_ref.shape
    keys, cols = kv_ref.shape[1], width // 8
    me.greet()
    sources = [kv_in, wq_in, wo_in, wg_in, wu_in, wd_in]
    outs = [kv_out, q_out, o_out, g_out, u_out, d_out]

    def piece(k, s, p, c):
        if k == 2:
            return o_out.at[p, c, s]
        return outs[k].at[s, p, c] if k < 2 else outs[k].at[p, c]

    def pair(k, s, c):
        if k == 2:
            return o_out.at[:, c, s]
        if k == 0:
            return kv_out.at[:, :, c]
        return q_out.at[s, :, c] if k == 1 else outs[k].at[:, c]

    def line_push(k, m):
        return copy_to(sources[k], piece(k, me.t, me.p, me.c), z_send.at[k, m - 1], z_recv.at[k, m - 1], me.line(xor4(me.t, m)))

    def line_first(k):
        for m in (1, 2, 3):
            line_push(k, m).start()

    def arrive(k, j):
        line_push(k, me.away[j]).wait_recv()

    def push(k, j, kind):
        s, i = me.order[j], (0, 1 + j, 5 + j, 9, 10, 11)[k]
        part = (lambda p: kv_out.at[:, p, me.c]) if k == 0 else (lambda p: piece(k, s, p, me.c))
        if kind < 2:
            dst = part(me.p)
            src = sources[k] if j == 0 and k > 0 else dst
        elif kind < 4:
            src = dst = half_of(part(me.px if kind == 2 else me.py), kind - 2)
        else:
            src = dst = pair(k, s, me.c)
        to = [me.x_side, me.y_side, me.y_side, me.x_side, me.twin][kind]()
        return copy_to(src, dst, send.at[i, kind], recv.at[i, kind], to)

    def keep(k):
        return pltpu.make_async_copy(sources[k], piece(k, me.t, me.p, me.c), local.at[k])

    def first(k, j):
        if k == 0:
            keep(k).wait()
        elif j == 0:
            keep(k).start()
        push(k, j, 0).start()
        push(k, j, 1).start()

    def second(k, j):
        push(k, j, 0).wait_recv()
        push(k, j, 2).start()
        push(k, j, 1).wait_recv()
        push(k, j, 3).start()

    def third(k, j):
        push(k, j, 2).wait_recv()
        push(k, j, 3).wait_recv()
        if j == 0 and k > 0:
            keep(k).wait()
        push(k, j, 4).start()

    def last(k, j):
        push(k, j, 4).wait_recv()

    def step(n, k, action):
        t, out, own = me.t, (ct_all, a2_all)[n], (ct_in, a2_ref)[n]
        for way, chunk, can in ((0, t - k + 1, (t < 3) & (t - k + 1 >= 0)), (1, t + k - 1, (t > 0) & (t + k - 1 <= 3))):

            @pl.when(can)
            def _():
                src = own if k == 1 else out.at[chunk]
                copy = copy_to(src, out.at[chunk], line_send.at[n, way, k - 1], line_recv.at[n, way, k - 1], me.line(t + 1 - 2 * way))
                copy.start() if action == "start" else copy.wait_send()

    def got(n, k):
        t, out = me.t, (ct_all, a2_all)[n]
        for way, chunk, can in ((0, t - k, t - k >= 0), (1, t + k, t + k <= 3)):

            @pl.when(can)
            def _():
                copy_to(out.at[chunk], out.at[chunk], line_send.at[n, way, k - 1], line_recv.at[n, way, k - 1], me.line(t + 1 - 2 * way)).wait_recv()

    def own_rows(n):
        return pltpu.make_async_copy((ct_in, a2_ref)[n], (ct_all, a2_all)[n].at[me.t], local.at[6 + n])

    kv_load = pltpu.make_async_copy(kv_out, wkv, load.at[0])
    kv_keep = pltpu.make_async_copy(rows_kv, kv_ref, load.at[1])

    def wq_load(j):
        return pltpu.make_async_copy(q_out.at[me.order[j]], wq.at[j % 2], load.at[2 + j % 2])

    def wo_load(j):
        s = me.order[j]
        return pltpu.make_async_copy(o_out.at[:, :, s], wo.at[:, :, pl.ds(pl.multiple_of(s * 2 * cols, cols), 2 * cols)], load.at[4 + j])

    own = pl.ds(pl.multiple_of(me.t * rows, rows), rows)

    def kv_push(m, g):
        part = rows_kv.at[g, own]
        return copy_to(part, part, kv_send.at[m - 1, g], kv_recv.at[m - 1, g], me.line(xor4(me.t, m)))

    def gain(n):
        parts = [wkv[0, d // 2, d % 2, cols + 2 * n + e : cols + 2 * n + e + 1] for d in range(8) for e in range(2)]
        return jnp.concatenate(parts, 1).astype(F32)

    def norm(value):
        return lax.rsqrt(jnp.mean(value * value, axis=-1, keepdims=True) + EPSILON)

    def project_keys():
        x = x_ref[...].astype(F32)
        r1_ref[...] = norm(x)
        gains_ref[0:1] = gain(0)
        gains_ref[1:2] = gain(1)
        a1_ref[...] = (x * r1_ref[...] * gains_ref[0:1]).astype(BF)
        for m in (1, 2, 3, 0):
            g = xor4(me.t, m)
            weights = wkv[g, :, :, :cols].reshape(width, 2 * HD)
            kvt = dot_nn(a1_ref[...], weights).T
            kvt = jnp.concatenate([rope_t(kvt[:HD], cos_ref[...], sin_ref[...]), kvt[HD:]], 0).astype(BF)
            rows_kv[g, own] = kvt.T
            if m > 0:
                kv_push(m, g).start()
        for more in (1, 2, 3):
            for m in (1, 2, 3):
                kv_push(m, xor4(me.t, m ^ more)).start()

    def attend(j, part):
        g = me.order[j]
        if part == 0:
            for m in (1, 2, 3):
                kv_push(m, g).wait_recv()
            qt_ref[...] = dot_nn(a1_ref[...], wq[j % 2].reshape(width, -1)).T
            vt_ref[...] = jnp.concatenate([rows_kv[g].T[HD:], jnp.ones((16, keys), BF)], 0)
        cos, sin = cos_ref[...], sin_ref[...]

        def head(h, _):
            part = pl.ds(pl.multiple_of(h * HD, HD), HD)
            q = (rope_t(qt_ref[part], cos, sin) * HD ** (-0.5)).astype(BF)
            q_ref[g, part] = q
            s_ref[...] = dot_nn(rows_kv[g], jnp.concatenate([q, jnp.zeros_like(q)], 0)) + bias_ref[...]
            peak = jnp.max(s_ref[...], axis=0, keepdims=True)
            e = jnp.exp(s_ref[...] - peak).astype(BF)
            ot = dot_nn(vt_ref[...], e)
            total = ot[HD : HD + 1]
            o_ref[g, part] = (ot[:HD] / total).astype(BF)
            lse_ref[g, pl.ds(h, 1)] = peak + jnp.log(total)
            return 0

        lax.fori_loop(part * RATIO // 2, (part + 1) * RATIO // 2, head, 0, unroll=2)
        if part == 1:
            o_rows[:, pl.ds(pl.multiple_of(g * 2 * cols, cols), 2 * cols)] = o_ref[g].T

    def mix():
        for d in range(8):
            part = slice(d * cols, (d + 1) * cols)
            h_ref[:, part] = x_ref[:, part].astype(F32) + dot_nn(o_rows[...], wo[d // 2, d % 2])
        h = h_ref[...]
        r2_ref[...] = norm(h)
        a2_ref[...] = (h * r2_ref[...] * gains_ref[1:2]).astype(BF)

    KV, Q, O, G, U, D = range(6)
    keep(KV).start()
    line_first(KV)
    first(Q, 0)
    own_rows(0).start()
    arrive(KV, 1)
    line_first(Q)
    arrive(KV, 2)
    arrive(KV, 3)
    first(KV, 0)
    first(O, 0)
    bias_ref[...] = bias_of(first_ref[...], me.t * rows, keys, rows)
    second(KV, 0)
    second(Q, 0)
    third(KV, 0)
    arrive(Q, 1)
    first(Q, 1)
    last(KV, 0)
    kv_load.start()
    second(O, 0)
    kv_load.wait()
    project_keys()
    line_first(O)
    arrive(Q, 2)
    first(Q, 2)
    third(Q, 0)
    second(Q, 1)
    arrive(Q, 3)
    first(Q, 3)
    last(Q, 0)
    wq_load(0).start()
    third(Q, 1)
    third(O, 0)
    second(Q, 2)
    arrive(O, 1)
    step(0, 1, "start")
    first(O, 1)
    wq_load(0).wait()
    attend(0, 0)
    third(Q, 2)
    last(Q, 1)
    wq_load(1).start()
    second(Q, 3)
    arrive(O, 2)
    first(O, 2)
    attend(0, 1)
    third(Q, 3)
    second(O, 1)
    arrive(O, 3)
    first(O, 3)
    wq_load(1).wait()
    attend(1, 0)
    last(Q, 2)
    wq_load(2).start()
    third(O, 1)
    second(O, 2)
    got(0, 1)
    step(0, 2, "start")
    attend(1, 1)
    last(Q, 3)
    wq_load(3).start()
    second(O, 3)
    first(G, 0)
    third(O, 2)
    wq_load(2).wait()
    attend(2, 0)
    third(O, 3)
    last(O, 0)
    wo_load(0).start()
    last(O, 1)
    wo_load(1).start()
    attend(2, 1)
    last(O, 2)
    wo_load(2).start()
    last(O, 3)
    wo_load(3).start()
    first(U, 0)
    wq_load(3).wait()
    attend(3, 0)
    got(0, 2)
    step(0, 3, "start")
    attend(3, 1)
    for j in range(4):
        wo_load(j).wait()
    mix()
    own_rows(1).start()
    step(1, 1, "start")
    kv_keep.start()
    second(G, 0)
    first(D, 0)
    third(G, 0)
    second(U, 0)
    got(1, 1)
    step(1, 2, "start")
    third(U, 0)
    second(D, 0)
    third(D, 0)
    for k in (G, U, D):
        last(k, 0)
    got(0, 3)
    got(1, 2)
    kv_keep.wait()
    for n in range(2):
        own_rows(n).wait()
        for k in (1, 2, 3)[: 3 - n]:
            step(n, k, "wait")
    for j in (1, 2, 3):
        for g in range(4):
            kv_push(j, g).wait_send()
        for k in (KV, Q, O):
            line_push(k, j).wait_send()
    for k in range(6):
        for j in range(4 if k in (Q, O) else 1):
            for kind in range(5):
                push(k, j, kind).wait_send()


def attn_gather(kv, wq, wo, wg, wu, wd, ct, x, cos, sin, first):
    rows, width = x.shape
    heads, cols, keys = wq.shape[1], wq.shape[0], 4 * rows
    dma, vmem = pltpu.SemaphoreType.DMA, lambda *shape: pltpu.VMEM(shape, BF)
    low = lambda *dims: jax.ShapeDtypeStruct(dims, BF)
    full = lambda *dims: jax.ShapeDtypeStruct(dims, F32)
    inside = pl.BlockSpec(memory_space=pltpu.VMEM)
    return pl.pallas_call(
        attn_gather_kernel,
        out_shape=[
            full(rows, width), low(rows, width), full(rows, 1), full(rows, 1), full(2, width), low(4, heads, rows), low(4, heads, rows), full(4, RATIO, rows),
            low(4, keys, 2 * HD), low(4, 4, 2, *kv.shape), low(4, 4, 2, *wq.shape), low(4, 2, 4, *wo.shape),
            low(4, 2, *wg.shape), low(4, 2, *wu.shape), low(4, 2, *wd.shape), low(4, rows, width), low(4, rows, width),
        ],
        in_specs=[ANY] * 7 + [inside] * 4,
        out_specs=[inside] * 8 + [ANY] * 9,
        scratch_shapes=[
            vmem(4, 4, 2, *kv.shape), vmem(2, 4, 2, cols, heads), vmem(4, 2, width, cols), vmem(4, keys, 2 * HD),
            pltpu.VMEM((keys, rows), F32), pltpu.VMEM((keys, rows), F32), vmem(HD + 16, keys), pltpu.VMEM((heads, rows), F32), vmem(rows, width), vmem(rows, width),
            dma((3, 3)), dma((3, 3)), dma((12, 5)), dma((12, 5)), dma((8,)), dma((8,)), dma((3, 4)), dma((3, 4)), dma((2, 2, 3)), dma((2, 2, 3)),
        ],
        compiler_params=pltpu.CompilerParams(collective_id=1, has_side_effects=True, vmem_limit_bytes=56 * 2**20),
        name="attn_gather",
    )(kv, wq, wo, wg, wu, wd, ct, x, cos, sin, first)


def xor4(a, m):
    return (a // 2 + m // 2) % 2 * 2 + (a % 2 + m % 2) % 2


def copy_to(src, dst, send_sem, recv_sem, to):
    return pltpu.make_async_remote_copy(src, dst, send_sem, recv_sem, device_id=to, device_id_type=MESH)


def add_low(left, right):
    return (left.astype(F32) + right.astype(F32)).astype(BF)


def mlp_kernel(a2_old, ct_in, wg_in, wu_in, wd_in, a2_in, da2_out, mo_out, mo_got, gg_out, gu_out, gd_out, twin_g, twin_u, twin_d, wg, wu, wd, a2_buf, ct_buf, mo_buf, a2_col, ct_col, zt, dg, du, out_buf, in_buf, diag_gu, x_gu, y_gu, diag_d, x_d, y_d, stage_gu, stage_d, load, store, line_send, line_recv, a2_send, a2_recv, mo_send, mo_recv, twin_send, twin_recv, send, recv, stage_sem):
    me = Place()
    rows, width = da2_out.shape
    hidden = wg.shape[1]
    cols = width // 8
    weights = [pltpu.make_async_copy(wg_in, wg, load.at[4]), pltpu.make_async_copy(wu_in, wu, load.at[5])]
    weights += [pltpu.make_async_copy(wd_in.at[d], wd.at[:, pl.ds(d * cols, cols)], load.at[6 + d]) for d in range(8)]
    for copy in weights:
        copy.start()

    def away(j):
        return 2 * (1 - j % 2) + (j % 2 + j // 2) % 2

    a2_push = copy_to(a2_in.at[xor4(me.t, 2)], a2_in.at[xor4(me.t, 2)], a2_send.at[0], a2_recv.at[0], me.line(xor4(me.t, 1)))

    def chunk_load(j, slot):
        s = xor4(me.t, away(j))
        return pltpu.make_async_copy(a2_in.at[s], a2_buf.at[slot], load.at[slot]), pltpu.make_async_copy(ct_in.at[s], ct_buf.at[slot], load.at[2 + slot])

    near, cross, both = in_buf.at[0], in_buf.at[1], in_buf.at[pl.ds(2, 2)]

    def near_send():
        return copy_to(out_buf.at[0], near, line_send.at[0], line_recv.at[0], me.line(xor4(me.t, 1)))

    def both_send(m):
        s = xor4(me.t, m)
        return copy_to(out_buf.at[m - 1], both.at[s % 2], line_send.at[m - 1], line_recv.at[2 + s % 2], me.line(xor4(me.t, 1)))

    def cross_send(m):
        return copy_to(out_buf.at[m - 1], cross, line_send.at[m - 1], line_recv.at[1], me.line(xor4(me.t, m)))

    def cross_add(m):
        s = xor4(me.t, m)
        copy_to(both.at[s % 2], both.at[s % 2], line_send.at[0], line_recv.at[2 + s % 2], me.line(xor4(me.t, 1))).wait_recv()
        out_buf[m - 1] = add_low(out_buf[m - 1], both[s % 2])
        cross_send(m).start()

    def mo_store(j, slot):
        return pltpu.make_async_copy(mo_buf.at[slot], mo_out.at[xor4(me.t, away(j))], store.at[slot])

    for copy in chunk_load(0, 0):
        copy.start()
    me.greet()

    @pl.when(me.inner)
    def _():
        a2_push.start()

    def chunk(j, _):
        slot = j % 2

        for copy in chunk_load(j, slot):
            copy.wait()
        where = pl.multiple_of(xor4(me.t, away(j)) * rows, rows)

        @pl.when(j == 0)
        def _():
            weights[0].wait()

        g = dot_nn(a2_buf[slot], wg[...])

        @pl.when(j == 0)
        def _():
            for copy in weights[1:]:
                copy.wait()

        u = dot_nn(a2_buf[slot], wu[...])
        dz = dot_nt(ct_buf[slot], wd[...])
        sig = 1.0 / (1.0 + jnp.exp(-g))
        act = g * sig
        z = (act * u).astype(BF)
        zt[:, pl.ds(where, rows)] = z.T
        dg_now = (dz * u * (sig * (1.0 + g * (1.0 - sig)))).astype(BF)
        du_now = (dz * act).astype(BF)
        dg[pl.ds(where, rows)] = dg_now
        du[pl.ds(where, rows)] = du_now
        part = dot_nt(dg_now, wg[...]) + dot_nt(du_now, wu[...])

        @pl.when(j < 3)
        def _():
            out_buf[away(j) - 1] = part.astype(BF)

        @pl.when((j == 1) & me.inner)
        def _():
            near_send().start()

        for at, m in ((0, 2), (2, 3)):

            @pl.when((j == at) & me.outer)
            def _():
                both_send(m).start()

        @pl.when(j == 3)
        def _():
            da2_out[...] = part

        @pl.when((j == 1) & me.outer)
        def _():
            a2_push.wait_recv()

        @pl.when(j < 3)
        def _():
            for copy in chunk_load(j + 1, 1 - slot):
                copy.start()

        @pl.when(j >= 2)
        def _():
            mo_store(j - 2, slot).wait()

        mo_buf[slot] = dot_nn(z, wd[...]).astype(BF)
        mo_store(j, slot).start()
        return 0

    lax.fori_loop(0, 4, chunk, 0)
    mo_store(2, 0).wait()
    mo_store(3, 1).wait()

    def mo_push(m):
        return copy_to(mo_out.at[xor4(me.t, m)], mo_got.at[m - 1], mo_send.at[m - 1], mo_recv.at[m - 1], me.line(xor4(me.t, m)))

    @pl.when(me.inner)
    def _():
        cross_add(3)

    def owner(i):
        return xor4(me.p, 3 - i % 4) * 2 + (1 - me.c + i // 4) % 2

    def tile_load(i, slot):
        at = pl.ds(pl.multiple_of(owner(i) * cols, cols), cols)
        return pltpu.make_async_copy(a2_in.at[:, :, at], a2_col.at[slot], load.at[slot]), pltpu.make_async_copy(ct_in.at[:, :, at], ct_col.at[slot], load.at[2 + slot])

    def piece(k, p, c):
        at = pl.ds(pl.multiple_of((p * 2 + c) * cols, cols), cols)
        return (wg, wu)[k].at[at] if k < 2 else wd.at[:, at]

    twins = [twin_g, twin_u, twin_d]

    def twin_push(k, i):
        p = xor4(me.p, 3 - i)
        return copy_to(piece(k, p, 1 - me.c), twins[k].at[p], twin_send.at[k, i], twin_recv.at[k, i], me.twin())

    diag = [diag_gu.at[0], diag_gu.at[1], diag_d]
    from_x = [x_gu.at[0], x_gu.at[1], x_d]
    from_y = [y_gu.at[0], y_gu.at[1], y_d]
    stage = [stage_gu.at[0], stage_gu.at[1], stage_d]

    def side(k, kind):
        if kind < 2:
            src, dst = half_of(piece(k, me.pd, me.c), kind), half_of(diag[k], kind)
        else:
            src, dst = (piece(k, me.px, me.c), from_x[k]) if kind == 2 else (piece(k, me.py, me.c), from_y[k])
        return copy_to(src, dst, send.at[k, kind], recv.at[k, kind], me.x_side() if kind % 2 == 0 else me.y_side())

    def fetch(k, p):
        return pltpu.make_async_copy(twins[k].at[p], stage[k], stage_sem.at[k])

    for copy in tile_load(0, 0):
        copy.start()

    def tile(i, _):
        slot = i % 2

        @pl.when(i < 7)
        def _():
            for copy in tile_load(i + 1, 1 - slot):
                copy.start()

        for copy in tile_load(i, slot):
            copy.wait()
        at = pl.ds(pl.multiple_of(owner(i) * cols, cols), cols)
        a2t = a2_col[slot].reshape(4 * rows, cols).T
        wg[at] = dot_nn(a2t, dg[...]).astype(BF)
        wu[at] = dot_nn(a2t, du[...]).astype(BF)
        wd[:, at] = dot_nn(zt[...], ct_col[slot].reshape(4 * rows, cols)).astype(BF)

        @pl.when(i < 4)
        def _():
            for k in range(3):
                twin_push(k, i).start()

        @pl.when(i >= 4)
        def _():
            p = xor4(me.p, 7 - i)
            for k in range(3):
                twin_push(k, i - 4).wait_recv()
                fetch(k, p).start()
            for k in range(3):
                fetch(k, p).wait()
                mine = piece(k, p, me.c)
                mine[...] = add_low(mine[...], stage[k][...])

        @pl.when(i == 4)
        def _():
            for k in range(3):
                side(k, 0).start()
                side(k, 1).start()

        @pl.when((i == 5) & me.inner)
        def _():
            cross_add(2)

        @pl.when((i == 5) & me.outer)
        def _():
            near_send().start()

        @pl.when(i == 5)
        def _():
            for m in (1, 2):
                mo_push(m).start()

        return 0

    lax.fori_loop(0, 8, tile, 0)
    for k in range(3):
        side(k, 1).wait_recv()
        part, extra = half_of(piece(k, me.px, me.c), 1), half_of(diag[k], 1)
        part[...] = add_low(part[...], extra[...])
        side(k, 2).start()
        side(k, 0).wait_recv()
        part, extra = half_of(piece(k, me.py, me.c), 0), half_of(diag[k], 0)
        part[...] = add_low(part[...], extra[...])
        side(k, 3).start()
    results = []
    for k in range(3):
        side(k, 2).wait_recv()
        side(k, 3).wait_recv()
        mine = piece(k, me.p, me.c)
        mine[...] = (mine[...].astype(F32) + from_x[k][...].astype(F32) + from_y[k][...].astype(F32)).astype(BF)
        results.append(pltpu.make_async_copy(mine, (gg_out, gu_out, gd_out)[k], stage_sem.at[k]))
        results[-1].start()
    near_send().wait_recv()
    cross_send(2).wait_recv()
    da2_out[...] += in_buf[0].astype(F32) + in_buf[1].astype(F32)
    for copy in results:
        copy.wait()
    for m in (1, 2):
        mo_push(m).wait()

    @pl.when(me.inner)
    def _():
        a2_push.wait_send()

    near_send().wait_send()
    for m in (2, 3):
        cross_send(m).wait_send()
    for k in range(3):
        for i in range(4):
            twin_push(k, i).wait_send()
            side(k, i).wait_send()


def mlp(a2, ct, wg, wu, wd):
    chunks, rows, width = a2.shape
    hidden, cols = wg.shape[1], width // 8
    dma, vmem = pltpu.SemaphoreType.DMA, lambda *shape: pltpu.VMEM(shape, BF)
    shape = lambda *dims: jax.ShapeDtypeStruct(dims, BF)
    return pl.pallas_call(
        mlp_kernel,
        out_shape=[shape(4, rows, width), jax.ShapeDtypeStruct((rows, width), F32), shape(4, rows, width), shape(2, rows, width), shape(cols, hidden), shape(cols, hidden), shape(hidden, cols), shape(4, cols, hidden), shape(4, cols, hidden), shape(4, hidden, cols)],
        in_specs=[ANY] * 5,
        out_specs=[ANY, pl.BlockSpec(memory_space=pltpu.VMEM)] + [ANY] * 8,
        input_output_aliases={0: 0},
        scratch_shapes=[
            vmem(width, hidden), vmem(width, hidden), vmem(hidden, width),
            vmem(2, rows, width), vmem(2, rows, width), vmem(2, rows, width),
            vmem(2, 4, rows, cols), vmem(2, 4, rows, cols),
            vmem(hidden, 4 * rows), vmem(4 * rows, hidden), vmem(4 * rows, hidden),
            vmem(3, rows, width), vmem(4, rows, width),
            vmem(2, cols, hidden), vmem(2, cols, hidden), vmem(2, cols, hidden),
            vmem(hidden, cols), vmem(hidden, cols), vmem(hidden, cols),
            vmem(2, cols, hidden), vmem(hidden, cols),
            dma((14,)), dma((2,)), dma((3,)), dma((4,)), dma((1,)), dma((1,)), dma((2,)), dma((2,)), dma((3, 4)), dma((3, 4)), dma((3, 4)), dma((3, 4)), dma((3,)),
        ],
        compiler_params=pltpu.CompilerParams(collective_id=2, has_side_effects=True, vmem_limit_bytes=62 * 2**20),
        name="mlp",
    )(a2, ct, wg, wu, wd)[1:7]


def home(v, dim):
    return lax.psum_scatter(v.astype(BF), "dp", scatter_dimension=dim, tiled=True)


def mlp_plain(h, a2, cot, wg, wu, wd):
    g, u = dot_nn(a2, wg), dot_nn(a2, wu)
    sig = jax.nn.sigmoid(g)
    act = g * sig
    z = (act * u).astype(BF)
    scatter = lambda v: lax.psum_scatter(v.astype(BF), "tensor", scatter_dimension=0, tiled=True).astype(F32)
    output = (h + scatter(dot_nn(z, wd))).astype(BF)
    dz = dot_nt(cot, wd)
    dg = (dz * u * (sig * (1.0 + g * (1.0 - sig)))).astype(BF)
    du = (dz * act).astype(BF)
    gd = home(dot_tn(z, cot), 1).astype(F32)
    gg = home(dot_tn(a2, dg), 0).astype(F32)
    gu = home(dot_tn(a2, du), 0).astype(F32)
    da2 = scatter(dot_nt(dg, wg) + dot_nt(du, wu))
    return output, da2, gg, gu, gd


def attn_back_kernel(wo_in, wq_in, wkv_in, mo_in, q_ref, o_ref, kv_ref, lse_ref, dh_ref, a1_ref, x_ref, r1_ref, gain2_ref, cos_ref, sin_ref, first_ref, da1_ref, go_ref, gq_ref, gkv_ref, mo_got, twin_o, twin_q, twin_kv, grad_o, grad_q, grad_kv, diag_o, diag_q, diag_kv, x_o, x_q, x_kv, y_o, y_q, y_kv, z_o, z_q, z_kv, stage_o, stage_q, stage_kv, wo, wq, wkv, a1t, do_ref, bias_ref, acc_ref, dqt_ref, dkv_own, dkv_out, dkv_got, load, mo_sem, dkv_send, dkv_recv, twin_send, twin_recv, send, recv, line_send, line_recv):
    me = Place()
    rows, width = dh_ref.shape
    keys, cols = kv_ref.shape[1], width // 8
    head_of = [3 - me.t // 2 * 3, 2 - me.t // 2, xor4(me.t, 1), me.t]

    def wo_load(j):
        return pltpu.make_async_copy(wo_in.at[:, head_of[j]], wo.at[j % 2], load.at[j % 2])

    def wq_load(j):
        return pltpu.make_async_copy(wq_in.at[head_of[j]], wq, load.at[2])

    wkv_load = pltpu.make_async_copy(wkv_in, wkv, load.at[3])
    mo_push = copy_to(mo_in.at[xor4(me.t, 3)], mo_got, mo_sem.at[0], mo_sem.at[1], me.line(xor4(me.t, 3)))
    wo_load(0).start()
    wo_load(1).start()
    wq_load(0).start()
    wkv_load.start()
    me.greet()
    mo_push.start()
    a1t[...] = a1_ref[...].T
    bias_ref[...] = bias_of(first_ref[...], me.t * rows, keys, rows)

    grads, twins, diags = [grad_o, grad_q, grad_kv], [twin_o, twin_q, twin_kv], [diag_o, diag_q, diag_kv]
    from_x, from_y, from_z = [x_o, x_q, x_kv], [y_o, y_q, y_kv], [z_o, z_q, z_kv]
    stages = [stage_o, stage_q, stage_kv]

    def twin_push(k, j):
        i = k * 4 + j
        return copy_to(grads[k].at[j, :, 1 - me.c], twins[k].at[j], twin_send.at[i], twin_recv.at[i], me.twin())

    def side(k, j, kind):
        i = k * 4 + j
        piece = lambda p: grads[k].at[j, p, me.c]
        if kind < 2:
            src, dst = half_of(piece(me.pd), kind), half_of(diags[k].at[j], kind)
        else:
            src, dst = (piece(me.px), from_x[k].at[j]) if kind == 2 else (piece(me.py), from_y[k].at[j])
        return copy_to(src, dst, send.at[i, kind], recv.at[i, kind], me.x_side() if kind % 2 == 0 else me.y_side())

    def line_push(k, j, slot):
        to = xor4(me.t, 1) if slot != 1 else head_of[j]
        return copy_to(grads[k].at[j, me.p, me.c], from_z[k].at[slot], line_send.at[k, j], line_recv.at[k, slot], me.line(to))

    def fourth(k, j):
        @pl.when(me.inner)
        def _():
            line_push(k, j, 2 + j).wait_recv()
            mine = grads[k].at[j, me.p, me.c]
            mine[...] = add_low(mine[...], from_z[k][2 + j])
            line_push(k, j, 1).start()

    def first(k, j):
        twin_push(k, j).wait_recv()
        copy = pltpu.make_async_copy(twins[k].at[j], stages[k], load.at[4])
        copy.start()
        copy.wait()
        for p in (me.pd, me.px, me.py, me.p):
            mine = grads[k].at[j, p, me.c]
            mine[...] = add_low(mine[...], stages[k][p])
            if p is me.pd:
                side(k, j, 0).start()
                side(k, j, 1).start()

    def second(k, j):
        for kind, p, to in ((1, me.px, 2), (0, me.py, 3)):
            side(k, j, kind).wait_recv()
            part, extra = half_of(grads[k].at[j, p, me.c], kind), half_of(diags[k].at[j], kind)
            part[...] = add_low(part[...], extra[...])
            side(k, j, to).start()

    def third(k, j):
        side(k, j, 2).wait_recv()
        side(k, j, 3).wait_recv()
        mine = grads[k].at[j, me.p, me.c]
        total = mine[...].astype(F32) + from_x[k][j].astype(F32) + from_y[k][j].astype(F32)
        if j < 3:
            mine[...] = total.astype(BF)
            if j == 2:
                line_push(k, j, 0).start()
            else:

                @pl.when(me.outer)
                def _():
                    line_push(k, j, 2 + j).start()
        else:
            (go_ref, gq_ref, gkv_ref)[k][...] = total

    def out_group(j):
        g = head_of[j]
        wo_load(j).wait()
        do = jnp.zeros((wo.shape[2], rows), F32)
        for d in range(8):
            part = slice(d * cols, (d + 1) * cols)
            do += dot_nt(wo[j % 2, d], dh_ref[:, part])
            grad_o[j, d // 2, d % 2] = dot_nn(o_ref[g], dh_ref[:, part]).astype(BF)
        twin_push(0, j).start()
        do_ref[j] = do.astype(BF)
        if j + 2 < 4:
            wo_load(j + 2).start()

    def dkv_push(j, m):
        z, s = xor4(me.t, m), head_of[j]
        src = dkv_out.at[j, pl.ds(pl.multiple_of(z * rows, rows), rows)]
        return copy_to(src, dkv_got.at[m - 1, s], dkv_send.at[m - 1, j], dkv_recv.at[m - 1, s], me.line(z))

    def back_group(j):
        g = head_of[j]
        kv = kv_ref[g]
        kt = kv.T[:HD]
        cos, sin = cos_ref[...], sin_ref[...]

        def head(h, _):
            part = pl.ds(pl.multiple_of(h * HD, HD), HD)
            q, do, o = q_ref[g, part], do_ref[j, part], o_ref[g, part]
            qz = jnp.concatenate([q, jnp.zeros_like(q)], 0)
            doz = jnp.concatenate([jnp.zeros_like(do), do], 0)
            delta = jnp.sum(do.astype(F32) * o.astype(F32), axis=0, keepdims=True)
            p = jnp.exp(dot_nn(kv, qz) + bias_ref[...] - lse_ref[g, pl.ds(h, 1)])
            ds = (p * (dot_nn(kv, doz) - delta)).astype(BF)
            acc_ref[...] += dot_nt(ds, qz) + dot_nt(p.astype(BF), doz)
            dqt_ref[part] = rope_back_t(dot_nn(kt, ds) * HD ** (-0.5), cos, sin).astype(BF)
            return 0

        acc_ref[...] = jnp.zeros_like(acc_ref)
        lax.fori_loop(0, RATIO, head, 0, unroll=2)
        dkv_out[j] = acc_ref[...].astype(BF)
        dkv_own[j] = acc_ref[pl.ds(pl.multiple_of(me.t * rows, rows), rows)]
        for m in (3, 2, 1):
            dkv_push(j, m).start()
        for d in range(8):
            grad_q[j, d // 2, d % 2] = dot_nt(a1t[d * cols : (d + 1) * cols], dqt_ref[...]).astype(BF)
        twin_push(1, j).start()
        wq_load(j).wait()
        part = dot_nt(dqt_ref[...].T, wq[...])
        if j == 0:
            da1_ref[...] = part
        else:
            da1_ref[...] += part
        if j < 3:
            wq_load(j + 1).start()

    def keys_back():
        wkv_load.wait()
        turned = []
        for j in range(4):
            total = dkv_own[j]
            for m in (3, 2, 1):
                dkv_push(j, m).wait_recv()
                total += dkv_got[m - 1, head_of[j]].astype(F32)
            total = total.T
            dkvt = jnp.concatenate([rope_back_t(total[:HD], cos_ref[...], sin_ref[...]), total[HD:]], 0)
            turned.append(dkvt.astype(BF))
            da1_ref[...] += dot_nt(dkvt.T.astype(BF), wkv[head_of[j], :, :cols].reshape(width, 2 * HD))
        gain1 = jnp.sum(da1_ref[...] * (x_ref[...].astype(F32) * r1_ref[...]), axis=0, keepdims=True)
        gain2 = gain2_ref[...]
        for j in range(4):
            for d in range(8):
                at = d * cols
                grad_kv[j, d // 2, d % 2, :cols] = dot_nt(a1t[at : at + cols], turned[j]).astype(BF)
                extra = [gain1[:, at : at + 128], gain1[:, at + 128 : at + 256], gain2[:, at : at + 128], gain2[:, at + 128 : at + 256], jnp.zeros((28, 128), F32)]
                grad_kv[j, d // 2, d % 2, cols:] = jnp.concatenate(extra, 0).astype(BF)
            twin_push(2, j).start()

    O, Q, KV = range(3)
    for j in range(4):
        out_group(j)
    for j in range(4):
        first(O, j)
    second(O, 0)
    second(O, 1)
    back_group(0)
    second(O, 2)
    second(O, 3)
    first(Q, 0)
    third(O, 0)
    back_group(1)
    third(O, 1)
    second(Q, 0)
    first(Q, 1)
    third(O, 2)
    fourth(O, 0)
    back_group(2)
    third(O, 3)
    second(Q, 1)
    first(Q, 2)
    third(Q, 0)
    fourth(O, 1)
    back_group(3)
    second(Q, 2)
    first(Q, 3)
    third(Q, 1)
    fourth(Q, 0)
    keys_back()
    second(Q, 3)
    third(Q, 2)
    fourth(Q, 1)
    for j in range(4):
        first(KV, j)
    third(Q, 3)
    for j in range(4):
        second(KV, j)
    for j in range(4):
        third(KV, j)
    for j in range(2):
        fourth(KV, j)
    for k in range(3):
        line_push(k, 2, 0).wait()
        line_push(k, 0, 1).wait()
        line_push(k, 1, 1).wait_send()
        total = (go_ref, gq_ref, gkv_ref)[k]
        total[...] += from_z[k][0].astype(F32) + from_z[k][1].astype(F32)
    mo_push.wait()
    for j in range(4):
        for m in (1, 2, 3):
            dkv_push(j, m).wait_send()
        for k in range(3):
            twin_push(k, j).wait_send()
            for kind in range(4):
                side(k, j, kind).wait_send()


def attn_back(wo, wq, wkv, mo, q, o, kv, lse, dh, a1, x, r1, gain2, cos, sin, first):
    rows, width = dh.shape
    groups, heads, _ = q.shape
    keys, cols = kv.shape[1], width // 8
    dma, vmem = pltpu.SemaphoreType.DMA, lambda *shape: pltpu.VMEM(shape, BF)
    low = lambda *dims: jax.ShapeDtypeStruct(dims, BF)
    full = lambda *dims: jax.ShapeDtypeStruct(dims, F32)
    inside = pl.BlockSpec(memory_space=pltpu.VMEM)
    pieces = ((heads, cols), (cols, heads), (cols + 32, 2 * HD))
    return pl.pallas_call(
        attn_back_kernel,
        out_shape=[full(rows, width)] + [full(*p) for p in pieces] + [low(rows, width)] + [low(4, 4, *p) for p in pieces],
        in_specs=[ANY] * 4 + [inside] * 12,
        out_specs=[inside] * 4 + [ANY] * 4,
        scratch_shapes=[vmem(4, 4, 2, *p) for p in pieces]
        + [vmem(4, *p) for _ in range(3) for p in pieces]
        + [vmem(4, *p) for p in pieces]
        + [vmem(4, *p) for p in pieces]
        + [
            vmem(2, 8, heads, cols), vmem(width, heads), vmem(4, 8, cols + 32, 2 * HD), vmem(width, rows), vmem(4, heads, rows),
            pltpu.VMEM((keys, rows), F32), pltpu.VMEM((keys, 2 * HD), F32), vmem(heads, rows),
            pltpu.VMEM((4, rows, 2 * HD), F32), vmem(4, keys, 2 * HD), vmem(3, 4, rows, 2 * HD),
            dma((5,)), dma((2,)), dma((3, 4)), dma((3, 4)), dma((12,)), dma((12,)), dma((12, 4)), dma((12, 4)), dma((3, 3)), dma((3, 4)),
        ],
        compiler_params=pltpu.CompilerParams(collective_id=3, has_side_effects=True, vmem_limit_bytes=63 * 2**20),
        name="attn_back",
    )(wo, wq, wkv, mo, q, o, kv, lse, dh, a1, x, r1, gain2, cos, sin, first)[:5]


def rope_tables(segments, rows, row0):
    own = lax.dynamic_slice_in_dim(segments, row0, rows)
    first = jnp.sum((segments[:, None] < own[None, :]).astype(jnp.int32), axis=0)
    index = jnp.arange(rows, dtype=jnp.int32) + row0
    freq = jnp.exp(jnp.arange(HD // 2, dtype=F32) * (-2.0 * math.log(10000.0) / HD))
    angle = freq[:, None] * (index - first).astype(F32)[None, :]
    cos, sin = jnp.cos(angle), jnp.sin(angle)
    return jnp.concatenate([cos, cos], 0), jnp.concatenate([sin, sin], 0), first[None, :]


def body(tokens, segments, attn_gain, w_query, w_key, w_value, w_out, mlp_gain, w_gate, w_up, w_down, cotangent):
    rows, width = tokens.shape
    cols, hidden = w_gate.shape
    t = lax.axis_index("tensor")
    cos, sin, first = rope_tables(segments, rows, t * rows)
    extra = jnp.concatenate([attn_gain.reshape(2, -1), mlp_gain.reshape(2, -1), jnp.zeros((28, 2 * HD), BF)], 0)
    w_kv = jnp.concatenate([jnp.concatenate([w_key, w_value], 1), extra], 0)
    h, a1, r1, r2, gains, q, o, lse, kv, wkv, wq, wo, wg, wu, wd, a2, ct = attn_gather(w_kv, w_query, w_out, w_gate, w_up, w_down, cotangent, tokens, cos, sin, first)
    wkv, wq, wo = wkv.reshape(4, 8, -1, 2 * HD), wq.reshape(4, width, -1), wo.reshape(8, 4, -1, cols)
    da2, mo, mo_near, gg, gu, gd = mlp(a2, ct, wg.reshape(width, -1), wu.reshape(width, -1), wd.reshape(8, hidden, -1))
    dres, gain2_part = rms_backward(h, r2, gains[1:2], da2)
    dh = cotangent.astype(F32) + dres
    da1, go, gq, gkv, mo_far = attn_back(wo, wq, wkv, mo, q, o, kv, lse, dh.astype(BF), a1, tokens, r1, gain2_part[None, :], cos, sin, first)
    mo_own = lax.dynamic_index_in_dim(mo, t, 0, keepdims=False)
    output = (h + mo_own.astype(F32) + mo_near[0].astype(F32) + mo_near[1].astype(F32) + mo_far.astype(F32)).astype(BF)
    din, _ = rms_backward(tokens.astype(F32), r1, gains[0:1], da1)
    grad_tokens = dh + din
    gain_grads = gkv[cols : cols + 4].reshape(2, -1)
    gkv = gkv[:cols]
    return (output, grad_tokens, gain_grads[0], gq, gkv[:, :HD], gkv[:, HD:], go, gain_grads[1], gg.astype(F32), gu.astype(F32), gd.astype(F32))


def body_plain(tokens, segments, attn_gain, w_query, w_key, w_value, w_out, mlp_gain, w_gate, w_up, w_down, cotangent):
    rows, width = tokens.shape
    hidden = w_gate.shape[1]
    nt = lax.axis_size("tensor")
    row0 = lax.axis_index("tensor") * rows
    cos, sin, first = rope_tables(segments, rows, row0)
    row0_s = row0[None].astype(jnp.int32)

    gain1 = lax.all_gather(attn_gain, "dp", axis=0, tiled=True).astype(F32)
    gain2 = lax.all_gather(mlp_gain, "dp", axis=0, tiled=True).astype(F32)
    w_kv = jnp.concatenate([w_key, w_value], 1)
    full = lambda w, axis: lax.all_gather(lax.all_gather(w, "dp", axis=axis, tiled=True), "tensor", axis=0)
    wq = full(w_query, 0)
    wkv = full(w_kv, 0)
    wo = full(w_out, 1).reshape(width, width)
    wg = lax.all_gather(w_gate, "dp", axis=0, tiled=True)
    wu = lax.all_gather(w_up, "dp", axis=0, tiled=True)
    wd = lax.all_gather(w_down, "dp", axis=1, tiled=True)

    x = tokens.astype(F32)
    n1, r1 = rms_forward(x, gain1)
    a1 = n1.astype(BF)
    kv = jnp.einsum("rd,gdc->grc", a1, wkv, preferred_element_type=F32)
    cos_r, sin_r = cos.T, sin.T
    k = kv[..., :HD]
    k = k * cos_r + jnp.concatenate([-k[..., HD // 2 :], k[..., : HD // 2]], -1) * sin_r
    kv = jnp.concatenate([k, kv[..., HD:]], -1).astype(BF)
    kv = lax.all_gather(kv, "tensor", axis=1, tiled=True)
    o, q, lse = attn_forward(row0_s, a1, wq, kv, cos, sin, first)
    o2 = o.reshape(-1, rows)
    h = x + dot_tn(o2, wo)

    n2, r2 = rms_forward(h, gain2)
    a2 = lax.all_gather(n2.astype(BF), "tensor", axis=0, tiled=True)
    cot = lax.all_gather(cotangent, "tensor", axis=0, tiled=True)
    output, da2, gg, gu, gd = mlp_plain(h, a2, cot, wg, wu, wd)
    dres, gain2_part = rms_backward(h, r2, gain2, da2)
    dh = cotangent.astype(F32) + dres
    dhb = dh.astype(BF)

    do = dot_nt(wo, dhb).astype(BF).reshape(o.shape)
    go_part = dot_nn(o2, dhb)
    dq, dkv = attn_backward(row0_s, q, kv, do, o, lse, cos, sin, first)
    groups = dkv.shape[0]
    dkv = lax.psum_scatter(dkv.astype(BF), "tensor", scatter_dimension=1, tiled=True).astype(F32)
    dk = dkv[..., :HD]
    ws = dk * sin_r
    dk = dk * cos_r + jnp.concatenate([ws[..., HD // 2 :], -ws[..., : HD // 2]], -1)
    dkv = jnp.concatenate([dk, dkv[..., HD:]], -1).astype(BF)
    gq_part = jnp.einsum("rd,gcr->gdc", a1, dq, preferred_element_type=F32)
    gkv_part = jnp.einsum("rd,grc->gdc", a1, dkv, preferred_element_type=F32)
    da1 = jnp.einsum("gcr,gdc->rd", dq, wq, preferred_element_type=F32) + jnp.einsum("grc,gdc->rd", dkv, wkv, preferred_element_type=F32)
    din, gain1_part = rms_backward(x, r1, gain1, da1)
    grad_tokens = dh + din

    def home_all(v, dim):
        return lax.psum_scatter(home(v, dim + 1), "tensor", scatter_dimension=0, tiled=False).astype(F32)

    gq = home_all(gq_part, 0)
    gkv = home_all(gkv_part, 0)
    go = home_all(go_part.reshape(nt, -1, width), 1)
    gains = lax.psum_scatter(jnp.stack([gain1_part, gain2_part]), "dp", scatter_dimension=1, tiled=True)
    gains = lax.psum(gains, "tensor")
    return (output, grad_tokens, gains[0], gq, gkv[:, :HD], gkv[:, HD:], go, gains[1], gg, gu, gd)


def solution(mesh):
    rows, block = P(("dp", "tensor"), None), P("dp", "tensor")
    turned, line = P("tensor", "dp"), P("dp")
    return jax.shard_map(
        body if (mesh.shape["dp"], mesh.shape["tensor"]) == (8, 4) else body_plain,
        mesh=mesh,
        in_specs=(rows, line, line, block, block, block, turned, line, block, block, turned, rows),
        out_specs=(rows, rows, line, block, block, block, turned, line, block, block, turned),
        check_vma=False,
    )
```

```python
import functools
import math

import jax
import jax.numpy as jnp
from jax import lax
from jax.experimental import pallas as pl
from jax.experimental.pallas import tpu as pltpu
from jax.sharding import PartitionSpec as P

HD = 64
RATIO = 8
EPSILON = 1e-05
MASKED = -1e30
BF = jnp.bfloat16
F32 = jnp.float32


def dot_nn(left, right):
    return lax.dot_general(left, right, (((1,), (0,)), ((), ())), preferred_element_type=F32)


def dot_nt(left, right):
    return lax.dot_general(left, right, (((1,), (1,)), ((), ())), preferred_element_type=F32)


def dot_tn(left, right):
    return lax.dot_general(left, right, (((0,), (0,)), ((), ())), preferred_element_type=F32)


def rms_forward(values_in, gain_row):
    factor = lax.rsqrt(jnp.mean(values_in * values_in, axis=-1, keepdims=True) + EPSILON)
    return (values_in * factor * gain_row, factor)


def rms_backward(values_in, factor, gain_row, gradient):
    scaled = gain_row * gradient
    grad_gain = jnp.sum(gradient * values_in * factor, axis=0)
    grad_input = factor * scaled - values_in * (factor * factor * factor) * jnp.mean(
        scaled * values_in, axis=-1, keepdims=True
    )
    return (grad_input, grad_gain)


def rope_t(u, cos, sin):
    half = HD // 2
    return u * cos + jnp.concatenate([-u[half:], u[:half]], 0) * sin


def rope_back_t(w, cos, sin):
    half = HD // 2
    ws = w * sin
    return w * cos + jnp.concatenate([ws[half:], -ws[:half]], 0)


def bias_of(first, row0, keys, rows):
    key = lax.broadcasted_iota(jnp.int32, (keys, rows), 0)
    row = lax.broadcasted_iota(jnp.int32, (keys, rows), 1) + row0
    return jnp.where((key <= row) & (key >= first), 0.0, MASKED).astype(F32)


def attn_forward_kernel(row0_ref, a1_ref, wq_ref, kv_ref, cos_ref, sin_ref, first_ref, o_ref, q_ref, lse_ref, bias_ref, s_ref, vt_ref):
    keys, rows = bias_ref.shape

    @pl.when(pl.program_id(0) == 0)
    def _():
        bias_ref[...] = bias_of(first_ref[...], row0_ref[0], keys, rows)

    kv = kv_ref[0]
    kvt = kv.T
    vt_ref[...] = jnp.concatenate([kvt[HD:], jnp.ones((16, keys), BF)], 0)
    qt = dot_nn(a1_ref[...], wq_ref[0]).T
    cos, sin = cos_ref[...], sin_ref[...]
    for h in range(RATIO):
        q = (rope_t(qt[h * HD : (h + 1) * HD], cos, sin) * HD ** (-0.5)).astype(BF)
        q_ref[0, h * HD : (h + 1) * HD] = q
        s_ref[...] = dot_nn(kv, jnp.concatenate([q, jnp.zeros_like(q)], 0)) + bias_ref[...]
        peak = jnp.max(s_ref[...], axis=0, keepdims=True)
        e = jnp.exp(s_ref[...] - peak).astype(BF)
        ot = dot_nn(vt_ref[...], e)
        total = ot[HD : HD + 1]
        o_ref[0, h * HD : (h + 1) * HD] = (ot[:HD] / total).astype(BF)
        lse_ref[0, h : h + 1] = peak + jnp.log(total)


def attn_backward_kernel(row0_ref, q_ref, kv_ref, do_ref, o_ref, lse_ref, cos_ref, sin_ref, first_ref, dq_ref, dkv_ref, bias_ref, acc_ref):
    keys, rows = bias_ref.shape

    @pl.when(pl.program_id(0) == 0)
    def _():
        bias_ref[...] = bias_of(first_ref[...], row0_ref[0], keys, rows)

    kv = kv_ref[0]
    kt = kv.T[:HD]
    cos, sin = cos_ref[...], sin_ref[...]
    for h in range(RATIO):
        part = slice(h * HD, (h + 1) * HD)
        q, do, o = q_ref[0, part], do_ref[0, part], o_ref[0, part]
        qz = jnp.concatenate([q, jnp.zeros_like(q)], 0)
        doz = jnp.concatenate([jnp.zeros_like(do), do], 0)
        delta = jnp.sum(do.astype(F32) * o.astype(F32), axis=0, keepdims=True)
        p = jnp.exp(dot_nn(kv, qz) + bias_ref[...] - lse_ref[0, h : h + 1])
        ds = (p * (dot_nn(kv, doz) - delta)).astype(BF)
        grad = dot_nt(ds, qz) + dot_nt(p.astype(BF), doz)
        if h == 0:
            acc_ref[...] = grad
        else:
            acc_ref[...] += grad
        dq = dot_nn(kt, ds) * HD ** (-0.5)
        dq_ref[0, part] = rope_back_t(dq, cos, sin).astype(BF)
    dkv_ref[0] = acc_ref[...]


def params():
    return pltpu.CompilerParams(vmem_limit_bytes=56 * 2**20)


def attn_forward(row0, a1, wq, kv, cos, sin, first):
    groups, width, cols = wq.shape
    rows, keys = a1.shape[0], kv.shape[1]
    whole = lambda *shape: pl.BlockSpec(shape, lambda i: (0,) * len(shape))
    part = lambda *shape: pl.BlockSpec((1,) + shape, lambda i: (i,) + (0,) * len(shape))
    return pl.pallas_call(
        attn_forward_kernel,
        grid=(groups,),
        in_specs=[pl.BlockSpec(memory_space=pltpu.SMEM), whole(rows, width), part(width, cols), part(keys, 2 * HD), whole(HD, rows), whole(HD, rows), whole(1, rows)],
        out_specs=[part(cols, rows), part(cols, rows), part(RATIO, rows)],
        out_shape=[jax.ShapeDtypeStruct((groups, cols, rows), BF), jax.ShapeDtypeStruct((groups, cols, rows), BF), jax.ShapeDtypeStruct((groups, RATIO, rows), F32)],
        scratch_shapes=[pltpu.VMEM((keys, rows), F32), pltpu.VMEM((keys, rows), F32), pltpu.VMEM((HD + 16, keys), BF)],
        compiler_params=params(),
        name="attn_forward",
    )(row0, a1, wq, kv, cos, sin, first)


def attn_backward(row0, q, kv, do, o, lse, cos, sin, first):
    groups, cols, rows = q.shape
    keys = kv.shape[1]
    whole = lambda *shape: pl.BlockSpec(shape, lambda i: (0,) * len(shape))
    part = lambda *shape: pl.BlockSpec((1,) + shape, lambda i: (i,) + (0,) * len(shape))
    return pl.pallas_call(
        attn_backward_kernel,
        grid=(groups,),
        in_specs=[pl.BlockSpec(memory_space=pltpu.SMEM), part(cols, rows), part(keys, 2 * HD), part(cols, rows), part(cols, rows), part(RATIO, rows), whole(HD, rows), whole(HD, rows), whole(1, rows)],
        out_specs=[part(cols, rows), part(keys, 2 * HD)],
        out_shape=[jax.ShapeDtypeStruct((groups, cols, rows), BF), jax.ShapeDtypeStruct((groups, keys, 2 * HD), F32)],
        scratch_shapes=[pltpu.VMEM((keys, rows), F32), pltpu.VMEM((keys, 2 * HD), F32)],
        compiler_params=params(),
        name="attn_backward",
    )(row0, q, kv, do, o, lse, cos, sin, first)


MESH = pl.DeviceIdType.MESH
ANY = pl.BlockSpec(memory_space=pl.ANY)


class Place:
    def __init__(self):
        d, self.t = lax.axis_index("dp"), lax.axis_index("tensor")
        self.c, self.p = d % 2, d // 2
        x, y = self.p % 2, self.p // 2
        self.px, self.py, self.pd = self.p + 1 - 2 * x, self.p + 2 - 4 * y, 3 - self.p
        self.across = [self.t + 1 - 2 * (self.t % 2), (self.t + 2) % 4, 3 - self.t]
        self.inner = (self.t == 1) | (self.t == 2)
        self.outer = (self.t == 0) | (self.t == 3)
        inner = self.t * (3 - self.t) // 2
        self.order = [self.t, self.across[0], 2 - self.t // 2, 3 - self.t // 2 * 3]
        self.away = [0, 1, 2 + inner, 3 - inner]

    def at(self, p, c, t):
        return {"dp": p * 2 + c, "tensor": t}

    def x_side(self):
        return self.at(self.px, self.c, self.t)

    def y_side(self):
        return self.at(self.py, self.c, self.t)

    def twin(self):
        return self.at(self.p, 1 - self.c, self.t)

    def line(self, t):
        return self.at(self.p, self.c, t)

    def greet(self):
        barrier = pltpu.get_barrier_semaphore()
        others = [self.x_side(), self.y_side(), self.twin()] + [self.line(t) for t in self.across]
        for other in others:
            pl.semaphore_signal(barrier, inc=1, device_id=other, device_id_type=MESH)
        pl.semaphore_wait(barrier, len(others))


def half_of(ref, part):
    rows = ref.shape[0] // 2
    return ref.at[pl.ds(part * rows, rows)]


def attn_gather_kernel(kv_in, wq_in, wo_in, wg_in, wu_in, wd_in, ct_in, x_ref, cos_ref, sin_ref, first_ref, h_ref, a1_ref, r1_ref, r2_ref, gains_ref, q_ref, o_ref, lse_ref, kv_ref, kv_out, q_out, o_out, g_out, u_out, d_out, a2_all, ct_all, wkv, wq, wo, rows_kv, bias_ref, s_ref, vt_ref, qt_ref, o_rows, a2_ref, z_send, z_recv, send, recv, local, load, kv_send, kv_recv, line_send, line_recv):
    me = Place()
    rows, width = x_ref.shape
    keys, cols = kv_ref.shape[1], width // 8
    me.greet()
    sources = [kv_in, wq_in, wo_in, wg_in, wu_in, wd_in]
    outs = [kv_out, q_out, o_out, g_out, u_out, d_out]

    def piece(k, s, p, c):
        if k == 2:
            return o_out.at[p, c, s]
        return outs[k].at[s, p, c] if k < 2 else outs[k].at[p, c]

    def pair(k, s, c):
        if k == 2:
            return o_out.at[:, c, s]
        if k == 0:
            return kv_out.at[:, :, c]
        return q_out.at[s, :, c] if k == 1 else outs[k].at[:, c]

    def line_push(k, m):
        return copy_to(sources[k], piece(k, me.t, me.p, me.c), z_send.at[k, m - 1], z_recv.at[k, m - 1], me.line(xor4(me.t, m)))

    def line_first(k):
        for m in (1, 2, 3):
            line_push(k, m).start()

    def arrive(k, j):
        line_push(k, me.away[j]).wait_recv()

    def push(k, j, kind):
        s, i = me.order[j], (0, 1 + j, 5 + j, 9, 10, 11)[k]
        part = (lambda p: kv_out.at[:, p, me.c]) if k == 0 else (lambda p: piece(k, s, p, me.c))
        if kind < 2:
            dst = part(me.p)
            src = sources[k] if j == 0 and k > 0 else dst
        elif kind < 4:
            src = dst = half_of(part(me.px if kind == 2 else me.py), kind - 2)
        else:
            src = dst = pair(k, s, me.c)
        to = [me.x_side, me.y_side, me.y_side, me.x_side, me.twin][kind]()
        return copy_to(src, dst, send.at[i, kind], recv.at[i, kind], to)

    def keep(k):
        return pltpu.make_async_copy(sources[k], piece(k, me.t, me.p, me.c), local.at[k])

    def first(k, j):
        if k == 0:
            keep(k).wait()
        elif j == 0:
            keep(k).start()
        push(k, j, 0).start()
        push(k, j, 1).start()

    def second(k, j):
        push(k, j, 0).wait_recv()
        push(k, j, 2).start()
        push(k, j, 1).wait_recv()
        push(k, j, 3).start()

    def third(k, j):
        push(k, j, 2).wait_recv()
        push(k, j, 3).wait_recv()
        if j == 0 and k > 0:
            keep(k).wait()
        push(k, j, 4).start()

    def last(k, j):
        push(k, j, 4).wait_recv()

    def step(n, k, action):
        t, out, own = me.t, (ct_all, a2_all)[n], (ct_in, a2_ref)[n]
        for way, chunk, can in ((0, t - k + 1, (t < 3) & (t - k + 1 >= 0)), (1, t + k - 1, (t > 0) & (t + k - 1 <= 3))):

            @pl.when(can)
            def _():
                src = own if k == 1 else out.at[chunk]
                copy = copy_to(src, out.at[chunk], line_send.at[n, way, k - 1], line_recv.at[n, way, k - 1], me.line(t + 1 - 2 * way))
                copy.start() if action == "start" else copy.wait_send()

    def got(n, k):
        t, out = me.t, (ct_all, a2_all)[n]
        for way, chunk, can in ((0, t - k, t - k >= 0), (1, t + k, t + k <= 3)):

            @pl.when(can)
            def _():
                copy_to(out.at[chunk], out.at[chunk], line_send.at[n, way, k - 1], line_recv.at[n, way, k - 1], me.line(t + 1 - 2 * way)).wait_recv()

    def own_rows(n):
        return pltpu.make_async_copy((ct_in, a2_ref)[n], (ct_all, a2_all)[n].at[me.t], local.at[6 + n])

    kv_load = pltpu.make_async_copy(kv_out, wkv, load.at[0])
    kv_keep = pltpu.make_async_copy(rows_kv, kv_ref, load.at[1])

    def wq_load(j):
        return pltpu.make_async_copy(q_out.at[me.order[j]], wq.at[j % 2], load.at[2 + j % 2])

    def wo_load(j):
        s = me.order[j]
        return pltpu.make_async_copy(o_out.at[:, :, s], wo.at[:, :, pl.ds(pl.multiple_of(s * 2 * cols, cols), 2 * cols)], load.at[4 + j])

    own = pl.ds(pl.multiple_of(me.t * rows, rows), rows)

    def kv_push(m, g):
        part = rows_kv.at[g, own]
        return copy_to(part, part, kv_send.at[m - 1, g], kv_recv.at[m - 1, g], me.line(xor4(me.t, m)))

    def gain(n):
        parts = [wkv[0, d // 2, d % 2, cols + 2 * n + e : cols + 2 * n + e + 1] for d in range(8) for e in range(2)]
        return jnp.concatenate(parts, 1).astype(F32)

    def norm(value):
        return lax.rsqrt(jnp.mean(value * value, axis=-1, keepdims=True) + EPSILON)

    def project_keys():
        x = x_ref[...].astype(F32)
        r1_ref[...] = norm(x)
        gains_ref[0:1] = gain(0)
        gains_ref[1:2] = gain(1)
        a1_ref[...] = (x * r1_ref[...] * gains_ref[0:1]).astype(BF)
        for m in (1, 2, 3, 0):
            g = xor4(me.t, m)
            weights = wkv[g, :, :, :cols].reshape(width, 2 * HD)
            kvt = dot_nn(a1_ref[...], weights).T
            kvt = jnp.concatenate([rope_t(kvt[:HD], cos_ref[...], sin_ref[...]), kvt[HD:]], 0).astype(BF)
            rows_kv[g, own] = kvt.T
            if m > 0:
                kv_push(m, g).start()
        for more in (1, 2, 3):
            for m in (1, 2, 3):
                kv_push(m, xor4(me.t, m ^ more)).start()

    def attend(j, part):
        g = me.order[j]
        if part == 0:
            for m in (1, 2, 3):
                kv_push(m, g).wait_recv()
            qt_ref[...] = dot_nn(a1_ref[...], wq[j % 2].reshape(width, -1)).T
            vt_ref[...] = jnp.concatenate([rows_kv[g].T[HD:], jnp.ones((16, keys), BF)], 0)
        cos, sin = cos_ref[...], sin_ref[...]

        def head(h, _):
            part = pl.ds(pl.multiple_of(h * HD, HD), HD)
            q = (rope_t(qt_ref[part], cos, sin) * HD ** (-0.5)).astype(BF)
            q_ref[g, part] = q
            s_ref[...] = dot_nn(rows_kv[g], jnp.concatenate([q, jnp.zeros_like(q)], 0)) + bias_ref[...]
            peak = jnp.max(s_ref[...], axis=0, keepdims=True)
            e = jnp.exp(s_ref[...] - peak).astype(BF)
            ot = dot_nn(vt_ref[...], e)
            total = ot[HD : HD + 1]
            o_ref[g, part] = (ot[:HD] / total).astype(BF)
            lse_ref[g, pl.ds(h, 1)] = peak + jnp.log(total)
            return 0

        lax.fori_loop(part * RATIO // 2, (part + 1) * RATIO // 2, head, 0, unroll=2)
        if part == 1:
            o_rows[:, pl.ds(pl.multiple_of(g * 2 * cols, cols), 2 * cols)] = o_ref[g].T

    def mix():
        for d in range(8):
            part = slice(d * cols, (d + 1) * cols)
            h_ref[:, part] = x_ref[:, part].astype(F32) + dot_nn(o_rows[...], wo[d // 2, d % 2])
        h = h_ref[...]
        r2_ref[...] = norm(h)
        a2_ref[...] = (h * r2_ref[...] * gains_ref[1:2]).astype(BF)

    KV, Q, O, G, U, D = range(6)
    keep(KV).start()
    line_first(KV)
    first(Q, 0)
    own_rows(0).start()
    arrive(KV, 1)
    line_first(Q)
    arrive(KV, 2)
    arrive(KV, 3)
    first(KV, 0)
    first(O, 0)
    bias_ref[...] = bias_of(first_ref[...], me.t * rows, keys, rows)
    second(KV, 0)
    second(Q, 0)
    third(KV, 0)
    arrive(Q, 1)
    first(Q, 1)
    last(KV, 0)
    kv_load.start()
    second(O, 0)
    kv_load.wait()
    project_keys()
    line_first(O)
    arrive(Q, 2)
    first(Q, 2)
    third(Q, 0)
    second(Q, 1)
    arrive(Q, 3)
    first(Q, 3)
    last(Q, 0)
    wq_load(0).start()
    third(Q, 1)
    third(O, 0)
    second(Q, 2)
    arrive(O, 1)
    step(0, 1, "start")
    first(O, 1)
    wq_load(0).wait()
    attend(0, 0)
    third(Q, 2)
    last(Q, 1)
    wq_load(1).start()
    second(Q, 3)
    arrive(O, 2)
    first(O, 2)
    attend(0, 1)
    third(Q, 3)
    second(O, 1)
    arrive(O, 3)
    first(O, 3)
    wq_load(1).wait()
    attend(1, 0)
    last(Q, 2)
    wq_load(2).start()
    third(O, 1)
    second(O, 2)
    got(0, 1)
    step(0, 2, "start")
    attend(1, 1)
    last(Q, 3)
    wq_load(3).start()
    second(O, 3)
    first(G, 0)
    third(O, 2)
    wq_load(2).wait()
    attend(2, 0)
    third(O, 3)
    last(O, 0)
    wo_load(0).start()
    last(O, 1)
    wo_load(1).start()
    attend(2, 1)
    last(O, 2)
    wo_load(2).start()
    last(O, 3)
    wo_load(3).start()
    first(U, 0)
    wq_load(3).wait()
    attend(3, 0)
    got(0, 2)
    step(0, 3, "start")
    attend(3, 1)
    for j in range(4):
        wo_load(j).wait()
    mix()
    own_rows(1).start()
    step(1, 1, "start")
    kv_keep.start()
    second(G, 0)
    first(D, 0)
    third(G, 0)
    second(U, 0)
    got(1, 1)
    step(1, 2, "start")
    third(U, 0)
    second(D, 0)
    third(D, 0)
    for k in (G, U, D):
        last(k, 0)
    got(0, 3)
    got(1, 2)
    kv_keep.wait()
    for n in range(2):
        own_rows(n).wait()
        for k in (1, 2, 3)[: 3 - n]:
            step(n, k, "wait")
    for j in (1, 2, 3):
        for g in range(4):
            kv_push(j, g).wait_send()
        for k in (KV, Q, O):
            line_push(k, j).wait_send()
    for k in range(6):
        for j in range(4 if k in (Q, O) else 1):
            for kind in range(5):
                push(k, j, kind).wait_send()


def attn_gather(kv, wq, wo, wg, wu, wd, ct, x, cos, sin, first):
    rows, width = x.shape
    heads, cols, keys = wq.shape[1], wq.shape[0], 4 * rows
    dma, vmem = pltpu.SemaphoreType.DMA, lambda *shape: pltpu.VMEM(shape, BF)
    low = lambda *dims: jax.ShapeDtypeStruct(dims, BF)
    full = lambda *dims: jax.ShapeDtypeStruct(dims, F32)
    inside = pl.BlockSpec(memory_space=pltpu.VMEM)
    return pl.pallas_call(
        attn_gather_kernel,
        out_shape=[
            full(rows, width), low(rows, width), full(rows, 1), full(rows, 1), full(2, width), low(4, heads, rows), low(4, heads, rows), full(4, RATIO, rows),
            low(4, keys, 2 * HD), low(4, 4, 2, *kv.shape), low(4, 4, 2, *wq.shape), low(4, 2, 4, *wo.shape),
            low(4, 2, *wg.shape), low(4, 2, *wu.shape), low(4, 2, *wd.shape), low(4, rows, width), low(4, rows, width),
        ],
        in_specs=[ANY] * 7 + [inside] * 4,
        out_specs=[inside] * 8 + [ANY] * 9,
        scratch_shapes=[
            vmem(4, 4, 2, *kv.shape), vmem(2, 4, 2, cols, heads), vmem(4, 2, width, cols), vmem(4, keys, 2 * HD),
            pltpu.VMEM((keys, rows), F32), pltpu.VMEM((keys, rows), F32), vmem(HD + 16, keys), pltpu.VMEM((heads, rows), F32), vmem(rows, width), vmem(rows, width),
            dma((3, 3)), dma((3, 3)), dma((12, 5)), dma((12, 5)), dma((8,)), dma((8,)), dma((3, 4)), dma((3, 4)), dma((2, 2, 3)), dma((2, 2, 3)),
        ],
        compiler_params=pltpu.CompilerParams(collective_id=1, has_side_effects=True, vmem_limit_bytes=56 * 2**20),
        name="attn_gather",
    )(kv, wq, wo, wg, wu, wd, ct, x, cos, sin, first)


def xor4(a, m):
    return (a // 2 + m // 2) % 2 * 2 + (a % 2 + m % 2) % 2


def copy_to(src, dst, send_sem, recv_sem, to):
    return pltpu.make_async_remote_copy(src, dst, send_sem, recv_sem, device_id=to, device_id_type=MESH)


def add_low(left, right):
    return (left.astype(F32) + right.astype(F32)).astype(BF)


def mlp_kernel(a2_old, ct_in, wg_in, wu_in, wd_in, h_in, r2_ref, gain_ref, a2_in, da2_out, dhb_out, gain_out, mo_out, mo_got, gg_out, gu_out, gd_out, twin_g, twin_u, twin_d, wg, wu, wd, a2_buf, ct_buf, mo_buf, a2_col, ct_col, zt, dg, du, out_buf, in_buf, diag_gu, x_gu, y_gu, diag_d, x_d, y_d, stage_gu, stage_d, h_buf, load, store, line_send, line_recv, a2_send, a2_recv, mo_send, mo_recv, twin_send, twin_recv, send, recv, stage_sem):
    me = Place()
    rows, width = da2_out.shape
    hidden = wg.shape[1]
    cols = width // 8
    weights = [pltpu.make_async_copy(wg_in, wg, load.at[4]), pltpu.make_async_copy(wu_in, wu, load.at[5])]
    weights += [pltpu.make_async_copy(wd_in.at[d], wd.at[:, pl.ds(d * cols, cols)], load.at[6 + d]) for d in range(8)]
    for copy in weights:
        copy.start()

    def away(j):
        return 2 * (1 - j % 2) + (j % 2 + j // 2) % 2

    a2_push = copy_to(a2_in.at[xor4(me.t, 2)], a2_in.at[xor4(me.t, 2)], a2_send.at[0], a2_recv.at[0], me.line(xor4(me.t, 1)))

    def chunk_load(j, slot):
        s = xor4(me.t, away(j))
        return pltpu.make_async_copy(a2_in.at[s], a2_buf.at[slot], load.at[slot]), pltpu.make_async_copy(ct_in.at[s], ct_buf.at[slot], load.at[2 + slot])

    near, cross, both = in_buf.at[0], in_buf.at[1], in_buf.at[pl.ds(2, 2)]

    def near_send():
        return copy_to(out_buf.at[0], near, line_send.at[0], line_recv.at[0], me.line(xor4(me.t, 1)))

    def both_send(m):
        s = xor4(me.t, m)
        return copy_to(out_buf.at[m - 1], both.at[s % 2], line_send.at[m - 1], line_recv.at[2 + s % 2], me.line(xor4(me.t, 1)))

    def cross_send(m):
        return copy_to(out_buf.at[m - 1], cross, line_send.at[m - 1], line_recv.at[1], me.line(xor4(me.t, m)))

    def cross_add(m):
        s = xor4(me.t, m)
        copy_to(both.at[s % 2], both.at[s % 2], line_send.at[0], line_recv.at[2 + s % 2], me.line(xor4(me.t, 1))).wait_recv()
        out_buf[m - 1] = add_low(out_buf[m - 1], both[s % 2])
        cross_send(m).start()

    def mo_store(j, slot):
        return pltpu.make_async_copy(mo_buf.at[slot], mo_out.at[xor4(me.t, away(j))], store.at[slot])

    for copy in chunk_load(0, 0):
        copy.start()
    me.greet()

    @pl.when(me.inner)
    def _():
        a2_push.start()

    def chunk(j, _):
        slot = j % 2

        for copy in chunk_load(j, slot):
            copy.wait()
        where = pl.multiple_of(xor4(me.t, away(j)) * rows, rows)

        @pl.when(j == 0)
        def _():
            weights[0].wait()

        g = dot_nn(a2_buf[slot], wg[...])

        @pl.when(j == 0)
        def _():
            for copy in weights[1:]:
                copy.wait()

        u = dot_nn(a2_buf[slot], wu[...])
        dz = dot_nt(ct_buf[slot], wd[...])
        sig = 1.0 / (1.0 + jnp.exp(-g))
        act = g * sig
        z = (act * u).astype(BF)
        zt[:, pl.ds(where, rows)] = z.T
        dg_now = (dz * u * (sig * (1.0 + g * (1.0 - sig)))).astype(BF)
        du_now = (dz * act).astype(BF)
        dg[pl.ds(where, rows)] = dg_now
        du[pl.ds(where, rows)] = du_now
        part = dot_nt(dg_now, wg[...]) + dot_nt(du_now, wu[...])

        @pl.when(j < 3)
        def _():
            out_buf[away(j) - 1] = part.astype(BF)

        @pl.when((j == 1) & me.inner)
        def _():
            near_send().start()

        for at, m in ((0, 2), (2, 3)):

            @pl.when((j == at) & me.outer)
            def _():
                both_send(m).start()

        @pl.when(j == 3)
        def _():
            da2_out[...] = part

        @pl.when((j == 1) & me.outer)
        def _():
            a2_push.wait_recv()

        @pl.when(j < 3)
        def _():
            for copy in chunk_load(j + 1, 1 - slot):
                copy.start()

        @pl.when(j >= 2)
        def _():
            mo_store(j - 2, slot).wait()

        mo_buf[slot] = dot_nn(z, wd[...]).astype(BF)
        mo_store(j, slot).start()
        return 0

    lax.fori_loop(0, 4, chunk, 0)
    mo_store(2, 0).wait()
    mo_store(3, 1).wait()

    def mo_push(m):
        return copy_to(mo_out.at[xor4(me.t, m)], mo_got.at[m - 1], mo_send.at[m - 1], mo_recv.at[m - 1], me.line(xor4(me.t, m)))

    @pl.when(me.inner)
    def _():
        cross_add(3)

    def owner(i):
        return xor4(me.p, 3 - i % 4) * 2 + (1 - me.c + i // 4) % 2

    def tile_load(i, slot):
        at = pl.ds(pl.multiple_of(owner(i) * cols, cols), cols)
        return pltpu.make_async_copy(a2_in.at[:, :, at], a2_col.at[slot], load.at[slot]), pltpu.make_async_copy(ct_in.at[:, :, at], ct_col.at[slot], load.at[2 + slot])

    def piece(k, p, c):
        at = pl.ds(pl.multiple_of((p * 2 + c) * cols, cols), cols)
        return (wg, wu)[k].at[at] if k < 2 else wd.at[:, at]

    twins = [twin_g, twin_u, twin_d]

    def twin_push(k, i):
        p = xor4(me.p, 3 - i)
        return copy_to(piece(k, p, 1 - me.c), twins[k].at[p], twin_send.at[k, i], twin_recv.at[k, i], me.twin())

    diag = [diag_gu.at[0], diag_gu.at[1], diag_d]
    from_x = [x_gu.at[0], x_gu.at[1], x_d]
    from_y = [y_gu.at[0], y_gu.at[1], y_d]
    stage = [stage_gu.at[0], stage_gu.at[1], stage_d]

    def side(k, kind):
        if kind < 2:
            src, dst = half_of(piece(k, me.pd, me.c), kind), half_of(diag[k], kind)
        else:
            src, dst = (piece(k, me.px, me.c), from_x[k]) if kind == 2 else (piece(k, me.py, me.c), from_y[k])
        return copy_to(src, dst, send.at[k, kind], recv.at[k, kind], me.x_side() if kind % 2 == 0 else me.y_side())

    def fetch(k, p):
        return pltpu.make_async_copy(twins[k].at[p], stage[k], stage_sem.at[k])

    for copy in tile_load(0, 0):
        copy.start()

    def tile(i, _):
        slot = i % 2

        @pl.when(i < 7)
        def _():
            for copy in tile_load(i + 1, 1 - slot):
                copy.start()

        for copy in tile_load(i, slot):
            copy.wait()
        at = pl.ds(pl.multiple_of(owner(i) * cols, cols), cols)
        a2t = a2_col[slot].reshape(4 * rows, cols).T
        wg[at] = dot_nn(a2t, dg[...]).astype(BF)
        wu[at] = dot_nn(a2t, du[...]).astype(BF)
        wd[:, at] = dot_nn(zt[...], ct_col[slot].reshape(4 * rows, cols)).astype(BF)

        @pl.when(i < 4)
        def _():
            for k in range(3):
                twin_push(k, i).start()

        @pl.when(i >= 4)
        def _():
            p = xor4(me.p, 7 - i)
            for k in range(3):
                twin_push(k, i - 4).wait_recv()
                fetch(k, p).start()
            for k in range(3):
                fetch(k, p).wait()
                mine = piece(k, p, me.c)
                mine[...] = add_low(mine[...], stage[k][...])

        @pl.when(i == 4)
        def _():
            for k in range(3):
                side(k, 0).start()
                side(k, 1).start()

        @pl.when((i == 5) & me.inner)
        def _():
            cross_add(2)

        @pl.when((i == 5) & me.outer)
        def _():
            near_send().start()

        @pl.when(i == 5)
        def _():
            for m in (1, 2):
                mo_push(m).start()

        return 0

    lax.fori_loop(0, 8, tile, 0)
    for k in range(3):
        side(k, 1).wait_recv()
        part, extra = half_of(piece(k, me.px, me.c), 1), half_of(diag[k], 1)
        part[...] = add_low(part[...], extra[...])
        side(k, 2).start()
        side(k, 0).wait_recv()
        part, extra = half_of(piece(k, me.py, me.c), 0), half_of(diag[k], 0)
        part[...] = add_low(part[...], extra[...])
        side(k, 3).start()
    own_ct = pltpu.make_async_copy(ct_in.at[me.t], ct_buf.at[0], load.at[2])
    own_ct.start()

    def h_load(n):
        return pltpu.make_async_copy(h_in.at[pl.ds(n * h_buf.shape[0], h_buf.shape[0])], h_buf, load.at[0])

    h_load(0).start()
    results = []
    for k in range(3):
        side(k, 2).wait_recv()
        side(k, 3).wait_recv()
        mine = piece(k, me.p, me.c)
        mine[...] = (mine[...].astype(F32) + from_x[k][...].astype(F32) + from_y[k][...].astype(F32)).astype(BF)
        results.append(pltpu.make_async_copy(mine, (gg_out, gu_out, gd_out)[k], stage_sem.at[k]))
        results[-1].start()
    own_ct.wait()
    near_send().wait_recv()
    cross_send(2).wait_recv()
    part_rows = h_buf.shape[0]
    for n in range(rows // part_rows):
        at = slice(n * part_rows, (n + 1) * part_rows)
        h_load(n).wait()
        da2 = da2_out[at] + in_buf[0, at].astype(F32) + in_buf[1, at].astype(F32)
        scaled, h, r2 = gain_ref[1:2] * da2, h_buf[...], r2_ref[at]
        gain = jnp.sum(da2 * h * r2, axis=0, keepdims=True)
        gain_out[...] = gain if n == 0 else gain_out[...] + gain
        dres = r2 * scaled - h * (r2 * r2 * r2) * jnp.mean(scaled * h, axis=-1, keepdims=True)
        if n + 1 < rows // part_rows:
            h_load(n + 1).start()
        dh = ct_buf[0, at].astype(F32) + dres
        da2_out[at] = dh
        ct_buf[1, at] = dh.astype(BF)
    results.append(pltpu.make_async_copy(ct_buf.at[1], dhb_out, load.at[1]))
    results[-1].start()
    for copy in results:
        copy.wait()
    for m in (1, 2):
        mo_push(m).wait()

    @pl.when(me.inner)
    def _():
        a2_push.wait_send()

    near_send().wait_send()
    for m in (2, 3):
        cross_send(m).wait_send()
    for k in range(3):
        for i in range(4):
            twin_push(k, i).wait_send()
            side(k, i).wait_send()


def mlp(a2, ct, wg, wu, wd, h, r2, gain):
    chunks, rows, width = a2.shape
    hidden, cols = wg.shape[1], width // 8
    dma, vmem = pltpu.SemaphoreType.DMA, lambda *shape: pltpu.VMEM(shape, BF)
    shape = lambda *dims: jax.ShapeDtypeStruct(dims, BF)
    full = lambda *dims: jax.ShapeDtypeStruct(dims, F32)
    inside = pl.BlockSpec(memory_space=pltpu.VMEM)
    return pl.pallas_call(
        mlp_kernel,
        out_shape=[shape(4, rows, width), full(rows, width), shape(rows, width), full(1, width), shape(4, rows, width), shape(2, rows, width), shape(cols, hidden), shape(cols, hidden), shape(hidden, cols), shape(4, cols, hidden), shape(4, cols, hidden), shape(4, hidden, cols)],
        in_specs=[ANY] * 6 + [inside] * 2,
        out_specs=[ANY, inside, ANY, inside] + [ANY] * 8,
        input_output_aliases={0: 0},
        scratch_shapes=[
            vmem(width, hidden), vmem(width, hidden), vmem(hidden, width),
            vmem(2, rows, width), vmem(2, rows, width), vmem(2, rows, width),
            vmem(2, 4, rows, cols), vmem(2, 4, rows, cols),
            vmem(hidden, 4 * rows), vmem(4 * rows, hidden), vmem(4 * rows, hidden),
            vmem(3, rows, width), vmem(4, rows, width),
            vmem(2, cols, hidden), vmem(2, cols, hidden), vmem(2, cols, hidden),
            vmem(hidden, cols), vmem(hidden, cols), vmem(hidden, cols),
            vmem(2, cols, hidden), vmem(hidden, cols), pltpu.VMEM((rows // 2, width), F32),
            dma((14,)), dma((2,)), dma((3,)), dma((4,)), dma((1,)), dma((1,)), dma((2,)), dma((2,)), dma((3, 4)), dma((3, 4)), dma((3, 4)), dma((3, 4)), dma((3,)),
        ],
        compiler_params=pltpu.CompilerParams(collective_id=2, has_side_effects=True, vmem_limit_bytes=63 * 2**20),
        name="mlp",
    )(a2, ct, wg, wu, wd, h, r2, gain)[1:9]


def home(v, dim):
    return lax.psum_scatter(v.astype(BF), "dp", scatter_dimension=dim, tiled=True)


def mlp_plain(h, a2, cot, wg, wu, wd):
    g, u = dot_nn(a2, wg), dot_nn(a2, wu)
    sig = jax.nn.sigmoid(g)
    act = g * sig
    z = (act * u).astype(BF)
    scatter = lambda v: lax.psum_scatter(v.astype(BF), "tensor", scatter_dimension=0, tiled=True).astype(F32)
    output = (h + scatter(dot_nn(z, wd))).astype(BF)
    dz = dot_nt(cot, wd)
    dg = (dz * u * (sig * (1.0 + g * (1.0 - sig)))).astype(BF)
    du = (dz * act).astype(BF)
    gd = home(dot_tn(z, cot), 1).astype(F32)
    gg = home(dot_tn(a2, dg), 0).astype(F32)
    gu = home(dot_tn(a2, du), 0).astype(F32)
    da2 = scatter(dot_nt(dg, wg) + dot_nt(du, wu))
    return output, da2, gg, gu, gd


def attn_back_kernel(wo_in, wq_in, wkv_in, mo_in, dh_in, q_ref, o_ref, kv_ref, lse_ref, dh_ref, a1_ref, x_ref, r1_ref, gain2_ref, gains_ref, cos_ref, sin_ref, first_ref, da1_ref, go_ref, gq_ref, gkv_ref, mo_got, twin_o, twin_q, twin_kv, grad_o, grad_q, grad_kv, diag_o, diag_q, diag_kv, x_o, x_q, x_kv, y_o, y_q, y_kv, z_o, z_q, z_kv, stage_o, stage_q, stage_kv, wo, wq, wkv, a1t, do_ref, bias_ref, acc_ref, dqt_ref, dkv_own, dkv_out, dkv_got, dh_buf, load, mo_sem, dkv_send, dkv_recv, twin_send, twin_recv, send, recv, line_send, line_recv):
    me = Place()
    rows, width = dh_ref.shape
    keys, cols = kv_ref.shape[1], width // 8
    head_of = [3 - me.t // 2 * 3, 2 - me.t // 2, xor4(me.t, 1), me.t]

    def wo_load(j):
        return pltpu.make_async_copy(wo_in.at[:, head_of[j]], wo.at[j % 2], load.at[j % 2])

    def wq_load(j):
        return pltpu.make_async_copy(wq_in.at[head_of[j]], wq, load.at[2])

    wkv_load = pltpu.make_async_copy(wkv_in, wkv, load.at[3])
    mo_push = copy_to(mo_in.at[xor4(me.t, 3)], mo_got, mo_sem.at[0], mo_sem.at[1], me.line(xor4(me.t, 3)))
    wo_load(0).start()
    wo_load(1).start()
    wq_load(0).start()
    wkv_load.start()
    me.greet()
    mo_push.start()
    a1t[...] = a1_ref[...].T
    bias_ref[...] = bias_of(first_ref[...], me.t * rows, keys, rows)

    grads, twins, diags = [grad_o, grad_q, grad_kv], [twin_o, twin_q, twin_kv], [diag_o, diag_q, diag_kv]
    from_x, from_y, from_z = [x_o, x_q, x_kv], [y_o, y_q, y_kv], [z_o, z_q, z_kv]
    stages = [stage_o, stage_q, stage_kv]

    def twin_push(k, j):
        i = k * 4 + j
        return copy_to(grads[k].at[j, :, 1 - me.c], twins[k].at[j], twin_send.at[i], twin_recv.at[i], me.twin())

    def side(k, j, kind):
        i = k * 4 + j
        piece = lambda p: grads[k].at[j, p, me.c]
        if kind < 2:
            src, dst = half_of(piece(me.pd), kind), half_of(diags[k].at[j], kind)
        else:
            src, dst = (piece(me.px), from_x[k].at[j]) if kind == 2 else (piece(me.py), from_y[k].at[j])
        return copy_to(src, dst, send.at[i, kind], recv.at[i, kind], me.x_side() if kind % 2 == 0 else me.y_side())

    def line_push(k, j, slot):
        to = xor4(me.t, 1) if slot != 1 else head_of[j]
        return copy_to(grads[k].at[j, me.p, me.c], from_z[k].at[slot], line_send.at[k, j], line_recv.at[k, slot], me.line(to))

    def fourth(k, j):
        @pl.when(me.inner)
        def _():
            line_push(k, j, 2 + j).wait_recv()
            mine = grads[k].at[j, me.p, me.c]
            mine[...] = add_low(mine[...], from_z[k][2 + j])
            line_push(k, j, 1).start()

    def first(k, j):
        twin_push(k, j).wait_recv()
        copy = pltpu.make_async_copy(twins[k].at[j], stages[k], load.at[4])
        copy.start()
        copy.wait()
        for p in (me.pd, me.px, me.py, me.p):
            mine = grads[k].at[j, p, me.c]
            mine[...] = add_low(mine[...], stages[k][p])
            if p is me.pd:
                side(k, j, 0).start()
                side(k, j, 1).start()

    def second(k, j):
        for kind, p, to in ((1, me.px, 2), (0, me.py, 3)):
            side(k, j, kind).wait_recv()
            part, extra = half_of(grads[k].at[j, p, me.c], kind), half_of(diags[k].at[j], kind)
            part[...] = add_low(part[...], extra[...])
            side(k, j, to).start()

    def third(k, j):
        side(k, j, 2).wait_recv()
        side(k, j, 3).wait_recv()
        mine = grads[k].at[j, me.p, me.c]
        total = mine[...].astype(F32) + from_x[k][j].astype(F32) + from_y[k][j].astype(F32)
        if j < 3:
            mine[...] = total.astype(BF)
            if j == 2:
                line_push(k, j, 0).start()
            else:

                @pl.when(me.outer)
                def _():
                    line_push(k, j, 2 + j).start()
        else:
            (go_ref, gq_ref, gkv_ref)[k][...] = total

    def out_group(j):
        g = head_of[j]
        wo_load(j).wait()
        do = jnp.zeros((wo.shape[2], rows), F32)
        for d in range(8):
            part = slice(d * cols, (d + 1) * cols)
            do += dot_nt(wo[j % 2, d], dh_ref[:, part])
            grad_o[j, d // 2, d % 2] = dot_nn(o_ref[g], dh_ref[:, part]).astype(BF)
        twin_push(0, j).start()
        do_ref[j] = do.astype(BF)
        if j + 2 < 4:
            wo_load(j + 2).start()

    def dkv_push(j, m):
        z, s = xor4(me.t, m), head_of[j]
        src = dkv_out.at[j, pl.ds(pl.multiple_of(z * rows, rows), rows)]
        return copy_to(src, dkv_got.at[m - 1, s], dkv_send.at[m - 1, j], dkv_recv.at[m - 1, s], me.line(z))

    def back_group(j):
        g = head_of[j]
        kv = kv_ref[g]
        kt = kv.T[:HD]
        cos, sin = cos_ref[...], sin_ref[...]

        def head(h, _):
            part = pl.ds(pl.multiple_of(h * HD, HD), HD)
            q, do, o = q_ref[g, part], do_ref[j, part], o_ref[g, part]
            qz = jnp.concatenate([q, jnp.zeros_like(q)], 0)
            doz = jnp.concatenate([jnp.zeros_like(do), do], 0)
            delta = jnp.sum(do.astype(F32) * o.astype(F32), axis=0, keepdims=True)
            p = jnp.exp(dot_nn(kv, qz) + bias_ref[...] - lse_ref[g, pl.ds(h, 1)])
            ds = (p * (dot_nn(kv, doz) - delta)).astype(BF)
            acc_ref[...] += dot_nt(ds, qz) + dot_nt(p.astype(BF), doz)
            dqt_ref[part] = rope_back_t(dot_nn(kt, ds) * HD ** (-0.5), cos, sin).astype(BF)
            return 0

        acc_ref[...] = jnp.zeros_like(acc_ref)
        lax.fori_loop(0, RATIO, head, 0, unroll=2)
        dkv_out[j] = acc_ref[...].astype(BF)
        dkv_own[j] = acc_ref[pl.ds(pl.multiple_of(me.t * rows, rows), rows)]
        for m in (3, 2, 1):
            dkv_push(j, m).start()
        for d in range(8):
            grad_q[j, d // 2, d % 2] = dot_nt(a1t[d * cols : (d + 1) * cols], dqt_ref[...]).astype(BF)
        twin_push(1, j).start()
        wq_load(j).wait()
        part = dot_nt(dqt_ref[...].T, wq[...])
        if j == 0:
            da1_ref[...] = part
        else:
            da1_ref[...] += part
        if j < 3:
            wq_load(j + 1).start()

    def keys_back():
        wkv_load.wait()
        turned = []
        for j in range(4):
            total = dkv_own[j]
            for m in (3, 2, 1):
                dkv_push(j, m).wait_recv()
                total += dkv_got[m - 1, head_of[j]].astype(F32)
            total = total.T
            dkvt = jnp.concatenate([rope_back_t(total[:HD], cos_ref[...], sin_ref[...]), total[HD:]], 0)
            turned.append(dkvt.astype(BF))
            da1_ref[...] += dot_nt(dkvt.T.astype(BF), wkv[head_of[j], :, :cols].reshape(width, 2 * HD))
        gain1 = jnp.sum(da1_ref[...] * (x_ref[...].astype(F32) * r1_ref[...]), axis=0, keepdims=True)
        gain2 = gain2_ref[...]
        for j in range(4):
            for d in range(8):
                at = d * cols
                grad_kv[j, d // 2, d % 2, :cols] = dot_nt(a1t[at : at + cols], turned[j]).astype(BF)
                extra = [gain1[:, at : at + 128], gain1[:, at + 128 : at + 256], gain2[:, at : at + 128], gain2[:, at + 128 : at + 256], jnp.zeros((28, 128), F32)]
                grad_kv[j, d // 2, d % 2, cols:] = jnp.concatenate(extra, 0).astype(BF)
            twin_push(2, j).start()

    def dh_load(n):
        return pltpu.make_async_copy(dh_in.at[pl.ds(n * dh_buf.shape[0], dh_buf.shape[0])], dh_buf, load.at[5])

    def norm_back():
        part_rows = dh_buf.shape[0]
        for n in range(rows // part_rows):
            at = slice(n * part_rows, (n + 1) * part_rows)
            scaled, x, r1 = gains_ref[0:1] * da1_ref[at], x_ref[at].astype(F32), r1_ref[at]
            din = r1 * scaled - x * (r1 * r1 * r1) * jnp.mean(scaled * x, axis=-1, keepdims=True)
            dh_load(n).wait()
            da1_ref[at] = dh_buf[...] + din
            if n + 1 < rows // part_rows:
                dh_load(n + 1).start()

    O, Q, KV = range(3)
    dh_load(0).start()
    for j in range(4):
        out_group(j)
    for j in range(4):
        first(O, j)
    second(O, 0)
    second(O, 1)
    back_group(0)
    second(O, 2)
    second(O, 3)
    first(Q, 0)
    third(O, 0)
    back_group(1)
    third(O, 1)
    second(Q, 0)
    first(Q, 1)
    third(O, 2)
    fourth(O, 0)
    back_group(2)
    third(O, 3)
    second(Q, 1)
    first(Q, 2)
    third(Q, 0)
    fourth(O, 1)
    back_group(3)
    second(Q, 2)
    first(Q, 3)
    third(Q, 1)
    fourth(Q, 0)
    keys_back()
    second(Q, 3)
    third(Q, 2)
    fourth(Q, 1)
    for j in range(4):
        first(KV, j)
    norm_back()
    third(Q, 3)
    for j in range(4):
        second(KV, j)
    for j in range(4):
        third(KV, j)
    for j in range(2):
        fourth(KV, j)
    for k in range(3):
        line_push(k, 2, 0).wait()
        line_push(k, 0, 1).wait()
        line_push(k, 1, 1).wait_send()
        total = (go_ref, gq_ref, gkv_ref)[k]
        total[...] += from_z[k][0].astype(F32) + from_z[k][1].astype(F32)
    mo_push.wait()
    for j in range(4):
        for m in (1, 2, 3):
            dkv_push(j, m).wait_send()
        for k in range(3):
            twin_push(k, j).wait_send()
            for kind in range(4):
                side(k, j, kind).wait_send()


def attn_back(wo, wq, wkv, mo, dh_full, q, o, kv, lse, dh, a1, x, r1, gain2, gains, cos, sin, first):
    rows, width = dh.shape
    groups, heads, _ = q.shape
    keys, cols = kv.shape[1], width // 8
    dma, vmem = pltpu.SemaphoreType.DMA, lambda *shape: pltpu.VMEM(shape, BF)
    low = lambda *dims: jax.ShapeDtypeStruct(dims, BF)
    full = lambda *dims: jax.ShapeDtypeStruct(dims, F32)
    inside = pl.BlockSpec(memory_space=pltpu.VMEM)
    pieces = ((heads, cols), (cols, heads), (cols + 32, 2 * HD))
    return pl.pallas_call(
        attn_back_kernel,
        out_shape=[full(rows, width)] + [full(*p) for p in pieces] + [low(rows, width)] + [low(4, 4, *p) for p in pieces],
        in_specs=[ANY] * 5 + [inside] * 13,
        out_specs=[inside] * 4 + [ANY] * 4,
        scratch_shapes=[vmem(4, 4, 2, *p) for p in pieces]
        + [vmem(4, *p) for _ in range(3) for p in pieces]
        + [vmem(4, *p) for p in pieces]
        + [vmem(4, *p) for p in pieces]
        + [
            vmem(2, 8, heads, cols), vmem(width, heads), vmem(4, 8, cols + 32, 2 * HD), vmem(width, rows), vmem(4, heads, rows),
            pltpu.VMEM((keys, rows), F32), pltpu.VMEM((keys, 2 * HD), F32), vmem(heads, rows),
            pltpu.VMEM((4, rows, 2 * HD), F32), vmem(4, keys, 2 * HD), vmem(3, 4, rows, 2 * HD), pltpu.VMEM((rows // 4, width), F32),
            dma((6,)), dma((2,)), dma((3, 4)), dma((3, 4)), dma((12,)), dma((12,)), dma((12, 4)), dma((12, 4)), dma((3, 3)), dma((3, 4)),
        ],
        compiler_params=pltpu.CompilerParams(collective_id=3, has_side_effects=True, vmem_limit_bytes=63 * 2**20),
        name="attn_back",
    )(wo, wq, wkv, mo, dh_full, q, o, kv, lse, dh, a1, x, r1, gain2, gains, cos, sin, first)[:5]


def rope_tables(segments, rows, row0):
    own = lax.dynamic_slice_in_dim(segments, row0, rows)
    first = jnp.sum((segments[:, None] < own[None, :]).astype(jnp.int32), axis=0)
    index = jnp.arange(rows, dtype=jnp.int32) + row0
    freq = jnp.exp(jnp.arange(HD // 2, dtype=F32) * (-2.0 * math.log(10000.0) / HD))
    angle = freq[:, None] * (index - first).astype(F32)[None, :]
    cos, sin = jnp.cos(angle), jnp.sin(angle)
    return jnp.concatenate([cos, cos], 0), jnp.concatenate([sin, sin], 0), first[None, :]


def body(tokens, segments, attn_gain, w_query, w_key, w_value, w_out, mlp_gain, w_gate, w_up, w_down, cotangent):
    rows, width = tokens.shape
    cols, hidden = w_gate.shape
    t = lax.axis_index("tensor")
    cos, sin, first = rope_tables(segments, rows, t * rows)
    extra = jnp.concatenate([attn_gain.reshape(2, -1), mlp_gain.reshape(2, -1), jnp.zeros((28, 2 * HD), BF)], 0)
    w_kv = jnp.concatenate([jnp.concatenate([w_key, w_value], 1), extra], 0)
    h, a1, r1, r2, gains, q, o, lse, kv, wkv, wq, wo, wg, wu, wd, a2, ct = attn_gather(w_kv, w_query, w_out, w_gate, w_up, w_down, cotangent, tokens, cos, sin, first)
    wkv, wq, wo = wkv.reshape(4, 8, -1, 2 * HD), wq.reshape(4, width, -1), wo.reshape(8, 4, -1, cols)
    dh, dhb, gain2_part, mo, mo_near, gg, gu, gd = mlp(a2, ct, wg.reshape(width, -1), wu.reshape(width, -1), wd.reshape(8, hidden, -1), h, r2, gains)
    grad_tokens, go, gq, gkv, mo_far = attn_back(wo, wq, wkv, mo, dh, q, o, kv, lse, dhb, a1, tokens, r1, gain2_part, gains, cos, sin, first)
    mo_own = lax.dynamic_index_in_dim(mo, t, 0, keepdims=False)
    output = (h + mo_own.astype(F32) + mo_near[0].astype(F32) + mo_near[1].astype(F32) + mo_far.astype(F32)).astype(BF)
    gain_grads = gkv[cols : cols + 4].reshape(2, -1)
    gkv = gkv[:cols]
    return (output, grad_tokens, gain_grads[0], gq, gkv[:, :HD], gkv[:, HD:], go, gain_grads[1], gg.astype(F32), gu.astype(F32), gd.astype(F32))


def body_plain(tokens, segments, attn_gain, w_query, w_key, w_value, w_out, mlp_gain, w_gate, w_up, w_down, cotangent):
    rows, width = tokens.shape
    hidden = w_gate.shape[1]
    nt = lax.axis_size("tensor")
    row0 = lax.axis_index("tensor") * rows
    cos, sin, first = rope_tables(segments, rows, row0)
    row0_s = row0[None].astype(jnp.int32)

    gain1 = lax.all_gather(attn_gain, "dp", axis=0, tiled=True).astype(F32)
    gain2 = lax.all_gather(mlp_gain, "dp", axis=0, tiled=True).astype(F32)
    w_kv = jnp.concatenate([w_key, w_value], 1)
    full = lambda w, axis: lax.all_gather(lax.all_gather(w, "dp", axis=axis, tiled=True), "tensor", axis=0)
    wq = full(w_query, 0)
    wkv = full(w_kv, 0)
    wo = full(w_out, 1).reshape(width, width)
    wg = lax.all_gather(w_gate, "dp", axis=0, tiled=True)
    wu = lax.all_gather(w_up, "dp", axis=0, tiled=True)
    wd = lax.all_gather(w_down, "dp", axis=1, tiled=True)

    x = tokens.astype(F32)
    n1, r1 = rms_forward(x, gain1)
    a1 = n1.astype(BF)
    kv = jnp.einsum("rd,gdc->grc", a1, wkv, preferred_element_type=F32)
    cos_r, sin_r = cos.T, sin.T
    k = kv[..., :HD]
    k = k * cos_r + jnp.concatenate([-k[..., HD // 2 :], k[..., : HD // 2]], -1) * sin_r
    kv = jnp.concatenate([k, kv[..., HD:]], -1).astype(BF)
    kv = lax.all_gather(kv, "tensor", axis=1, tiled=True)
    o, q, lse = attn_forward(row0_s, a1, wq, kv, cos, sin, first)
    o2 = o.reshape(-1, rows)
    h = x + dot_tn(o2, wo)

    n2, r2 = rms_forward(h, gain2)
    a2 = lax.all_gather(n2.astype(BF), "tensor", axis=0, tiled=True)
    cot = lax.all_gather(cotangent, "tensor", axis=0, tiled=True)
    output, da2, gg, gu, gd = mlp_plain(h, a2, cot, wg, wu, wd)
    dres, gain2_part = rms_backward(h, r2, gain2, da2)
    dh = cotangent.astype(F32) + dres
    dhb = dh.astype(BF)

    do = dot_nt(wo, dhb).astype(BF).reshape(o.shape)
    go_part = dot_nn(o2, dhb)
    dq, dkv = attn_backward(row0_s, q, kv, do, o, lse, cos, sin, first)
    groups = dkv.shape[0]
    dkv = lax.psum_scatter(dkv.astype(BF), "tensor", scatter_dimension=1, tiled=True).astype(F32)
    dk = dkv[..., :HD]
    ws = dk * sin_r
    dk = dk * cos_r + jnp.concatenate([ws[..., HD // 2 :], -ws[..., : HD // 2]], -1)
    dkv = jnp.concatenate([dk, dkv[..., HD:]], -1).astype(BF)
    gq_part = jnp.einsum("rd,gcr->gdc", a1, dq, preferred_element_type=F32)
    gkv_part = jnp.einsum("rd,grc->gdc", a1, dkv, preferred_element_type=F32)
    da1 = jnp.einsum("gcr,gdc->rd", dq, wq, preferred_element_type=F32) + jnp.einsum("grc,gdc->rd", dkv, wkv, preferred_element_type=F32)
    din, gain1_part = rms_backward(x, r1, gain1, da1)
    grad_tokens = dh + din

    def home_all(v, dim):
        return lax.psum_scatter(home(v, dim + 1), "tensor", scatter_dimension=0, tiled=False).astype(F32)

    gq = home_all(gq_part, 0)
    gkv = home_all(gkv_part, 0)
    go = home_all(go_part.reshape(nt, -1, width), 1)
    gains = lax.psum_scatter(jnp.stack([gain1_part, gain2_part]), "dp", scatter_dimension=1, tiled=True)
    gains = lax.psum(gains, "tensor")
    return (output, grad_tokens, gains[0], gq, gkv[:, :HD], gkv[:, HD:], go, gains[1], gg, gu, gd)


def solution(mesh):
    rows, block = P(("dp", "tensor"), None), P("dp", "tensor")
    turned, line = P("tensor", "dp"), P("dp")
    return jax.shard_map(
        body if (mesh.shape["dp"], mesh.shape["tensor"]) == (8, 4) else body_plain,
        mesh=mesh,
        in_specs=(rows, line, line, block, block, block, turned, line, block, block, turned, rows),
        out_specs=(rows, rows, line, block, block, block, turned, line, block, block, turned),
        check_vma=False,
    )
```

```python
import functools
import math

import jax
import jax.numpy as jnp
from jax import lax
from jax.experimental import pallas as pl
from jax.experimental.pallas import tpu as pltpu
from jax.sharding import PartitionSpec as P

HD = 64
RATIO = 8
EPSILON = 1e-05
MASKED = -1e30
BF = jnp.bfloat16
F32 = jnp.float32


def dot_nn(left, right):
    return lax.dot_general(left, right, (((1,), (0,)), ((), ())), preferred_element_type=F32)


def dot_nt(left, right):
    return lax.dot_general(left, right, (((1,), (1,)), ((), ())), preferred_element_type=F32)


def dot_tn(left, right):
    return lax.dot_general(left, right, (((0,), (0,)), ((), ())), preferred_element_type=F32)


def rms_forward(values_in, gain_row):
    factor = lax.rsqrt(jnp.mean(values_in * values_in, axis=-1, keepdims=True) + EPSILON)
    return (values_in * factor * gain_row, factor)


def rms_backward(values_in, factor, gain_row, gradient):
    scaled = gain_row * gradient
    grad_gain = jnp.sum(gradient * values_in * factor, axis=0)
    grad_input = factor * scaled - values_in * (factor * factor * factor) * jnp.mean(
        scaled * values_in, axis=-1, keepdims=True
    )
    return (grad_input, grad_gain)


def rope_t(u, cos, sin):
    half = HD // 2
    return u * cos + jnp.concatenate([-u[half:], u[:half]], 0) * sin


def rope_back_t(w, cos, sin):
    half = HD // 2
    ws = w * sin
    return w * cos + jnp.concatenate([ws[half:], -ws[:half]], 0)


def bias_of(first, row0, keys, rows):
    key = lax.broadcasted_iota(jnp.int32, (keys, rows), 0)
    row = lax.broadcasted_iota(jnp.int32, (keys, rows), 1) + row0
    return jnp.where((key <= row) & (key >= first), 0.0, MASKED).astype(F32)


def attn_forward_kernel(row0_ref, a1_ref, wq_ref, kv_ref, cos_ref, sin_ref, first_ref, o_ref, q_ref, lse_ref, bias_ref, s_ref, vt_ref):
    keys, rows = bias_ref.shape

    @pl.when(pl.program_id(0) == 0)
    def _():
        bias_ref[...] = bias_of(first_ref[...], row0_ref[0], keys, rows)

    kv = kv_ref[0]
    kvt = kv.T
    vt_ref[...] = jnp.concatenate([kvt[HD:], jnp.ones((16, keys), BF)], 0)
    qt = dot_nn(a1_ref[...], wq_ref[0]).T
    cos, sin = cos_ref[...], sin_ref[...]
    for h in range(RATIO):
        q = (rope_t(qt[h * HD : (h + 1) * HD], cos, sin) * HD ** (-0.5)).astype(BF)
        q_ref[0, h * HD : (h + 1) * HD] = q
        s_ref[...] = dot_nn(kv, jnp.concatenate([q, jnp.zeros_like(q)], 0)) + bias_ref[...]
        peak = jnp.max(s_ref[...], axis=0, keepdims=True)
        e = jnp.exp(s_ref[...] - peak).astype(BF)
        ot = dot_nn(vt_ref[...], e)
        total = ot[HD : HD + 1]
        o_ref[0, h * HD : (h + 1) * HD] = (ot[:HD] / total).astype(BF)
        lse_ref[0, h : h + 1] = peak + jnp.log(total)


def attn_backward_kernel(row0_ref, q_ref, kv_ref, do_ref, o_ref, lse_ref, cos_ref, sin_ref, first_ref, dq_ref, dkv_ref, bias_ref, acc_ref):
    keys, rows = bias_ref.shape

    @pl.when(pl.program_id(0) == 0)
    def _():
        bias_ref[...] = bias_of(first_ref[...], row0_ref[0], keys, rows)

    kv = kv_ref[0]
    kt = kv.T[:HD]
    cos, sin = cos_ref[...], sin_ref[...]
    for h in range(RATIO):
        part = slice(h * HD, (h + 1) * HD)
        q, do, o = q_ref[0, part], do_ref[0, part], o_ref[0, part]
        qz = jnp.concatenate([q, jnp.zeros_like(q)], 0)
        doz = jnp.concatenate([jnp.zeros_like(do), do], 0)
        delta = jnp.sum(do.astype(F32) * o.astype(F32), axis=0, keepdims=True)
        p = jnp.exp(dot_nn(kv, qz) + bias_ref[...] - lse_ref[0, h : h + 1])
        ds = (p * (dot_nn(kv, doz) - delta)).astype(BF)
        grad = dot_nt(ds, qz) + dot_nt(p.astype(BF), doz)
        if h == 0:
            acc_ref[...] = grad
        else:
            acc_ref[...] += grad
        dq = dot_nn(kt, ds) * HD ** (-0.5)
        dq_ref[0, part] = rope_back_t(dq, cos, sin).astype(BF)
    dkv_ref[0] = acc_ref[...]


def params():
    return pltpu.CompilerParams(vmem_limit_bytes=56 * 2**20)


def attn_forward(row0, a1, wq, kv, cos, sin, first):
    groups, width, cols = wq.shape
    rows, keys = a1.shape[0], kv.shape[1]
    whole = lambda *shape: pl.BlockSpec(shape, lambda i: (0,) * len(shape))
    part = lambda *shape: pl.BlockSpec((1,) + shape, lambda i: (i,) + (0,) * len(shape))
    return pl.pallas_call(
        attn_forward_kernel,
        grid=(groups,),
        in_specs=[pl.BlockSpec(memory_space=pltpu.SMEM), whole(rows, width), part(width, cols), part(keys, 2 * HD), whole(HD, rows), whole(HD, rows), whole(1, rows)],
        out_specs=[part(cols, rows), part(cols, rows), part(RATIO, rows)],
        out_shape=[jax.ShapeDtypeStruct((groups, cols, rows), BF), jax.ShapeDtypeStruct((groups, cols, rows), BF), jax.ShapeDtypeStruct((groups, RATIO, rows), F32)],
        scratch_shapes=[pltpu.VMEM((keys, rows), F32), pltpu.VMEM((keys, rows), F32), pltpu.VMEM((HD + 16, keys), BF)],
        compiler_params=params(),
        name="attn_forward",
    )(row0, a1, wq, kv, cos, sin, first)


def attn_backward(row0, q, kv, do, o, lse, cos, sin, first):
    groups, cols, rows = q.shape
    keys = kv.shape[1]
    whole = lambda *shape: pl.BlockSpec(shape, lambda i: (0,) * len(shape))
    part = lambda *shape: pl.BlockSpec((1,) + shape, lambda i: (i,) + (0,) * len(shape))
    return pl.pallas_call(
        attn_backward_kernel,
        grid=(groups,),
        in_specs=[pl.BlockSpec(memory_space=pltpu.SMEM), part(cols, rows), part(keys, 2 * HD), part(cols, rows), part(cols, rows), part(RATIO, rows), whole(HD, rows), whole(HD, rows), whole(1, rows)],
        out_specs=[part(cols, rows), part(keys, 2 * HD)],
        out_shape=[jax.ShapeDtypeStruct((groups, cols, rows), BF), jax.ShapeDtypeStruct((groups, keys, 2 * HD), F32)],
        scratch_shapes=[pltpu.VMEM((keys, rows), F32), pltpu.VMEM((keys, 2 * HD), F32)],
        compiler_params=params(),
        name="attn_backward",
    )(row0, q, kv, do, o, lse, cos, sin, first)


MESH = pl.DeviceIdType.MESH
ANY = pl.BlockSpec(memory_space=pl.ANY)


class Place:
    def __init__(self):
        d, self.t = lax.axis_index("dp"), lax.axis_index("tensor")
        self.c, self.p = d % 2, d // 2
        x, y = self.p % 2, self.p // 2
        self.px, self.py, self.pd = self.p + 1 - 2 * x, self.p + 2 - 4 * y, 3 - self.p
        self.across = [self.t + 1 - 2 * (self.t % 2), (self.t + 2) % 4, 3 - self.t]
        self.inner = (self.t == 1) | (self.t == 2)
        self.outer = (self.t == 0) | (self.t == 3)
        inner = self.t * (3 - self.t) // 2
        self.order = [self.t, self.across[0], 2 - self.t // 2, 3 - self.t // 2 * 3]
        self.away = [0, 1, 2 + inner, 3 - inner]

    def at(self, p, c, t):
        return {"dp": p * 2 + c, "tensor": t}

    def x_side(self):
        return self.at(self.px, self.c, self.t)

    def y_side(self):
        return self.at(self.py, self.c, self.t)

    def twin(self):
        return self.at(self.p, 1 - self.c, self.t)

    def line(self, t):
        return self.at(self.p, self.c, t)

    def greet(self):
        barrier = pltpu.get_barrier_semaphore()
        others = [self.x_side(), self.y_side(), self.twin()] + [self.line(t) for t in self.across]
        for other in others:
            pl.semaphore_signal(barrier, inc=1, device_id=other, device_id_type=MESH)
        pl.semaphore_wait(barrier, len(others))


def half_of(ref, part):
    rows = ref.shape[0] // 2
    return ref.at[pl.ds(part * rows, rows)]


def attn_gather_kernel(kv_in, wq_in, wo_in, wg_in, wu_in, wd_in, ct_in, x_ref, cos_ref, sin_ref, first_ref, h_ref, a1_ref, r1_ref, r2_ref, gains_ref, q_ref, o_ref, lse_ref, kv_ref, kv_out, q_out, o_out, g_out, u_out, d_out, a2_all, ct_all, wkv, wq, wo, rows_kv, bias_ref, s_ref, vt_ref, qt_ref, o_rows, a2_ref, z_send, z_recv, send, recv, local, load, kv_send, kv_recv, line_send, line_recv):
    me = Place()
    rows, width = x_ref.shape
    keys, cols = kv_ref.shape[1], width // 8
    me.greet()
    sources = [kv_in, wq_in, wo_in, wg_in, wu_in, wd_in]
    outs = [kv_out, q_out, o_out, g_out, u_out, d_out]

    def piece(k, s, p, c):
        if k == 2:
            return o_out.at[p, c, s]
        return outs[k].at[s, p, c] if k < 2 else outs[k].at[p, c]

    def pair(k, s, c):
        if k == 2:
            return o_out.at[:, c, s]
        if k == 0:
            return kv_out.at[:, :, c]
        return q_out.at[s, :, c] if k == 1 else outs[k].at[:, c]

    def line_push(k, m):
        return copy_to(sources[k], piece(k, me.t, me.p, me.c), z_send.at[k, m - 1], z_recv.at[k, m - 1], me.line(xor4(me.t, m)))

    def line_first(k):
        for m in (1, 2, 3):
            line_push(k, m).start()

    def arrive(k, j):
        line_push(k, me.away[j]).wait_recv()

    def push(k, j, kind):
        s, i = me.order[j], (0, 1 + j, 5 + j, 9, 10, 11)[k]
        part = (lambda p: kv_out.at[:, p, me.c]) if k == 0 else (lambda p: piece(k, s, p, me.c))
        if kind < 2:
            dst = part(me.p)
            src = sources[k] if j == 0 and k > 0 else dst
        elif kind < 4:
            src = dst = half_of(part(me.px if kind == 2 else me.py), kind - 2)
        else:
            src = dst = pair(k, s, me.c)
        to = [me.x_side, me.y_side, me.y_side, me.x_side, me.twin][kind]()
        return copy_to(src, dst, send.at[i, kind], recv.at[i, kind], to)

    def keep(k):
        return pltpu.make_async_copy(sources[k], piece(k, me.t, me.p, me.c), local.at[k])

    def first(k, j):
        if k == 0:
            keep(k).wait()
        elif j == 0:
            keep(k).start()
        push(k, j, 0).start()
        push(k, j, 1).start()

    def second(k, j):
        push(k, j, 0).wait_recv()
        push(k, j, 2).start()
        push(k, j, 1).wait_recv()
        push(k, j, 3).start()

    def third(k, j):
        push(k, j, 2).wait_recv()
        push(k, j, 3).wait_recv()
        if j == 0 and k > 0:
            keep(k).wait()
        push(k, j, 4).start()

    def last(k, j):
        push(k, j, 4).wait_recv()

    def step(n, k, action):
        t, out, own = me.t, (ct_all, a2_all)[n], (ct_in, a2_ref)[n]
        for way, chunk, can in ((0, t - k + 1, (t < 3) & (t - k + 1 >= 0)), (1, t + k - 1, (t > 0) & (t + k - 1 <= 3))):

            @pl.when(can)
            def _():
                src = own if k == 1 else out.at[chunk]
                copy = copy_to(src, out.at[chunk], line_send.at[n, way, k - 1], line_recv.at[n, way, k - 1], me.line(t + 1 - 2 * way))
                copy.start() if action == "start" else copy.wait_send()

    def got(n, k):
        t, out = me.t, (ct_all, a2_all)[n]
        for way, chunk, can in ((0, t - k, t - k >= 0), (1, t + k, t + k <= 3)):

            @pl.when(can)
            def _():
                copy_to(out.at[chunk], out.at[chunk], line_send.at[n, way, k - 1], line_recv.at[n, way, k - 1], me.line(t + 1 - 2 * way)).wait_recv()

    def own_rows(n):
        return pltpu.make_async_copy((ct_in, a2_ref)[n], (ct_all, a2_all)[n].at[me.t], local.at[6 + n])

    kv_load = pltpu.make_async_copy(kv_out, wkv, load.at[0])
    kv_keep = pltpu.make_async_copy(rows_kv, kv_ref, load.at[1])

    def wq_load(j):
        return pltpu.make_async_copy(q_out.at[me.order[j]], wq.at[j % 2], load.at[2 + j % 2])

    def wo_load(j):
        s = me.order[j]
        return pltpu.make_async_copy(o_out.at[:, :, s], wo.at[:, :, pl.ds(pl.multiple_of(s * 2 * cols, cols), 2 * cols)], load.at[4 + j])

    own = pl.ds(pl.multiple_of(me.t * rows, rows), rows)

    def kv_push(m, g):
        part = rows_kv.at[g, own]
        return copy_to(part, part, kv_send.at[m - 1, g], kv_recv.at[m - 1, g], me.line(xor4(me.t, m)))

    def gain(n):
        parts = [wkv[0, d // 2, d % 2, cols + 2 * n + e : cols + 2 * n + e + 1] for d in range(8) for e in range(2)]
        return jnp.concatenate(parts, 1).astype(F32)

    def norm(value):
        return lax.rsqrt(jnp.mean(value * value, axis=-1, keepdims=True) + EPSILON)

    def project_keys():
        x = x_ref[...].astype(F32)
        r1_ref[...] = norm(x)
        gains_ref[0:1] = gain(0)
        gains_ref[1:2] = gain(1)
        a1_ref[...] = (x * r1_ref[...] * gains_ref[0:1]).astype(BF)
        for m in (1, 2, 3, 0):
            g = xor4(me.t, m)
            weights = wkv[g, :, :, :cols].reshape(width, 2 * HD)
            kvt = dot_nn(a1_ref[...], weights).T
            kvt = jnp.concatenate([rope_t(kvt[:HD], cos_ref[...], sin_ref[...]), kvt[HD:]], 0).astype(BF)
            rows_kv[g, own] = kvt.T
            if m > 0:
                kv_push(m, g).start()
        for more in (1, 2, 3):
            for m in (1, 2, 3):
                kv_push(m, xor4(me.t, m ^ more)).start()

    def attend(j, part):
        g = me.order[j]
        if part == 0:
            for m in (1, 2, 3):
                kv_push(m, g).wait_recv()
            qt_ref[...] = dot_nn(a1_ref[...], wq[j % 2].reshape(width, -1)).T
            vt_ref[...] = jnp.concatenate([rows_kv[g].T[HD:], jnp.ones((16, keys), BF)], 0)
        cos, sin = cos_ref[...], sin_ref[...]

        def head(h, _):
            part = pl.ds(pl.multiple_of(h * HD, HD), HD)
            q = (rope_t(qt_ref[part], cos, sin) * HD ** (-0.5)).astype(BF)
            q_ref[g, part] = q
            s_ref[...] = dot_nn(rows_kv[g], jnp.concatenate([q, jnp.zeros_like(q)], 0)) + bias_ref[...]
            peak = jnp.max(s_ref[...], axis=0, keepdims=True)
            e = jnp.exp(s_ref[...] - peak).astype(BF)
            ot = dot_nn(vt_ref[...], e)
            total = ot[HD : HD + 1]
            o_ref[g, part] = (ot[:HD] / total).astype(BF)
            lse_ref[g, pl.ds(h, 1)] = peak + jnp.log(total)
            return 0

        lax.fori_loop(part * RATIO // 2, (part + 1) * RATIO // 2, head, 0, unroll=2)
        if part == 1:
            o_rows[:, pl.ds(pl.multiple_of(g * 2 * cols, cols), 2 * cols)] = o_ref[g].T

    def mix():
        for d in range(8):
            part = slice(d * cols, (d + 1) * cols)
            h_ref[:, part] = x_ref[:, part].astype(F32) + dot_nn(o_rows[...], wo[d // 2, d % 2])
        h = h_ref[...]
        r2_ref[...] = norm(h)
        a2_ref[...] = (h * r2_ref[...] * gains_ref[1:2]).astype(BF)

    KV, Q, O, G, U, D = range(6)
    keep(KV).start()
    line_first(KV)
    first(Q, 0)
    own_rows(0).start()
    arrive(KV, 1)
    line_first(Q)
    arrive(KV, 2)
    arrive(KV, 3)
    first(KV, 0)
    first(O, 0)
    bias_ref[...] = bias_of(first_ref[...], me.t * rows, keys, rows)
    second(KV, 0)
    second(Q, 0)
    third(KV, 0)
    arrive(Q, 1)
    first(Q, 1)
    last(KV, 0)
    kv_load.start()
    second(O, 0)
    kv_load.wait()
    project_keys()
    line_first(O)
    arrive(Q, 2)
    first(Q, 2)
    third(Q, 0)
    second(Q, 1)
    arrive(Q, 3)
    first(Q, 3)
    last(Q, 0)
    wq_load(0).start()
    third(Q, 1)
    third(O, 0)
    second(Q, 2)
    arrive(O, 1)
    step(0, 1, "start")
    first(O, 1)
    wq_load(0).wait()
    attend(0, 0)
    third(Q, 2)
    last(Q, 1)
    wq_load(1).start()
    second(Q, 3)
    arrive(O, 2)
    first(O, 2)
    attend(0, 1)
    third(Q, 3)
    second(O, 1)
    arrive(O, 3)
    first(O, 3)
    wq_load(1).wait()
    attend(1, 0)
    last(Q, 2)
    wq_load(2).start()
    third(O, 1)
    second(O, 2)
    got(0, 1)
    step(0, 2, "start")
    attend(1, 1)
    last(Q, 3)
    wq_load(3).start()
    second(O, 3)
    first(G, 0)
    third(O, 2)
    wq_load(2).wait()
    attend(2, 0)
    third(O, 3)
    last(O, 0)
    wo_load(0).start()
    last(O, 1)
    wo_load(1).start()
    attend(2, 1)
    last(O, 2)
    wo_load(2).start()
    last(O, 3)
    wo_load(3).start()
    first(U, 0)
    wq_load(3).wait()
    attend(3, 0)
    attend(3, 1)
    for j in range(4):
        wo_load(j).wait()
    mix()
    own_rows(1).start()
    step(1, 1, "start")
    got(0, 2)
    step(0, 3, "start")
    kv_keep.start()
    second(G, 0)
    first(D, 0)
    third(G, 0)
    second(U, 0)
    got(1, 1)
    step(1, 2, "start")
    third(U, 0)
    second(D, 0)
    third(D, 0)
    for k in (G, U, D):
        last(k, 0)
    got(0, 3)
    got(1, 2)
    kv_keep.wait()
    for n in range(2):
        own_rows(n).wait()
        for k in (1, 2, 3)[: 3 - n]:
            step(n, k, "wait")
    for j in (1, 2, 3):
        for g in range(4):
            kv_push(j, g).wait_send()
        for k in (KV, Q, O):
            line_push(k, j).wait_send()
    for k in range(6):
        for j in range(4 if k in (Q, O) else 1):
            for kind in range(5):
                push(k, j, kind).wait_send()


def attn_gather(kv, wq, wo, wg, wu, wd, ct, x, cos, sin, first):
    rows, width = x.shape
    heads, cols, keys = wq.shape[1], wq.shape[0], 4 * rows
    dma, vmem = pltpu.SemaphoreType.DMA, lambda *shape: pltpu.VMEM(shape, BF)
    low = lambda *dims: jax.ShapeDtypeStruct(dims, BF)
    full = lambda *dims: jax.ShapeDtypeStruct(dims, F32)
    inside = pl.BlockSpec(memory_space=pltpu.VMEM)
    return pl.pallas_call(
        attn_gather_kernel,
        out_shape=[
            full(rows, width), low(rows, width), full(rows, 1), full(rows, 1), full(2, width), low(4, heads, rows), low(4, heads, rows), full(4, RATIO, rows),
            low(4, keys, 2 * HD), low(4, 4, 2, *kv.shape), low(4, 4, 2, *wq.shape), low(4, 2, 4, *wo.shape),
            low(4, 2, *wg.shape), low(4, 2, *wu.shape), low(4, 2, *wd.shape), low(4, rows, width), low(4, rows, width),
        ],
        in_specs=[ANY] * 7 + [inside] * 4,
        out_specs=[inside] * 8 + [ANY] * 9,
        scratch_shapes=[
            vmem(4, 4, 2, *kv.shape), vmem(2, 4, 2, cols, heads), vmem(4, 2, width, cols), vmem(4, keys, 2 * HD),
            pltpu.VMEM((keys, rows), F32), pltpu.VMEM((keys, rows), F32), vmem(HD + 16, keys), pltpu.VMEM((heads, rows), F32), vmem(rows, width), vmem(rows, width),
            dma((3, 3)), dma((3, 3)), dma((12, 5)), dma((12, 5)), dma((8,)), dma((8,)), dma((3, 4)), dma((3, 4)), dma((2, 2, 3)), dma((2, 2, 3)),
        ],
        compiler_params=pltpu.CompilerParams(collective_id=1, has_side_effects=True, vmem_limit_bytes=56 * 2**20),
        name="attn_gather",
    )(kv, wq, wo, wg, wu, wd, ct, x, cos, sin, first)


def xor4(a, m):
    return (a // 2 + m // 2) % 2 * 2 + (a % 2 + m % 2) % 2


def copy_to(src, dst, send_sem, recv_sem, to):
    return pltpu.make_async_remote_copy(src, dst, send_sem, recv_sem, device_id=to, device_id_type=MESH)


def add_low(left, right):
    return (left.astype(F32) + right.astype(F32)).astype(BF)


def mlp_kernel(a2_old, ct_in, wg_in, wu_in, wd_in, h_in, r2_ref, gain_ref, a2_in, da2_out, dhb_out, gain_out, mo_out, mo_got, gg_out, gu_out, gd_out, twin_g, twin_u, twin_d, wg, wu, wd, a2_buf, ct_buf, mo_buf, a2_col, ct_col, zt, dg, du, out_buf, in_buf, diag_gu, x_gu, y_gu, diag_d, x_d, y_d, stage_gu, stage_d, h_buf, load, store, line_send, line_recv, a2_send, a2_recv, mo_send, mo_recv, twin_send, twin_recv, send, recv, stage_sem):
    me = Place()
    rows, width = da2_out.shape
    hidden = wg.shape[1]
    cols = width // 8
    weights = [pltpu.make_async_copy(wg_in, wg, load.at[4]), pltpu.make_async_copy(wu_in, wu, load.at[5])]
    weights += [pltpu.make_async_copy(wd_in.at[d], wd.at[:, pl.ds(d * cols, cols)], load.at[6 + d]) for d in range(8)]
    for copy in weights:
        copy.start()

    def away(j):
        return 2 * (1 - j % 2) + (j % 2 + j // 2) % 2

    a2_push = copy_to(a2_in.at[xor4(me.t, 2)], a2_in.at[xor4(me.t, 2)], a2_send.at[0], a2_recv.at[0], me.line(xor4(me.t, 1)))

    def chunk_load(j, slot):
        s = xor4(me.t, away(j))
        return pltpu.make_async_copy(a2_in.at[s], a2_buf.at[slot], load.at[slot]), pltpu.make_async_copy(ct_in.at[s], ct_buf.at[slot], load.at[2 + slot])

    near, cross, both = in_buf.at[0], in_buf.at[1], in_buf.at[pl.ds(2, 2)]

    def near_send():
        return copy_to(out_buf.at[0], near, line_send.at[0], line_recv.at[0], me.line(xor4(me.t, 1)))

    def both_send(m):
        s = xor4(me.t, m)
        return copy_to(out_buf.at[m - 1], both.at[s % 2], line_send.at[m - 1], line_recv.at[2 + s % 2], me.line(xor4(me.t, 1)))

    def cross_send(m):
        return copy_to(out_buf.at[m - 1], cross, line_send.at[m - 1], line_recv.at[1], me.line(xor4(me.t, m)))

    def cross_add(m):
        s = xor4(me.t, m)
        copy_to(both.at[s % 2], both.at[s % 2], line_send.at[0], line_recv.at[2 + s % 2], me.line(xor4(me.t, 1))).wait_recv()
        out_buf[m - 1] = add_low(out_buf[m - 1], both[s % 2])
        cross_send(m).start()

    def mo_store(j, slot):
        return pltpu.make_async_copy(mo_buf.at[slot], mo_out.at[xor4(me.t, away(j))], store.at[slot])

    for copy in chunk_load(0, 0):
        copy.start()
    me.greet()

    @pl.when(me.inner)
    def _():
        a2_push.start()

    def chunk(j, _):
        slot = j % 2

        for copy in chunk_load(j, slot):
            copy.wait()
        where = pl.multiple_of(xor4(me.t, away(j)) * rows, rows)

        @pl.when(j == 0)
        def _():
            weights[0].wait()

        g = dot_nn(a2_buf[slot], wg[...])

        @pl.when(j == 0)
        def _():
            for copy in weights[1:]:
                copy.wait()

        u = dot_nn(a2_buf[slot], wu[...])
        dz = dot_nt(ct_buf[slot], wd[...])
        sig = 1.0 / (1.0 + jnp.exp(-g))
        act = g * sig
        z = (act * u).astype(BF)
        zt[:, pl.ds(where, rows)] = z.T
        dg_now = (dz * u * (sig * (1.0 + g * (1.0 - sig)))).astype(BF)
        du_now = (dz * act).astype(BF)
        dg[pl.ds(where, rows)] = dg_now
        du[pl.ds(where, rows)] = du_now
        part = dot_nt(dg_now, wg[...]) + dot_nt(du_now, wu[...])

        @pl.when(j < 3)
        def _():
            out_buf[away(j) - 1] = part.astype(BF)

        @pl.when((j == 1) & me.inner)
        def _():
            near_send().start()

        for at, m in ((0, 2), (2, 3)):

            @pl.when((j == at) & me.outer)
            def _():
                both_send(m).start()

        @pl.when(j == 3)
        def _():
            da2_out[...] = part

        @pl.when((j == 1) & me.outer)
        def _():
            a2_push.wait_recv()

        @pl.when(j < 3)
        def _():
            for copy in chunk_load(j + 1, 1 - slot):
                copy.start()

        @pl.when(j >= 2)
        def _():
            mo_store(j - 2, slot).wait()

        mo_buf[slot] = dot_nn(z, wd[...]).astype(BF)
        mo_store(j, slot).start()
        return 0

    lax.fori_loop(0, 4, chunk, 0)
    mo_store(2, 0).wait()
    mo_store(3, 1).wait()

    def mo_push(m):
        return copy_to(mo_out.at[xor4(me.t, m)], mo_got.at[m - 1], mo_send.at[m - 1], mo_recv.at[m - 1], me.line(xor4(me.t, m)))

    @pl.when(me.inner)
    def _():
        cross_add(3)

    def owner(i):
        return xor4(me.p, 3 - i % 4) * 2 + (1 - me.c + i // 4) % 2

    def tile_load(i, slot):
        at = pl.ds(pl.multiple_of(owner(i) * cols, cols), cols)
        return pltpu.make_async_copy(a2_in.at[:, :, at], a2_col.at[slot], load.at[slot]), pltpu.make_async_copy(ct_in.at[:, :, at], ct_col.at[slot], load.at[2 + slot])

    def piece(k, p, c):
        at = pl.ds(pl.multiple_of((p * 2 + c) * cols, cols), cols)
        return (wg, wu)[k].at[at] if k < 2 else wd.at[:, at]

    twins = [twin_g, twin_u, twin_d]

    def twin_push(k, i):
        p = xor4(me.p, 3 - i)
        return copy_to(piece(k, p, 1 - me.c), twins[k].at[p], twin_send.at[k, i], twin_recv.at[k, i], me.twin())

    diag = [diag_gu.at[0], diag_gu.at[1], diag_d]
    from_x = [x_gu.at[0], x_gu.at[1], x_d]
    from_y = [y_gu.at[0], y_gu.at[1], y_d]
    stage = [stage_gu.at[0], stage_gu.at[1], stage_d]

    def side(k, kind):
        if kind < 2:
            src, dst = half_of(piece(k, me.pd, me.c), kind), half_of(diag[k], kind)
        else:
            src, dst = (piece(k, me.px, me.c), from_x[k]) if kind == 2 else (piece(k, me.py, me.c), from_y[k])
        return copy_to(src, dst, send.at[k, kind], recv.at[k, kind], me.x_side() if kind % 2 == 0 else me.y_side())

    def fetch(k, p):
        return pltpu.make_async_copy(twins[k].at[p], stage[k], stage_sem.at[k])

    for copy in tile_load(0, 0):
        copy.start()

    def tile(i, _):
        slot = i % 2

        @pl.when(i < 7)
        def _():
            for copy in tile_load(i + 1, 1 - slot):
                copy.start()

        for copy in tile_load(i, slot):
            copy.wait()
        at = pl.ds(pl.multiple_of(owner(i) * cols, cols), cols)
        a2t = a2_col[slot].reshape(4 * rows, cols).T
        wg[at] = dot_nn(a2t, dg[...]).astype(BF)
        wu[at] = dot_nn(a2t, du[...]).astype(BF)
        wd[:, at] = dot_nn(zt[...], ct_col[slot].reshape(4 * rows, cols)).astype(BF)

        @pl.when(i < 4)
        def _():
            for k in range(3):
                twin_push(k, i).start()

        @pl.when(i >= 4)
        def _():
            p = xor4(me.p, 7 - i)
            for k in range(3):
                twin_push(k, i - 4).wait_recv()
                fetch(k, p).start()
            for k in range(3):
                fetch(k, p).wait()
                mine = piece(k, p, me.c)
                mine[...] = add_low(mine[...], stage[k][...])

        @pl.when(i == 4)
        def _():
            for k in range(3):
                side(k, 0).start()
                side(k, 1).start()

        @pl.when((i == 5) & me.inner)
        def _():
            cross_add(2)

        @pl.when((i == 5) & me.outer)
        def _():
            near_send().start()

        @pl.when(i == 5)
        def _():
            for m in (1, 2):
                mo_push(m).start()

        return 0

    lax.fori_loop(0, 8, tile, 0)
    for k in range(3):
        side(k, 1).wait_recv()
        part, extra = half_of(piece(k, me.px, me.c), 1), half_of(diag[k], 1)
        part[...] = add_low(part[...], extra[...])
        side(k, 2).start()
        side(k, 0).wait_recv()
        part, extra = half_of(piece(k, me.py, me.c), 0), half_of(diag[k], 0)
        part[...] = add_low(part[...], extra[...])
        side(k, 3).start()
    own_ct = pltpu.make_async_copy(ct_in.at[me.t], ct_buf.at[0], load.at[2])
    own_ct.start()

    def h_load(n):
        return pltpu.make_async_copy(h_in.at[pl.ds(n * h_buf.shape[0], h_buf.shape[0])], h_buf, load.at[0])

    h_load(0).start()
    results = []
    for k in range(3):
        side(k, 2).wait_recv()
        side(k, 3).wait_recv()
        mine = piece(k, me.p, me.c)
        mine[...] = (mine[...].astype(F32) + from_x[k][...].astype(F32) + from_y[k][...].astype(F32)).astype(BF)
        results.append(pltpu.make_async_copy(mine, (gg_out, gu_out, gd_out)[k], stage_sem.at[k]))
        results[-1].start()
    own_ct.wait()
    near_send().wait_recv()
    cross_send(2).wait_recv()
    part_rows = h_buf.shape[0]
    for n in range(rows // part_rows):
        at = slice(n * part_rows, (n + 1) * part_rows)
        h_load(n).wait()
        da2 = da2_out[at] + in_buf[0, at].astype(F32) + in_buf[1, at].astype(F32)
        scaled, h, r2 = gain_ref[1:2] * da2, h_buf[...], r2_ref[at]
        gain = jnp.sum(da2 * h * r2, axis=0, keepdims=True)
        gain_out[...] = gain if n == 0 else gain_out[...] + gain
        dres = r2 * scaled - h * (r2 * r2 * r2) * jnp.mean(scaled * h, axis=-1, keepdims=True)
        if n + 1 < rows // part_rows:
            h_load(n + 1).start()
        dh = ct_buf[0, at].astype(F32) + dres
        da2_out[at] = dh
        ct_buf[1, at] = dh.astype(BF)
    results.append(pltpu.make_async_copy(ct_buf.at[1], dhb_out, load.at[1]))
    results[-1].start()
    for copy in results:
        copy.wait()
    for m in (1, 2):
        mo_push(m).wait()

    @pl.when(me.inner)
    def _():
        a2_push.wait_send()

    near_send().wait_send()
    for m in (2, 3):
        cross_send(m).wait_send()
    for k in range(3):
        for i in range(4):
            twin_push(k, i).wait_send()
            side(k, i).wait_send()


def mlp(a2, ct, wg, wu, wd, h, r2, gain):
    chunks, rows, width = a2.shape
    hidden, cols = wg.shape[1], width // 8
    dma, vmem = pltpu.SemaphoreType.DMA, lambda *shape: pltpu.VMEM(shape, BF)
    shape = lambda *dims: jax.ShapeDtypeStruct(dims, BF)
    full = lambda *dims: jax.ShapeDtypeStruct(dims, F32)
    inside = pl.BlockSpec(memory_space=pltpu.VMEM)
    return pl.pallas_call(
        mlp_kernel,
        out_shape=[shape(4, rows, width), full(rows, width), shape(rows, width), full(1, width), shape(4, rows, width), shape(2, rows, width), shape(cols, hidden), shape(cols, hidden), shape(hidden, cols), shape(4, cols, hidden), shape(4, cols, hidden), shape(4, hidden, cols)],
        in_specs=[ANY] * 6 + [inside] * 2,
        out_specs=[ANY, inside, ANY, inside] + [ANY] * 8,
        input_output_aliases={0: 0},
        scratch_shapes=[
            vmem(width, hidden), vmem(width, hidden), vmem(hidden, width),
            vmem(2, rows, width), vmem(2, rows, width), vmem(2, rows, width),
            vmem(2, 4, rows, cols), vmem(2, 4, rows, cols),
            vmem(hidden, 4 * rows), vmem(4 * rows, hidden), vmem(4 * rows, hidden),
            vmem(3, rows, width), vmem(4, rows, width),
            vmem(2, cols, hidden), vmem(2, cols, hidden), vmem(2, cols, hidden),
            vmem(hidden, cols), vmem(hidden, cols), vmem(hidden, cols),
            vmem(2, cols, hidden), vmem(hidden, cols), pltpu.VMEM((rows // 2, width), F32),
            dma((14,)), dma((2,)), dma((3,)), dma((4,)), dma((1,)), dma((1,)), dma((2,)), dma((2,)), dma((3, 4)), dma((3, 4)), dma((3, 4)), dma((3, 4)), dma((3,)),
        ],
        compiler_params=pltpu.CompilerParams(collective_id=2, has_side_effects=True, vmem_limit_bytes=63 * 2**20),
        name="mlp",
    )(a2, ct, wg, wu, wd, h, r2, gain)[1:9]


def home(v, dim):
    return lax.psum_scatter(v.astype(BF), "dp", scatter_dimension=dim, tiled=True)


def mlp_plain(h, a2, cot, wg, wu, wd):
    g, u = dot_nn(a2, wg), dot_nn(a2, wu)
    sig = jax.nn.sigmoid(g)
    act = g * sig
    z = (act * u).astype(BF)
    scatter = lambda v: lax.psum_scatter(v.astype(BF), "tensor", scatter_dimension=0, tiled=True).astype(F32)
    output = (h + scatter(dot_nn(z, wd))).astype(BF)
    dz = dot_nt(cot, wd)
    dg = (dz * u * (sig * (1.0 + g * (1.0 - sig)))).astype(BF)
    du = (dz * act).astype(BF)
    gd = home(dot_tn(z, cot), 1).astype(F32)
    gg = home(dot_tn(a2, dg), 0).astype(F32)
    gu = home(dot_tn(a2, du), 0).astype(F32)
    da2 = scatter(dot_nt(dg, wg) + dot_nt(du, wu))
    return output, da2, gg, gu, gd


def attn_back_kernel(wo_in, wq_in, wkv_in, mo_in, dh_in, q_ref, o_ref, kv_ref, lse_ref, dh_ref, a1_ref, x_ref, r1_ref, gain2_ref, gains_ref, cos_ref, sin_ref, first_ref, da1_ref, go_ref, gq_ref, gkv_ref, mo_got, twin_o, twin_q, twin_kv, grad_o, grad_q, grad_kv, diag_o, diag_q, diag_kv, x_o, x_q, x_kv, y_o, y_q, y_kv, z_o, z_q, z_kv, stage_o, stage_q, stage_kv, wo, wq, wkv, a1t, do_ref, bias_ref, acc_ref, dqt_ref, dkv_own, dkv_out, dkv_got, dh_buf, load, mo_sem, dkv_send, dkv_recv, twin_send, twin_recv, send, recv, line_send, line_recv):
    me = Place()
    rows, width = dh_ref.shape
    keys, cols = kv_ref.shape[1], width // 8
    head_of = [3 - me.t // 2 * 3, 2 - me.t // 2, xor4(me.t, 1), me.t]

    def wo_load(j):
        return pltpu.make_async_copy(wo_in.at[:, head_of[j]], wo.at[j % 2], load.at[j % 2])

    def wq_load(j):
        return pltpu.make_async_copy(wq_in.at[head_of[j]], wq, load.at[2])

    wkv_load = pltpu.make_async_copy(wkv_in, wkv, load.at[3])
    mo_push = copy_to(mo_in.at[xor4(me.t, 3)], mo_got, mo_sem.at[0], mo_sem.at[1], me.line(xor4(me.t, 3)))
    wo_load(0).start()
    wo_load(1).start()
    wq_load(0).start()
    wkv_load.start()
    me.greet()
    mo_push.start()
    a1t[...] = a1_ref[...].T
    bias_ref[...] = bias_of(first_ref[...], me.t * rows, keys, rows)

    grads, twins, diags = [grad_o, grad_q, grad_kv], [twin_o, twin_q, twin_kv], [diag_o, diag_q, diag_kv]
    from_x, from_y, from_z = [x_o, x_q, x_kv], [y_o, y_q, y_kv], [z_o, z_q, z_kv]
    stages = [stage_o, stage_q, stage_kv]

    def twin_push(k, j):
        i = k * 4 + j
        return copy_to(grads[k].at[j, :, 1 - me.c], twins[k].at[j], twin_send.at[i], twin_recv.at[i], me.twin())

    def side(k, j, kind):
        i = k * 4 + j
        piece = lambda p: grads[k].at[j, p, me.c]
        if kind < 2:
            src, dst = half_of(piece(me.pd), kind), half_of(diags[k].at[j], kind)
        else:
            src, dst = (piece(me.px), from_x[k].at[j]) if kind == 2 else (piece(me.py), from_y[k].at[j])
        return copy_to(src, dst, send.at[i, kind], recv.at[i, kind], me.x_side() if kind % 2 == 0 else me.y_side())

    def line_push(k, j, slot):
        to = xor4(me.t, 1) if slot != 1 else head_of[j]
        return copy_to(grads[k].at[j, me.p, me.c], from_z[k].at[slot], line_send.at[k, j], line_recv.at[k, slot], me.line(to))

    def fourth(k, j):
        @pl.when(me.inner)
        def _():
            line_push(k, j, 2 + j).wait_recv()
            mine = grads[k].at[j, me.p, me.c]
            mine[...] = add_low(mine[...], from_z[k][2 + j])
            line_push(k, j, 1).start()

    def first(k, j):
        twin_push(k, j).wait_recv()
        copy = pltpu.make_async_copy(twins[k].at[j], stages[k], load.at[4])
        copy.start()
        copy.wait()
        for p in (me.pd, me.px, me.py, me.p):
            mine = grads[k].at[j, p, me.c]
            mine[...] = add_low(mine[...], stages[k][p])
            if p is me.pd:
                side(k, j, 0).start()
                side(k, j, 1).start()

    def second(k, j):
        for kind, p, to in ((1, me.px, 2), (0, me.py, 3)):
            side(k, j, kind).wait_recv()
            part, extra = half_of(grads[k].at[j, p, me.c], kind), half_of(diags[k].at[j], kind)
            part[...] = add_low(part[...], extra[...])
            side(k, j, to).start()

    def third(k, j):
        side(k, j, 2).wait_recv()
        side(k, j, 3).wait_recv()
        mine = grads[k].at[j, me.p, me.c]
        total = mine[...].astype(F32) + from_x[k][j].astype(F32) + from_y[k][j].astype(F32)
        if j < 3:
            mine[...] = total.astype(BF)
            if j == 2:
                line_push(k, j, 0).start()
            else:

                @pl.when(me.outer)
                def _():
                    line_push(k, j, 2 + j).start()
        else:
            (go_ref, gq_ref, gkv_ref)[k][...] = total

    def out_group(j):
        g = head_of[j]
        wo_load(j).wait()
        do = jnp.zeros((wo.shape[2], rows), F32)
        for d in range(8):
            part = slice(d * cols, (d + 1) * cols)
            do += dot_nt(wo[j % 2, d], dh_ref[:, part])
            grad_o[j, d // 2, d % 2] = dot_nn(o_ref[g], dh_ref[:, part]).astype(BF)
        twin_push(0, j).start()
        do_ref[j] = do.astype(BF)
        if j + 2 < 4:
            wo_load(j + 2).start()

    def dkv_push(j, m):
        z, s = xor4(me.t, m), head_of[j]
        src = dkv_out.at[j, pl.ds(pl.multiple_of(z * rows, rows), rows)]
        return copy_to(src, dkv_got.at[m - 1, s], dkv_send.at[m - 1, j], dkv_recv.at[m - 1, s], me.line(z))

    def back_group(j):
        g = head_of[j]
        kv = kv_ref[g]
        kt = kv.T[:HD]
        cos, sin = cos_ref[...], sin_ref[...]

        def head(h, _):
            part = pl.ds(pl.multiple_of(h * HD, HD), HD)
            q, do, o = q_ref[g, part], do_ref[j, part], o_ref[g, part]
            qz = jnp.concatenate([q, jnp.zeros_like(q)], 0)
            doz = jnp.concatenate([jnp.zeros_like(do), do], 0)
            delta = jnp.sum(do.astype(F32) * o.astype(F32), axis=0, keepdims=True)
            p = jnp.exp(dot_nn(kv, qz) + bias_ref[...] - lse_ref[g, pl.ds(h, 1)])
            ds = (p * (dot_nn(kv, doz) - delta)).astype(BF)
            acc_ref[...] += dot_nt(ds, qz) + dot_nt(p.astype(BF), doz)
            dqt_ref[part] = rope_back_t(dot_nn(kt, ds) * HD ** (-0.5), cos, sin).astype(BF)
            return 0

        acc_ref[...] = jnp.zeros_like(acc_ref)
        lax.fori_loop(0, RATIO, head, 0, unroll=2)
        dkv_out[j] = acc_ref[...].astype(BF)
        dkv_own[j] = acc_ref[pl.ds(pl.multiple_of(me.t * rows, rows), rows)]
        for m in (3, 2, 1):
            dkv_push(j, m).start()
        for d in range(8):
            grad_q[j, d // 2, d % 2] = dot_nt(a1t[d * cols : (d + 1) * cols], dqt_ref[...]).astype(BF)
        twin_push(1, j).start()
        wq_load(j).wait()
        part = dot_nt(dqt_ref[...].T, wq[...])
        if j == 0:
            da1_ref[...] = part
        else:
            da1_ref[...] += part
        if j < 3:
            wq_load(j + 1).start()

    def keys_back():
        wkv_load.wait()
        turned = []
        for j in range(4):
            total = dkv_own[j]
            for m in (3, 2, 1):
                dkv_push(j, m).wait_recv()
                total += dkv_got[m - 1, head_of[j]].astype(F32)
            total = total.T
            dkvt = jnp.concatenate([rope_back_t(total[:HD], cos_ref[...], sin_ref[...]), total[HD:]], 0)
            turned.append(dkvt.astype(BF))
            da1_ref[...] += dot_nt(dkvt.T.astype(BF), wkv[head_of[j], :, :cols].reshape(width, 2 * HD))
        gain1 = jnp.sum(da1_ref[...] * (x_ref[...].astype(F32) * r1_ref[...]), axis=0, keepdims=True)
        gain2 = gain2_ref[...]
        for j in range(4):
            for d in range(8):
                at = d * cols
                grad_kv[j, d // 2, d % 2, :cols] = dot_nt(a1t[at : at + cols], turned[j]).astype(BF)
                extra = [gain1[:, at : at + 128], gain1[:, at + 128 : at + 256], gain2[:, at : at + 128], gain2[:, at + 128 : at + 256], jnp.zeros((28, 128), F32)]
                grad_kv[j, d // 2, d % 2, cols:] = jnp.concatenate(extra, 0).astype(BF)
            twin_push(2, j).start()

    def dh_load(n):
        return pltpu.make_async_copy(dh_in.at[pl.ds(n * dh_buf.shape[0], dh_buf.shape[0])], dh_buf, load.at[5])

    def norm_back():
        part_rows = dh_buf.shape[0]
        for n in range(rows // part_rows):
            at = slice(n * part_rows, (n + 1) * part_rows)
            scaled, x, r1 = gains_ref[0:1] * da1_ref[at], x_ref[at].astype(F32), r1_ref[at]
            din = r1 * scaled - x * (r1 * r1 * r1) * jnp.mean(scaled * x, axis=-1, keepdims=True)
            dh_load(n).wait()
            da1_ref[at] = dh_buf[...] + din
            if n + 1 < rows // part_rows:
                dh_load(n + 1).start()

    O, Q, KV = range(3)
    dh_load(0).start()
    for j in range(4):
        out_group(j)
    for j in range(4):
        first(O, j)
    second(O, 0)
    second(O, 1)
    back_group(0)
    second(O, 2)
    second(O, 3)
    first(Q, 0)
    third(O, 0)
    back_group(1)
    third(O, 1)
    second(Q, 0)
    first(Q, 1)
    third(O, 2)
    fourth(O, 0)
    back_group(2)
    third(O, 3)
    second(Q, 1)
    first(Q, 2)
    third(Q, 0)
    fourth(O, 1)
    back_group(3)
    second(Q, 2)
    first(Q, 3)
    third(Q, 1)
    fourth(Q, 0)
    keys_back()
    second(Q, 3)
    third(Q, 2)
    fourth(Q, 1)
    for j in range(4):
        first(KV, j)
    norm_back()
    third(Q, 3)
    for j in range(4):
        second(KV, j)
    for j in range(4):
        third(KV, j)
    for j in range(2):
        fourth(KV, j)
    for k in range(3):
        line_push(k, 2, 0).wait()
        line_push(k, 0, 1).wait()
        line_push(k, 1, 1).wait_send()
        total = (go_ref, gq_ref, gkv_ref)[k]
        total[...] += from_z[k][0].astype(F32) + from_z[k][1].astype(F32)
    mo_push.wait()
    for j in range(4):
        for m in (1, 2, 3):
            dkv_push(j, m).wait_send()
        for k in range(3):
            twin_push(k, j).wait_send()
            for kind in range(4):
                side(k, j, kind).wait_send()


def attn_back(wo, wq, wkv, mo, dh_full, q, o, kv, lse, dh, a1, x, r1, gain2, gains, cos, sin, first):
    rows, width = dh.shape
    groups, heads, _ = q.shape
    keys, cols = kv.shape[1], width // 8
    dma, vmem = pltpu.SemaphoreType.DMA, lambda *shape: pltpu.VMEM(shape, BF)
    low = lambda *dims: jax.ShapeDtypeStruct(dims, BF)
    full = lambda *dims: jax.ShapeDtypeStruct(dims, F32)
    inside = pl.BlockSpec(memory_space=pltpu.VMEM)
    pieces = ((heads, cols), (cols, heads), (cols + 32, 2 * HD))
    return pl.pallas_call(
        attn_back_kernel,
        out_shape=[full(rows, width)] + [full(*p) for p in pieces] + [low(rows, width)] + [low(4, 4, *p) for p in pieces],
        in_specs=[ANY] * 5 + [inside] * 13,
        out_specs=[inside] * 4 + [ANY] * 4,
        scratch_shapes=[vmem(4, 4, 2, *p) for p in pieces]
        + [vmem(4, *p) for _ in range(3) for p in pieces]
        + [vmem(4, *p) for p in pieces]
        + [vmem(4, *p) for p in pieces]
        + [
            vmem(2, 8, heads, cols), vmem(width, heads), vmem(4, 8, cols + 32, 2 * HD), vmem(width, rows), vmem(4, heads, rows),
            pltpu.VMEM((keys, rows), F32), pltpu.VMEM((keys, 2 * HD), F32), vmem(heads, rows),
            pltpu.VMEM((4, rows, 2 * HD), F32), vmem(4, keys, 2 * HD), vmem(3, 4, rows, 2 * HD), pltpu.VMEM((rows // 4, width), F32),
            dma((6,)), dma((2,)), dma((3, 4)), dma((3, 4)), dma((12,)), dma((12,)), dma((12, 4)), dma((12, 4)), dma((3, 3)), dma((3, 4)),
        ],
        compiler_params=pltpu.CompilerParams(collective_id=3, has_side_effects=True, vmem_limit_bytes=63 * 2**20),
        name="attn_back",
    )(wo, wq, wkv, mo, dh_full, q, o, kv, lse, dh, a1, x, r1, gain2, gains, cos, sin, first)[:5]


def rope_tables(segments, rows, row0):
    own = lax.dynamic_slice_in_dim(segments, row0, rows)
    first = jnp.sum((segments[:, None] < own[None, :]).astype(jnp.int32), axis=0)
    index = jnp.arange(rows, dtype=jnp.int32) + row0
    freq = jnp.exp(jnp.arange(HD // 2, dtype=F32) * (-2.0 * math.log(10000.0) / HD))
    angle = freq[:, None] * (index - first).astype(F32)[None, :]
    cos, sin = jnp.cos(angle), jnp.sin(angle)
    return jnp.concatenate([cos, cos], 0), jnp.concatenate([sin, sin], 0), first[None, :]


def body(tokens, segments, attn_gain, w_query, w_key, w_value, w_out, mlp_gain, w_gate, w_up, w_down, cotangent):
    rows, width = tokens.shape
    cols, hidden = w_gate.shape
    t = lax.axis_index("tensor")
    cos, sin, first = rope_tables(segments, rows, t * rows)
    extra = jnp.concatenate([attn_gain.reshape(2, -1), mlp_gain.reshape(2, -1), jnp.zeros((28, 2 * HD), BF)], 0)
    w_kv = jnp.concatenate([jnp.concatenate([w_key, w_value], 1), extra], 0)
    h, a1, r1, r2, gains, q, o, lse, kv, wkv, wq, wo, wg, wu, wd, a2, ct = attn_gather(w_kv, w_query, w_out, w_gate, w_up, w_down, cotangent, tokens, cos, sin, first)
    wkv, wq, wo = wkv.reshape(4, 8, -1, 2 * HD), wq.reshape(4, width, -1), wo.reshape(8, 4, -1, cols)
    dh, dhb, gain2_part, mo, mo_near, gg, gu, gd = mlp(a2, ct, wg.reshape(width, -1), wu.reshape(width, -1), wd.reshape(8, hidden, -1), h, r2, gains)
    grad_tokens, go, gq, gkv, mo_far = attn_back(wo, wq, wkv, mo, dh, q, o, kv, lse, dhb, a1, tokens, r1, gain2_part, gains, cos, sin, first)
    mo_own = lax.dynamic_index_in_dim(mo, t, 0, keepdims=False)
    output = (h + mo_own.astype(F32) + mo_near[0].astype(F32) + mo_near[1].astype(F32) + mo_far.astype(F32)).astype(BF)
    gain_grads = gkv[cols : cols + 4].reshape(2, -1)
    gkv = gkv[:cols]
    return (output, grad_tokens, gain_grads[0], gq, gkv[:, :HD], gkv[:, HD:], go, gain_grads[1], gg.astype(F32), gu.astype(F32), gd.astype(F32))


def body_plain(tokens, segments, attn_gain, w_query, w_key, w_value, w_out, mlp_gain, w_gate, w_up, w_down, cotangent):
    rows, width = tokens.shape
    hidden = w_gate.shape[1]
    nt = lax.axis_size("tensor")
    row0 = lax.axis_index("tensor") * rows
    cos, sin, first = rope_tables(segments, rows, row0)
    row0_s = row0[None].astype(jnp.int32)

    gain1 = lax.all_gather(attn_gain, "dp", axis=0, tiled=True).astype(F32)
    gain2 = lax.all_gather(mlp_gain, "dp", axis=0, tiled=True).astype(F32)
    w_kv = jnp.concatenate([w_key, w_value], 1)
    full = lambda w, axis: lax.all_gather(lax.all_gather(w, "dp", axis=axis, tiled=True), "tensor", axis=0)
    wq = full(w_query, 0)
    wkv = full(w_kv, 0)
    wo = full(w_out, 1).reshape(width, width)
    wg = lax.all_gather(w_gate, "dp", axis=0, tiled=True)
    wu = lax.all_gather(w_up, "dp", axis=0, tiled=True)
    wd = lax.all_gather(w_down, "dp", axis=1, tiled=True)

    x = tokens.astype(F32)
    n1, r1 = rms_forward(x, gain1)
    a1 = n1.astype(BF)
    kv = jnp.einsum("rd,gdc->grc", a1, wkv, preferred_element_type=F32)
    cos_r, sin_r = cos.T, sin.T
    k = kv[..., :HD]
    k = k * cos_r + jnp.concatenate([-k[..., HD // 2 :], k[..., : HD // 2]], -1) * sin_r
    kv = jnp.concatenate([k, kv[..., HD:]], -1).astype(BF)
    kv = lax.all_gather(kv, "tensor", axis=1, tiled=True)
    o, q, lse = attn_forward(row0_s, a1, wq, kv, cos, sin, first)
    o2 = o.reshape(-1, rows)
    h = x + dot_tn(o2, wo)

    n2, r2 = rms_forward(h, gain2)
    a2 = lax.all_gather(n2.astype(BF), "tensor", axis=0, tiled=True)
    cot = lax.all_gather(cotangent, "tensor", axis=0, tiled=True)
    output, da2, gg, gu, gd = mlp_plain(h, a2, cot, wg, wu, wd)
    dres, gain2_part = rms_backward(h, r2, gain2, da2)
    dh = cotangent.astype(F32) + dres
    dhb = dh.astype(BF)

    do = dot_nt(wo, dhb).astype(BF).reshape(o.shape)
    go_part = dot_nn(o2, dhb)
    dq, dkv = attn_backward(row0_s, q, kv, do, o, lse, cos, sin, first)
    groups = dkv.shape[0]
    dkv = lax.psum_scatter(dkv.astype(BF), "tensor", scatter_dimension=1, tiled=True).astype(F32)
    dk = dkv[..., :HD]
    ws = dk * sin_r
    dk = dk * cos_r + jnp.concatenate([ws[..., HD // 2 :], -ws[..., : HD // 2]], -1)
    dkv = jnp.concatenate([dk, dkv[..., HD:]], -1).astype(BF)
    gq_part = jnp.einsum("rd,gcr->gdc", a1, dq, preferred_element_type=F32)
    gkv_part = jnp.einsum("rd,grc->gdc", a1, dkv, preferred_element_type=F32)
    da1 = jnp.einsum("gcr,gdc->rd", dq, wq, preferred_element_type=F32) + jnp.einsum("grc,gdc->rd", dkv, wkv, preferred_element_type=F32)
    din, gain1_part = rms_backward(x, r1, gain1, da1)
    grad_tokens = dh + din

    def home_all(v, dim):
        return lax.psum_scatter(home(v, dim + 1), "tensor", scatter_dimension=0, tiled=False).astype(F32)

    gq = home_all(gq_part, 0)
    gkv = home_all(gkv_part, 0)
    go = home_all(go_part.reshape(nt, -1, width), 1)
    gains = lax.psum_scatter(jnp.stack([gain1_part, gain2_part]), "dp", scatter_dimension=1, tiled=True)
    gains = lax.psum(gains, "tensor")
    return (output, grad_tokens, gains[0], gq, gkv[:, :HD], gkv[:, HD:], go, gains[1], gg, gu, gd)


def solution(mesh):
    rows, block = P(("dp", "tensor"), None), P("dp", "tensor")
    turned, line = P("tensor", "dp"), P("dp")
    return jax.shard_map(
        body if (mesh.shape["dp"], mesh.shape["tensor"]) == (8, 4) else body_plain,
        mesh=mesh,
        in_specs=(rows, line, line, block, block, block, turned, line, block, block, turned, rows),
        out_specs=(rows, rows, line, block, block, block, turned, line, block, block, turned),
        check_vma=False,
    )
```
